32 devices in a mesh: dp: 8 (over z, x), head: 4 (over y, core).
Axes of the slice: x: 2, y: 2, z: 4, core: 2. Of those that a mesh axis runs over, the one named last changes fastest.
Arguments:
- tokens: bfloat16 [64, 512, 768], P('dp', 'head'), may hold values from -8 to 8
- segment_labels: int32 [64, 512], P('dp'), may hold values from 0 to 3, as said below
- joint_projection: bfloat16 [768, 2304], replicated, may hold values from -0.21875 to 0.21875
- output_projection: bfloat16 [768, 768], replicated, may hold values from -0.625 to 0.625
- first_gain: float32 [768], replicated, may hold values from 0.1 to 1.9
- first_offset: float32 [768], replicated, may hold values from -1.75 to 1.75
- expand_weight: bfloat16 [768, 6144], replicated, may hold values from -0.21875 to 0.21875
- reduce_weight: bfloat16 [3072, 768], replicated, may hold values from -0.15625 to 0.15625
- second_gain: float32 [768], replicated, may hold values from 0.1 to 1.9
- second_offset: float32 [768], replicated, may hold values from -1.75 to 1.75
- cotangent: bfloat16 [64, 512, 768], P('dp', 'head'), may hold values from -8 to 8
Outputs:
- layer_output: bfloat16 [64, 512, 768], P('dp', 'head')
- tokens_gradient: bfloat16 [64, 512, 768], P('dp', 'head')
- joint_gradient: float32 [768, 2304], P('dp')
- projection_gradient: float32 [768, 768], P('dp')
- first_gain_gradient: float32 [768], P('dp')
- first_offset_gradient: float32 [768], P('dp')
- expand_gradient: float32 [768, 6144], P('dp')
- reduce_gradient: float32 [3072, 768], P('dp')
- second_gain_gradient: float32 [768], P('dp')
- second_offset_gradient: float32 [768], P('dp')
The draws below stay inside these ranges and needn't reach their ends.
Inputs may be any that keep to these rules, and one draw needn't show every extreme that they name: `segment_labels`: in every row the labels never fall and take each value from 0 to 3; label 1 covers every position from 64 up to 447.
All inputs are finite; a program needn't handle non-finite values.
Results may differ from the reference program's by a relative error of at most 0.015.
Values may be sent and summed in bfloat16 or wider, within the bound.
No kernel may reach another device: no remote copies, remote signals or barrier semaphores. Data moves between devices by JAX's collectives and lax.ppermute only.
A program may use at most 256 MiB of HBM per device.

```python
import math
import jax
import jax.numpy as jnp
import numpy as np
from jax import lax

D = 768
H = 12
DH = 64
FF = 3072
L = 512
ROWS = 64


def draw_segment_labels(key, part):
    key = jax.random.fold_in(key, 11)
    opening_key, closing_key, cutting_key = jax.random.split(key, 3)
    eighth = L // 8
    opening = jax.random.randint(opening_key, (ROWS, 1), 1, eighth + 1)
    closing = jax.random.randint(closing_key, (ROWS, 1), L - eighth, L - 1)
    cutting = jax.random.randint(cutting_key, (ROWS, 1), 1, L - closing)
    places = jnp.arange(L)[None, :]
    labels = (places >= opening).astype(jnp.int32) + (places >= closing).astype(jnp.int32)
    labels = labels + (places >= closing + cutting).astype(jnp.int32)
    return labels.astype(jnp.int32)


def with_spikes(values, key, source, target, parts, factor):
    def block_of(dim):
        return (jnp.arange(values.shape[dim]) // (values.shape[dim] // parts)).reshape((-1,) + (1,) * (values.ndim - 1 - dim))

    near = jax.random.permutation(key, parts)[block_of(target)]
    far = (block_of(target) + parts // 2) % parts
    return jnp.where((block_of(source) == near) | (block_of(source) == far), factor * values, values)


def levels(rng, shape, shards, smallest, top_value):
    level, own = 1.0, jax.random.fold_in(rng, 6)
    for position, parts in shards:
        steps = jnp.exp(jax.random.uniform(jax.random.fold_in(own, position), (parts,), jnp.float32, smallest / len(shards), top_value / len(shards)))
        level = level * jnp.repeat(steps, shape[position] // parts).reshape([-1 if axis == position else 1 for axis in range(len(shape))])
    return level


def scatter_about(own_key, shape, deviation, limit, cuts=(), kind=jnp.bfloat16):
    values = deviation * jax.random.normal(own_key, shape, jnp.float32)
    if cuts:
        values = values * levels(own_key, shape, cuts, -0.22, 0.18)
    return jnp.clip(values, -limit, limit).astype(kind)


def heavy_noise(stream_key, shape, scale, limit, cuts, heavy, held_as=jnp.bfloat16):
    values = scale * jax.random.normal(stream_key, shape, jnp.float32)
    if cuts:
        values = values * levels(stream_key, shape, cuts, -0.22, 0.18)
    return jnp.clip(with_spikes(values, jax.random.fold_in(stream_key, 3), *heavy), -limit, limit).astype(held_as)


def setup_inputs(seed: int = 0) -> dict:
    seeds = jax.random.split(jax.random.key(seed), 12)
    return {
        "tokens": heavy_noise(seeds[0], (ROWS, L, D), 1.0, 8.0, ((0, 8), (1, 4)), (0, 2, 8, 2.0)),
        "segment_labels": draw_segment_labels(jax.random.fold_in(seeds[11], 71), 0),
        "joint_projection": scatter_about(seeds[2], (D, 3 * D), D ** -0.5, 0.21875),
        "output_projection": scatter_about(seeds[3], (D, D), (D // 8) ** -0.5, 0.625),
        "first_gain": jnp.clip(1.0 + 0.18 * jax.random.normal(seeds[4], (D,), jnp.float32), 0.1, 1.9),
        "first_offset": scatter_about(seeds[5], (D,), 0.3, 1.75, (), jnp.float32),
        "expand_weight": scatter_about(seeds[6], (D, 2 * FF), D ** -0.5, 0.21875),
        "reduce_weight": scatter_about(seeds[7], (FF, D), (FF // 2) ** -0.5, 0.15625),
        "second_gain": jnp.clip(1.0 + 0.18 * jax.random.normal(seeds[8], (D,), jnp.float32), 0.1, 1.9),
        "second_offset": scatter_about(seeds[9], (D,), 0.3, 1.75, (), jnp.float32),
        "cotangent": heavy_noise(seeds[10], (ROWS, L, D), 1.0, 8.0, ((0, 8), (1, 4)), (0, 2, 8, 2.0)),
    }


EPSILON = 1e-12
NEG_FILL = -1e+30

@jax.custom_vjp
def low(v):
    return lax.optimization_barrier(v.astype(jnp.bfloat16)).astype(jnp.float32)

@jax.custom_vjp
def low_back(v):
    return v

def low_keep(v):
    return (low(v), None)

def low_pass(kept, grad):
    return (grad,)

def back_keep(v):
    return (v, None)

def back_low(kept, grad):
    return (low(grad),)
low.defvjp(low_keep, low_pass)
low_back.defvjp(back_keep, back_low)

def head_slopes(heads_total):
    closest = 2 ** int(math.floor(math.log2(heads_total)))

    def power_slopes(number):
        first_slope = 2.0 ** (-8.0 / number)
        return [first_slope ** (counter + 1) for counter in range(number)]
    listed = power_slopes(closest)
    if closest < heads_total:
        listed = listed + power_slopes(2 * closest)[0::2][:heads_total - closest]
    return np.array(listed, dtype=np.float32)

def layer_norm(values, gain, offset):
    center = values - lax.optimization_barrier(jnp.mean(values, axis=-1, keepdims=True))
    spread = lax.optimization_barrier(jnp.mean(center * center, axis=-1, keepdims=True))
    return center * lax.rsqrt(spread + EPSILON) * gain + offset

def layer_rows(inputs, labels, parameters):
    joint_w, output_w, gain_one, offset_one, expand_w, reduce_w, gain_two, offset_two = parameters
    highest = lax.Precision.HIGHEST
    row_count = inputs.shape[0]
    flat_inputs = inputs.reshape(-1, D)
    joint = low(low_back(jnp.dot(flat_inputs, joint_w, precision=highest)))
    joint = joint.reshape(row_count, L, 3, H, DH)
    queries = joint[:, :, 0]
    keys_block = joint[:, :, 1]
    values_block = joint[:, :, 2]
    raw_scores = jnp.einsum('rqhd,rkhd->rhqk', queries, keys_block, precision=highest)
    places = jnp.arange(L)
    distance = jnp.abs(places[:, None] - places[None, :]).astype(jnp.float32)
    slopes = jnp.asarray(head_slopes(H), dtype=jnp.float32)
    scores = low_back(raw_scores * DH ** (-0.5) - slopes[None, :, None, None] * distance[None, None])
    matching = labels[:, None, :, None] == labels[:, None, None, :]
    masked = jnp.where(matching, scores, NEG_FILL)
    row_top = lax.optimization_barrier(jnp.max(masked, axis=-1, keepdims=True))
    exponent = jnp.exp(masked - row_top)
    probability = exponent / lax.optimization_barrier(jnp.sum(exponent, axis=-1, keepdims=True))
    attended = jnp.einsum('rhqk,rkhd->rqhd', low(probability), values_block, precision=highest)
    attended = low(low_back(attended)).reshape(-1, D)
    branch = low_back(jnp.dot(attended, output_w, precision=highest))
    hidden = layer_norm(flat_inputs + branch, gain_one, offset_one)
    gate_up = low_back(jnp.dot(low(hidden), expand_w, precision=highest))
    active = jax.nn.gelu(gate_up[:, :FF], approximate=False) * gate_up[:, FF:]
    mixed = low_back(jnp.dot(low(active), reduce_w, precision=highest))
    result = layer_norm(hidden + mixed, gain_two, offset_two)
    return result.reshape(row_count, L, D)

def reference(tokens, segment_labels, joint_projection, output_projection, first_gain, first_offset, expand_weight, reduce_weight, second_gain, second_offset, cotangent):
    grouped = tokens.astype(jnp.float32).reshape(ROWS // 8, 8, L, D)
    labels = segment_labels.reshape(ROWS // 8, 8, L)
    weights = (joint_projection.astype(jnp.float32), output_projection.astype(jnp.float32), first_gain.astype(jnp.float32), first_offset.astype(jnp.float32), expand_weight.astype(jnp.float32), reduce_weight.astype(jnp.float32), second_gain.astype(jnp.float32), second_offset.astype(jnp.float32))

    def forward(inputs, parameters):

        def one_group(couple):
            return layer_rows(couple[0], couple[1], parameters)
        return lax.map(jax.checkpoint(one_group), (inputs, labels))
    outputs, pullback = jax.vjp(forward, grouped, weights)
    tokens_back, weights_back = pullback(cotangent.astype(jnp.float32).reshape(grouped.shape))
    return (outputs.reshape(ROWS, L, D).astype(jnp.bfloat16), tokens_back.reshape(ROWS, L, D).astype(jnp.bfloat16), weights_back[0], weights_back[1], weights_back[2], weights_back[3], weights_back[4], weights_back[5], weights_back[6], weights_back[7])
```

```python
import math

import jax
import jax.numpy as jnp
import numpy as np
from jax import lax
from jax.sharding import PartitionSpec as P

H = 12
DH = 64


EPSILON = 1e-12
NEG_FILL = -1e30


def head_slopes(heads_total):
    closest = 2 ** int(math.floor(math.log2(heads_total)))

    def power_slopes(number):
        first_slope = 2.0 ** (-8.0 / number)
        return [first_slope ** (counter + 1) for counter in range(number)]

    listed = power_slopes(closest)
    listed = listed + power_slopes(2 * closest)[0::2][: heads_total - closest]
    return np.array(listed, dtype=np.float32)


def layer_norm(values, gain, offset):
    center = values - jnp.mean(values, axis=-1, keepdims=True)
    spread = jnp.mean(center * center, axis=-1, keepdims=True)
    return center * lax.rsqrt(spread + EPSILON) * gain + offset


def gated_unit(gate_up):
    half_width = gate_up.shape[-1] // 2
    return jax.nn.gelu(gate_up[:, :half_width], approximate=False) * gate_up[:, half_width:]


def masked_scores(queries, keys_block, labels, slopes):
    length = queries.shape[1]
    raw_scores = jnp.einsum(
        "rqhd,rkhd->rhqk", queries, keys_block, preferred_element_type=jnp.float32
    )
    places = jnp.arange(length)
    distance = jnp.abs(places[:, None] - places[None, :]).astype(jnp.float32)
    scores = (
        raw_scores * queries.shape[-1] ** (-0.5)
        - slopes[None, :, None, None] * distance[None, None]
    )
    matching = labels[:, None, :, None] == labels[:, None, None, :]
    return jnp.where(matching, scores, NEG_FILL)


def attend_forward(queries, keys_block, values_block, labels, slopes):
    masked = masked_scores(queries, keys_block, labels, slopes)
    row_top = jnp.max(masked, axis=-1, keepdims=True)
    exponent = jnp.exp(masked - row_top)
    row_total = jnp.sum(exponent, axis=-1, keepdims=True)
    probability = (exponent / row_total).astype(jnp.bfloat16)
    attended = jnp.einsum(
        "rhqk,rkhd->rqhd", probability, values_block, preferred_element_type=jnp.float32
    )
    return (attended, row_top + jnp.log(row_total))


def attend_backward(queries, keys_block, values_block, labels, slopes, log_total, back_out):
    masked = masked_scores(queries, keys_block, labels, slopes)
    probability = jnp.exp(masked - log_total)
    back_probs = jnp.einsum(
        "rqhd,rkhd->rhqk", back_out, values_block, preferred_element_type=jnp.float32
    )
    inner = jnp.sum(probability * back_probs, axis=-1, keepdims=True)
    back_scores = (probability * (back_probs - inner)).astype(jnp.bfloat16)
    score_scale = queries.shape[-1] ** (-0.5)
    back_queries = (
        jnp.einsum("rhqk,rkhd->rqhd", back_scores, keys_block, preferred_element_type=jnp.float32)
        * score_scale
    )
    back_keys = (
        jnp.einsum("rhqk,rqhd->rkhd", back_scores, queries, preferred_element_type=jnp.float32)
        * score_scale
    )
    back_values = jnp.einsum(
        "rhqk,rqhd->rkhd",
        probability.astype(jnp.bfloat16),
        back_out,
        preferred_element_type=jnp.float32,
    )
    return (back_queries, back_keys, back_values)


def exchange(value, axis, bit):
    sizes = (lax.axis_size("dp"), lax.axis_size("head"))
    pairs = []
    for dp in range(sizes[0]):
        for head in range(sizes[1]):
            if axis == "dp":
                target = (dp ^ (1 << bit), head)
            else:
                target = (dp, head ^ bit)
            pairs.append((dp * sizes[1] + head, target[0] * sizes[1] + target[1]))
    return lax.ppermute(value, ("dp", "head"), pairs)


def rows_to_devices(values):
    groups = lax.axis_size("head")
    me = lax.axis_index("head")
    rows, quarter, width = values.shape
    own = rows // groups
    blocks = values.reshape(groups, own, quarter, width)
    got = jnp.zeros((own, groups, quarter, width), values.dtype)
    for step in range(groups):
        block = lax.dynamic_index_in_dim(blocks, me ^ step, 0, keepdims=False)
        if step:
            block = exchange(block, "head", step)
        got = lax.dynamic_update_index_in_dim(got, block, me ^ step, 1)
    return got.reshape(own, groups * quarter, width)


def rows_from_devices(values):
    groups = lax.axis_size("head")
    me = lax.axis_index("head")
    own, length, width = values.shape
    quarter = length // groups
    blocks = values.reshape(own, groups, quarter, width)
    got = jnp.zeros((groups, own, quarter, width), values.dtype)
    for step in range(groups):
        block = lax.dynamic_index_in_dim(blocks, me ^ step, 1, keepdims=False)
        if step:
            block = exchange(block, "head", step)
        got = lax.dynamic_update_index_in_dim(got, block, me ^ step, 0)
    return got.reshape(groups * own, quarter, width)


def low(value):
    return value.astype(jnp.bfloat16)


def wide(value):
    return value.astype(jnp.float32)


def sum_over_devices(left, right_halves, order):
    dp_size = lax.axis_size("dp")
    bits = dp_size.bit_length() - 1
    dp_index = lax.axis_index("dp")
    core = lax.axis_index("head") & 1
    y_index = lax.axis_index("head") >> 1

    def product(half):
        right = lax.dynamic_index_in_dim(right_halves, half, 0, keepdims=False)
        return low(
            lax.dot_general(
                left, right, (((0,), (0,)), ((), ())), preferred_element_type=jnp.float32
            )
        )

    sent = product(1 - core)
    received = exchange(sent, "head", 1)
    kept = product(core)
    rows, columns = kept.shape
    shape = (2,) * bits + (rows // dp_size, 2, columns // 2)
    terms = [(kept.reshape(shape), {}), (received.reshape(shape), {})]
    chosen = {}

    def part(term, cut, wanted):
        starts, sizes = [], []
        for axis, size in enumerate(term.shape):
            if axis in wanted and axis not in cut:
                starts.append(wanted[axis])
                sizes.append(1)
            else:
                starts.append(0)
                sizes.append(size)
        return wide(lax.dynamic_slice(term, starts, sizes))

    def total(wanted):
        value = None
        for term, cut in terms:
            piece = part(term, cut, wanted)
            value = piece if value is None else value + piece
        return value

    y_first = "y" in order
    for step in order:
        if step == "y":
            axis, mine = bits + 1, y_index
        else:
            axis, mine = bits - 1 - step, (dp_index >> step) & 1
        away = dict(chosen)
        away[axis] = 1 - mine
        chosen[axis] = mine
        sent = low(total(away))
        got = exchange(sent, "head", 2) if step == "y" else exchange(sent, "dp", step)
        terms.append((got, dict.fromkeys(chosen)))
    own = low(total(chosen))
    if y_first:
        own = own.reshape(rows // dp_size, columns // 2)
        other = exchange(own, "head", 2)
        own = jnp.where(
            y_index == 0,
            jnp.concatenate((own, other), axis=-1),
            jnp.concatenate((other, own), axis=-1),
        )
    else:
        own = own.reshape(rows // dp_size, columns)
        own = low(wide(own) + wide(exchange(own, "head", 2)))
    other = exchange(own, "head", 1)
    return jnp.where(core == 0, jnp.stack((own, other)), jnp.stack((other, own)))


def halves(value):
    width = value.shape[1] // 2
    return jnp.stack((value[:, :width], value[:, width:]))


def join_halves(value):
    return wide(jnp.concatenate((value[0], value[1]), axis=-1))


def local(
    tokens,
    segment_labels,
    joint_projection,
    output_projection,
    first_gain,
    first_offset,
    expand_weight,
    reduce_weight,
    second_gain,
    second_offset,
    cotangent,
):
    model_width = tokens.shape[2]
    length = segment_labels.shape[1]
    groups_count = lax.axis_size("head")
    group_index = lax.axis_index("head")
    bits = lax.axis_size("dp").bit_length() - 1
    up_order = tuple(range(bits))
    down_order = tuple(range(1, bits)) + (0,)
    inner = expand_weight.shape[1] // 2
    slopes = jnp.asarray(head_slopes(H), dtype=jnp.float32)
    own_tokens = rows_to_devices(tokens)
    own_cotangent = rows_to_devices(cotangent)
    row_count = own_tokens.shape[0]
    labels = lax.dynamic_slice_in_dim(segment_labels, group_index * row_count, row_count)
    flat_tokens = own_tokens.reshape(-1, model_width)
    joint = low(jnp.dot(flat_tokens, joint_projection, preferred_element_type=jnp.float32))
    joint_heads = joint.reshape(row_count, length, 3, H, DH)
    queries = joint_heads[:, :, 0]
    keys_block = joint_heads[:, :, 1]
    values_block = joint_heads[:, :, 2]
    attended, log_total = attend_forward(queries, keys_block, values_block, labels, slopes)
    token_heads = low(attended).reshape(-1, model_width)
    branch = jnp.dot(token_heads, output_projection, preferred_element_type=jnp.float32)
    hidden, first_norm_back = jax.vjp(
        layer_norm, wide(flat_tokens) + branch, first_gain, first_offset
    )
    hidden_low = low(hidden)
    gate_up = jnp.dot(hidden_low, expand_weight, preferred_element_type=jnp.float32)
    active, gated_back = jax.vjp(gated_unit, gate_up)
    active_low = low(active)
    mixed = jnp.dot(active_low, reduce_weight, preferred_element_type=jnp.float32)
    output, second_norm_back = jax.vjp(layer_norm, hidden + mixed, second_gain, second_offset)
    layer_output = rows_from_devices(low(output).reshape(own_tokens.shape))
    back_two, second_gain_back, second_offset_back = second_norm_back(
        wide(own_cotangent.reshape(-1, model_width))
    )
    back_mixed = low(back_two)
    reduce_sum = sum_over_devices(active_low, halves(back_mixed), up_order)
    (back_gate_up,) = gated_back(
        jnp.dot(back_mixed, reduce_weight.T, preferred_element_type=jnp.float32)
    )
    back_gate_up = low(back_gate_up)
    expand_sums = []
    for number, order in enumerate((down_order, ("y",) + up_order)):
        start = number * (inner // 2)
        part = jnp.stack(
            (
                back_gate_up[:, start : start + inner // 2],
                back_gate_up[:, inner + start : inner + start + inner // 2],
            )
        )
        expand_sums.append(sum_over_devices(hidden_low, part, order))
    back_hidden = back_two + jnp.dot(
        back_gate_up, expand_weight.T, preferred_element_type=jnp.float32
    )
    back_one, first_gain_back, first_offset_back = first_norm_back(back_hidden)
    back_branch = low(back_one)
    projection_sum = sum_over_devices(token_heads, halves(back_branch), up_order)
    back_attended = low(
        jnp.dot(back_branch, output_projection.T, preferred_element_type=jnp.float32)
    ).reshape(row_count, length, H, DH)
    back_queries, back_keys, back_values = attend_backward(
        queries, keys_block, values_block, labels, slopes, log_total, back_attended
    )
    back_joint = low(jnp.stack((back_queries, back_keys, back_values), axis=2)).reshape(
        -1, 3 * model_width
    )
    joint_sum = sum_over_devices(flat_tokens, halves(back_joint), down_order)
    tokens_back = back_one + jnp.dot(
        back_joint, joint_projection.T, preferred_element_type=jnp.float32
    )
    tokens_gradient = rows_from_devices(low(tokens_back).reshape(own_tokens.shape))
    vectors = lax.psum(
        jnp.stack((first_gain_back, first_offset_back, second_gain_back, second_offset_back)),
        ("dp", "head"),
    )
    own_width = model_width // lax.axis_size("dp")
    vectors = lax.dynamic_slice_in_dim(
        vectors, lax.axis_index("dp") * own_width, own_width, axis=1
    )
    expand_gradient = wide(
        jnp.concatenate(
            (expand_sums[0][0], expand_sums[1][0], expand_sums[0][1], expand_sums[1][1]), axis=-1
        )
    )
    return (
        layer_output,
        tokens_gradient,
        join_halves(joint_sum),
        join_halves(projection_sum),
        vectors[0],
        vectors[1],
        expand_gradient,
        join_halves(reduce_sum),
        vectors[2],
        vectors[3],
    )


def solution(mesh):
    placed = (
        P("dp", "head", None),
        P("dp", None),
        P(),
        P(),
        P(),
        P(),
        P(),
        P(),
        P(),
        P(),
        P("dp", "head", None),
    )
    return jax.shard_map(
        local,
        mesh=mesh,
        in_specs=placed,
        out_specs=(
            P("dp", "head", None),
            P("dp", "head", None),
            P("dp", None),
            P("dp", None),
            P("dp"),
            P("dp"),
            P("dp", None),
            P("dp", None),
            P("dp"),
            P("dp"),
        ),
        check_vma=False,
    )
```

```python
import functools
import math

import jax
import jax.numpy as jnp
import numpy as np
from jax import lax
from jax.experimental import pallas as pl
from jax.experimental.pallas import tpu as pltpu
from jax.sharding import PartitionSpec as P

H = 12
DH = 64


EPSILON = 1e-12
NEG_FILL = -1e30
LOG2E = 1.4426950408889634
NN = (((1,), (0,)), ((), ()))
NT = (((1,), (1,)), ((), ()))
TN = (((0,), (0,)), ((), ()))
VMEM_BYTES = 60 * 2**20
ANY = pl.BlockSpec(memory_space=pl.ANY)
SMEM = pl.BlockSpec(memory_space=pltpu.SMEM)


def head_slopes(heads_total):
    closest = 2 ** int(math.floor(math.log2(heads_total)))

    def power_slopes(number):
        first_slope = 2.0 ** (-8.0 / number)
        return [first_slope ** (counter + 1) for counter in range(number)]

    listed = power_slopes(closest)
    listed = listed + power_slopes(2 * closest)[0::2][: heads_total - closest]
    return np.array(listed, dtype=np.float32)


def low(value):
    return value.astype(jnp.bfloat16)


def wide(value):
    return value.astype(jnp.float32)


def dot(left, right, dims=NN):
    return lax.dot_general(left, right, dims, preferred_element_type=jnp.float32)


def shaped(shape, dtype=jnp.bfloat16):
    return jax.ShapeDtypeStruct(shape, dtype)


def whole(shape):
    return pl.BlockSpec(shape, lambda *_: (0,) * len(shape))


def call(kernel, name, grid, in_specs, out_specs, out_shape, scratch, operands, after, cost):
    count = len(operands)
    extra = len(after)

    def run(*refs):
        kernel(*refs[:count], *refs[count + extra :])

    return pl.pallas_call(
        run,
        grid=grid,
        in_specs=list(in_specs) + [ANY] * extra,
        out_specs=out_specs,
        out_shape=out_shape,
        scratch_shapes=scratch,
        compiler_params=pltpu.CompilerParams(
            vmem_limit_bytes=VMEM_BYTES, dimension_semantics=("arbitrary",) * len(grid)
        ),
        cost_estimate=pl.CostEstimate(flops=cost, bytes_accessed=0, transcendentals=0),
        name=name,
    )(*operands, *after)


def normalize(value):
    center = value - jnp.mean(value, axis=-1, keepdims=True)
    scale = lax.rsqrt(jnp.mean(center * center, axis=-1, keepdims=True) + EPSILON)
    return center * scale, scale


def norm_back(scale, normal, back):
    return scale * (
        back
        - jnp.mean(back, axis=-1, keepdims=True)
        - normal * jnp.mean(back * normal, axis=-1, keepdims=True)
    )


def attend_kernel(
    slopes,
    column_labels,
    row_labels,
    tokens,
    query_weight,
    key_weight,
    value_weight,
    queries_out,
    keys_out,
    values_out,
    probs_out,
    attended_out,
    bias,
    *,
    heads,
):
    group = pl.program_id(1)
    length = tokens.shape[1]

    @pl.when(group == 0)
    def _():
        rows = lax.broadcasted_iota(jnp.int32, (length, length), 0)
        columns = lax.broadcasted_iota(jnp.int32, (length, length), 1)
        gap = -wide(jnp.abs(rows - columns))
        bias[...] = jnp.where(column_labels[0] == row_labels[0], gap, NEG_FILL)

    row = tokens[0]
    queries = low(dot(row, query_weight[...]))
    keys = low(dot(row, key_weight[...]))
    values = low(dot(row, value_weight[...]))
    queries_out[0] = queries
    keys_out[0] = keys
    values_out[0] = values
    owner = lax.broadcasted_iota(jnp.int32, keys.shape, 1) // DH
    turned = values.T
    parts = []
    for head in range(heads):
        slope = slopes[group * heads + head]
        own_keys = jnp.where(owner == head, keys, jnp.zeros_like(keys))
        scores = dot(own_keys, queries, NT) * (DH**-0.5 * LOG2E) + bias[...] * slope
        exponent = jnp.exp2(scores - jnp.max(scores, axis=0, keepdims=True))
        probs = low(exponent * (1.0 / jnp.sum(exponent, axis=0, keepdims=True)))
        probs_out[0, head] = probs
        parts.append(dot(turned[head * DH : (head + 1) * DH], probs))
    attended_out[0] = low(jnp.concatenate(parts, axis=0).T)


def attend(tokens, labels, joint_projection, slopes, after=(), heads=4):
    rows, length, width = tokens.shape
    groups = H // heads
    group_width = heads * DH
    weight = [
        pl.BlockSpec((width, group_width), lambda r, g, which=which: (0, which * groups + g))
        for which in range(3)
    ]
    out = pl.BlockSpec((1, length, group_width), lambda r, g: (r, 0, g))
    like = shaped((rows, length, width))
    return call(
        functools.partial(attend_kernel, heads=heads),
        "attend",
        (rows, groups),
        [
            SMEM,
            pl.BlockSpec((1, length, 1), lambda r, g: (r, 0, 0)),
            pl.BlockSpec((1, 1, length), lambda r, g: (r, 0, 0)),
            pl.BlockSpec((1, length, width), lambda r, g: (r, 0, 0)),
        ]
        + weight,
        [out, out, out, pl.BlockSpec((1, heads, length, length), lambda r, g: (r, g, 0, 0)), out],
        [like, like, like, shaped((rows, H, length, length)), like],
        [pltpu.VMEM((length, length), jnp.float32)],
        (slopes * LOG2E, labels[:, :, None], labels[:, None, :], tokens) + (joint_projection,) * 3,
        after,
        16 * 10**9,
    )


def attend_back_kernel(
    queries_ref, keys_ref, values_ref, probs_ref, attended, back_attended, back_joint, *, heads
):
    queries, keys, values = queries_ref[0], keys_ref[0], values_ref[0]
    back = back_attended[0]
    owner = lax.broadcasted_iota(jnp.int32, keys.shape, 1) // DH
    zero = jnp.zeros_like(keys)
    product = (wide(attended[0]) * wide(back)).T
    turned = keys.T
    probs_all, scores_all, back_all, queries_all, parts = [], [], [], [], []
    for head in range(heads):
        mine = owner == head
        lanes = slice(head * DH, (head + 1) * DH)
        inner = jnp.sum(product[lanes], axis=0, keepdims=True)
        back_probs = dot(jnp.where(mine, values, zero), back, NT)
        probs = probs_ref[0, head]
        back_scores = low(wide(probs) * (back_probs - inner))
        probs_all.append(probs)
        scores_all.append(back_scores)
        back_all.append(jnp.where(mine, back, zero))
        queries_all.append(jnp.where(mine, queries, zero))
        parts.append(dot(turned[lanes], back_scores))
    scale = DH**-0.5
    back_joint[2, 0] = low(dot(jnp.concatenate(probs_all, 1), jnp.concatenate(back_all, 0)))
    back_joint[1, 0] = low(
        dot(jnp.concatenate(scores_all, 1), jnp.concatenate(queries_all, 0)) * scale
    )
    back_joint[0, 0] = low(jnp.concatenate(parts, 0).T * scale)


def attend_back(queries, keys, values, probs, attended, back_attended, after=(), heads=4):
    rows, length, width = queries.shape
    groups = H // heads
    group_width = heads * DH
    spec = pl.BlockSpec((1, length, group_width), lambda r, g: (r, 0, g))
    return call(
        functools.partial(attend_back_kernel, heads=heads),
        "attend_back",
        (rows, groups),
        [spec] * 3
        + [pl.BlockSpec((1, heads, length, length), lambda r, g: (r, g, 0, 0)), spec, spec],
        pl.BlockSpec((3, 1, length, group_width), lambda r, g: (0, r, 0, g)),
        shaped((3, rows, length, width)),
        [],
        (queries, keys, values, probs, attended, back_attended),
        after,
        14 * 10**9,
    )


def ahead_kernel(
    tokens,
    attended,
    output_projection,
    first_gain,
    first_offset,
    gate_weight,
    up_weight,
    reduce_weight,
    second_gain,
    second_offset,
    cotangent,
    normal_out,
    scale_out,
    hidden_out,
    gate_out,
    slope_out,
    active_out,
    output,
    two_out,
    mixed_out,
    gain_out,
    offset_out,
    total,
    *,
    block,
):
    step = pl.program_id(0)
    count, width = tokens.shape
    blocks = [pl.ds(start, block) for start in range(0, count, block)]

    @pl.when(step == 0)
    def _():
        for rows in blocks:
            branch = dot(attended[rows, :], output_projection[...])
            normal, scale = normalize(wide(tokens[rows, :]) + branch)
            normal_out[rows, :] = normal
            scale_out[rows, :] = jnp.broadcast_to(scale, (block, scale_out.shape[1]))
            hidden = normal * first_gain[...] + first_offset[...]
            hidden_out[rows, :] = low(hidden)
            total[rows, :] = hidden

    for rows in blocks:
        hidden = hidden_out[rows, :]
        gate = dot(hidden, gate_weight[...])
        up = dot(hidden, up_weight[...])
        share = 0.5 * (1.0 + lax.erf(gate * 0.5**0.5))
        density = jnp.exp(gate * gate * -0.5) * (2.0 * math.pi) ** -0.5
        unit = gate * share
        active = low(unit * up)
        gate_out[rows, :] = low(unit)
        slope_out[rows, :] = low(up * (share + gate * density))
        active_out[rows, :] = active
        total[rows, :] += dot(active, reduce_weight[...])

    @pl.when(step == pl.num_programs(0) - 1)
    def _():
        gain = jnp.zeros((1, width), jnp.float32)
        offset = gain
        for rows in blocks:
            normal, scale = normalize(total[rows, :])
            output[rows, :] = low(normal * second_gain[...] + second_offset[...])
            back = wide(cotangent[rows, :])
            gain += jnp.sum(back * normal, axis=0, keepdims=True)
            offset += jnp.sum(back, axis=0, keepdims=True)
            two = norm_back(scale, normal, back * second_gain[...])
            two_out[rows, :] = two
            mixed_out[rows, :] = low(two)
        gain_out[...] = gain
        offset_out[...] = offset


def ahead(
    tokens,
    attended,
    output_projection,
    first_gain,
    first_offset,
    expand_weight,
    reduce_weight,
    second_gain,
    second_offset,
    cotangent,
    after=(),
    chunk=512,
    block=256,
):
    count, width = tokens.shape
    inner = reduce_weight.shape[0]
    steps = inner // chunk
    vector = whole((1, width))
    rows = whole((count, width))
    column = pl.BlockSpec((count, chunk), lambda s: (0, s))
    return call(
        functools.partial(ahead_kernel, block=block),
        "ahead",
        (steps,),
        [
            rows,
            rows,
            whole((width, width)),
            vector,
            vector,
            pl.BlockSpec((width, chunk), lambda s: (0, s)),
            pl.BlockSpec((width, chunk), lambda s: (0, s + steps)),
            pl.BlockSpec((chunk, width), lambda s: (s, 0)),
            vector,
            vector,
            rows,
        ],
        [rows, whole((count, 128)), rows, column, column, column, rows, rows, rows, vector, vector],
        [
            shaped((count, width), jnp.float32),
            shaped((count, 128), jnp.float32),
            shaped((count, width)),
            shaped((count, inner)),
            shaped((count, inner)),
            shaped((count, inner)),
            shaped((count, width)),
            shaped((count, width), jnp.float32),
            shaped((count, width)),
            shaped((1, width), jnp.float32),
            shaped((1, width), jnp.float32),
        ],
        [pltpu.VMEM((count, width), jnp.float32)],
        (
            tokens,
            attended,
            output_projection,
            first_gain[None],
            first_offset[None],
            expand_weight,
            expand_weight,
            reduce_weight,
            second_gain[None],
            second_offset[None],
            cotangent,
        ),
        after,
        25 * 10**9,
    )


def reduce_kernel(core, mixed, active, sent, kept, turned):
    half = turned.shape[0] // 2

    @pl.when(pl.program_id(0) == 0)
    def _():
        turned[...] = mixed[...].T

    for out, place in ((sent, 1 - core[0]), (kept, core[0])):
        left = turned[pl.ds(pl.multiple_of(place * half, half), half), :]
        part = low(dot(left, active[...]))
        columns = out.shape[2]
        for number in range(out.shape[0]):
            out[number] = part[:, number * columns : (number + 1) * columns]


def reduce_gradient(core, mixed, active, after=(), blocks=8, together=2):
    count, width = mixed.shape
    columns = active.shape[1] // blocks
    out = pl.BlockSpec((together, width // 2, columns), lambda s: (s, 0, 0))
    like = shaped((blocks, width // 2, columns))
    return call(
        reduce_kernel,
        "reduce_gradient",
        (blocks // together,),
        [
            SMEM,
            whole((count, width)),
            pl.BlockSpec((count, columns * together), lambda s: (0, s)),
        ],
        [out, out],
        [like, like],
        [pltpu.VMEM((width, count), jnp.bfloat16)],
        (core, mixed, active),
        after,
        7 * 10**9,
    )


def expand_kernel(
    core,
    mixed,
    hidden,
    gate_part,
    slope_part,
    reduce_weight,
    gate_weight,
    up_weight,
    start,
    sent,
    kept,
    back,
    turned,
):
    @pl.when(pl.program_id(0) == 0)
    def _():
        turned[...] = hidden[...].T
        back[...] = start[...]

    weight = jnp.concatenate([gate_weight[...], up_weight[...]], 1)
    back_active = dot(mixed[...], reduce_weight[...], NT)
    both = jnp.concatenate(
        [low(back_active * wide(slope_part[...])), low(back_active * wide(gate_part[...]))], 1
    )
    back[...] += dot(both, weight, NT)
    gradient = low(dot(turned[...], both))
    chunk = gradient.shape[1] // 2
    first = core[0] == 0
    sent[0] = jnp.where(first, gradient[:, chunk:], gradient[:, :chunk])
    kept[0] = jnp.where(first, gradient[:, :chunk], gradient[:, chunk:])


def expand_gradient(
    core,
    mixed,
    hidden,
    gate_part,
    slope_part,
    reduce_weight,
    expand_weight,
    start,
    part,
    parts=2,
    after=(),
    chunk=768,
):
    count, width = mixed.shape
    inner = reduce_weight.shape[0]
    steps = inner // parts // chunk
    base = part * steps
    all_steps = inner // chunk
    rows = whole((count, width))
    column = pl.BlockSpec((count, chunk), lambda s: (0, base + s))
    out = pl.BlockSpec((1, width, chunk), lambda s: (s, 0, 0))
    like = shaped((steps, width, chunk))
    return call(
        expand_kernel,
        "expand_gradient",
        (steps,),
        [
            SMEM,
            rows,
            rows,
            column,
            column,
            pl.BlockSpec((chunk, width), lambda s: (base + s, 0)),
            pl.BlockSpec((width, chunk), lambda s: (0, base + s)),
            pl.BlockSpec((width, chunk), lambda s: (0, all_steps + base + s)),
            rows,
        ],
        [out, out, rows],
        [like, like, shaped((count, width), jnp.float32)],
        [pltpu.VMEM((width, count), jnp.bfloat16)],
        (
            core,
            mixed,
            hidden,
            gate_part,
            slope_part,
            reduce_weight,
            expand_weight,
            expand_weight,
            start,
        ),
        after,
        16 * 10**9,
    )


def branch_kernel(
    core,
    back_hidden,
    normal,
    scale,
    first_gain,
    attended,
    output_projection,
    one_out,
    back_attended,
    sent,
    kept,
    gain_out,
    offset_out,
    branch,
    *,
    block,
):
    count, width = back_hidden.shape
    half = width // 2
    gain = jnp.zeros((1, width), jnp.float32)
    offset = gain
    for start in range(0, count, block):
        rows = pl.ds(start, block)
        back = back_hidden[rows, :]
        gain += jnp.sum(back * normal[rows, :], axis=0, keepdims=True)
        offset += jnp.sum(back, axis=0, keepdims=True)
        one = norm_back(scale[rows, :1], normal[rows, :], back * first_gain[...])
        one_out[rows, :] = one
        branch[rows, :] = low(one)
        back_attended[rows, :] = low(dot(low(one), output_projection[...], NT))
    gain_out[...] = gain
    offset_out[...] = offset
    gradient = low(dot(attended[...].T, branch[...]))
    first = core[0] == 0
    sent[...] = jnp.where(first, gradient[:, half:], gradient[:, :half])
    kept[...] = jnp.where(first, gradient[:, :half], gradient[:, half:])


def branch_back(
    core, back_hidden, normal, scale, first_gain, attended, output_projection, after=(), block=256
):
    count, width = back_hidden.shape
    rows = whole((count, width))
    vector = whole((1, width))
    halves = whole((width, width // 2))
    return call(
        functools.partial(branch_kernel, block=block),
        "branch_back",
        (1,),
        [SMEM, rows, rows, whole((count, 128)), vector, rows, whole((width, width))],
        [rows, rows, halves, halves, vector, vector],
        [
            shaped((count, width), jnp.float32),
            shaped((count, width)),
            shaped((width, width // 2)),
            shaped((width, width // 2)),
            shaped((1, width), jnp.float32),
            shaped((1, width), jnp.float32),
        ],
        [pltpu.VMEM((count, width), jnp.bfloat16)],
        (core, back_hidden, normal, scale, first_gain[None], attended, output_projection),
        after,
        7 * 10**9,
    )


def joint_kernel(core, tokens, back_joint, sent, kept, turned):
    half = sent.shape[2]

    @pl.when(pl.program_id(0) == 0)
    def _():
        turned[...] = tokens[...].T

    gradient = low(dot(turned[...], back_joint[0]))
    first = core[0] == 0
    sent[0] = jnp.where(first, gradient[:, half:], gradient[:, :half])
    kept[0] = jnp.where(first, gradient[:, :half], gradient[:, half:])


def joint_gradient(core, tokens, back_joint, after=()):
    count, width = tokens.shape
    out = pl.BlockSpec((1, width, width // 2), lambda s: (s, 0, 0))
    like = shaped((3, width, width // 2))
    return call(
        joint_kernel,
        "joint_gradient",
        (3,),
        [SMEM, whole((count, width)), pl.BlockSpec((1, count, width), lambda s: (s, 0, 0))],
        [out, out],
        [like, like],
        [pltpu.VMEM((width, count), jnp.bfloat16)],
        (core, tokens, back_joint),
        after,
        5 * 10**9,
    )


def tokens_kernel(back_joint, weight, one, out, total):
    step = pl.program_id(0)
    part = dot(back_joint[0], weight[...], NT)

    @pl.when(step == 0)
    def _():
        total[...] = one[...] + part

    @pl.when(step == 1)
    def _():
        total[...] += part

    @pl.when(step == 2)
    def _():
        out[...] = low(total[...] + part)


def tokens_gradient_of(back_joint, joint_projection, one, after=()):
    _, count, width = back_joint.shape
    rows = whole((count, width))
    return call(
        tokens_kernel,
        "tokens_gradient",
        (3,),
        [
            pl.BlockSpec((1, count, width), lambda s: (s, 0, 0)),
            pl.BlockSpec((width, width), lambda s: (0, s)),
            rows,
        ],
        rows,
        shaped((count, width)),
        [pltpu.VMEM((count, width), jnp.float32)],
        (back_joint, joint_projection, one),
        after,
        5 * 10**9,
    )


def exchange(value, axis, bit):
    sizes = (lax.axis_size("dp"), lax.axis_size("head"))
    pairs = []
    for dp in range(sizes[0]):
        for head in range(sizes[1]):
            target = (dp ^ bit, head) if axis == "dp" else (dp, head ^ bit)
            pairs.append((dp * sizes[1] + head, target[0] * sizes[1] + target[1]))
    return lax.ppermute(value, ("dp", "head"), pairs)


def pick(pieces, place):
    value = pieces[0]
    for number in range(1, len(pieces)):
        value = jnp.where(place == number, pieces[number], value)
    return value


def rows_to_devices(values):
    groups = lax.axis_size("head")
    me = lax.axis_index("head")
    rows, quarter, width = values.shape
    blocks = values.reshape(groups, rows // groups, quarter, width)
    pieces = [
        lax.dynamic_index_in_dim(blocks, me ^ step, 0, keepdims=False) for step in range(groups)
    ]
    pieces = [pieces[0]] + [exchange(pieces[step], "head", step) for step in range(1, groups)]
    return jnp.concatenate([pick(pieces, me ^ place) for place in range(groups)], axis=1)


def rows_from_devices(values, length):
    groups = lax.axis_size("head")
    me = lax.axis_index("head")
    width = values.shape[1]
    blocks = values.reshape(-1, groups, length // groups, width)
    pieces = [
        lax.dynamic_index_in_dim(blocks, me ^ step, 1, keepdims=False) for step in range(groups)
    ]
    sent = pieces[1:]
    pieces = [pieces[0]] + [exchange(sent[step - 1], "head", step) for step in range(1, groups)]
    finish = lambda: jnp.concatenate(
        [pick(pieces, me ^ place) for place in range(groups)], axis=0
    )
    return finish, sent


class Sum:
    def __init__(self, sent, kept):
        self.bits = lax.axis_size("dp").bit_length() - 1
        self.lead = kept.ndim - 3
        self.tail = kept.shape[-2:]
        self.front = kept.shape[: self.lead]
        self.chosen = {}
        self.terms = [(self.split(kept), ())]
        self.coming = self.split(exchange(sent, "head", 1))

    def split(self, value):
        return value.reshape(self.front + (2,) * self.bits + self.tail)

    def total(self, wanted):
        value = None
        for term, cut in self.terms:
            starts = [0] * term.ndim
            sizes = list(term.shape)
            for axis, place in wanted.items():
                if axis not in cut:
                    starts[axis], sizes[axis] = place, 1
            piece = wide(lax.dynamic_slice(term, starts, sizes))
            value = piece if value is None else value + piece
        return value

    def arrive(self):
        if self.coming is not None:
            self.terms.append((self.coming, tuple(self.chosen)))
            self.coming = None

    def halve(self, step):
        self.arrive()
        if step == "y":
            axis, mine = 0, lax.axis_index("head") >> 1
        else:
            axis, mine = self.lead + self.bits - 1 - step, (lax.axis_index("dp") >> step) & 1
        away = dict(self.chosen)
        away[axis] = 1 - mine
        sent = low(self.total(away))
        self.chosen[axis] = mine
        self.coming = exchange(sent, *(("head", 2) if step == "y" else ("dp", 1 << step)))
        return sent

    def own(self):
        self.arrive()
        value = low(self.total(self.chosen))
        return value.reshape(value.shape[: self.lead] + self.tail)


def sum_y(own):
    return low(wide(own) + wide(exchange(own, "head", 2)))


def join(own, bit, axis):
    other = exchange(own, "head", bit)
    first = lax.axis_index("head") & bit == 0
    return jnp.concatenate(
        (jnp.where(first, own, other), jnp.where(first, other, own)), axis=axis
    )


def local(
    tokens,
    segment_labels,
    joint_projection,
    output_projection,
    first_gain,
    first_offset,
    expand_weight,
    reduce_weight,
    second_gain,
    second_offset,
    cotangent,
):
    width = tokens.shape[2]
    length = segment_labels.shape[1]
    dp_size = lax.axis_size("dp")
    bits = dp_size.bit_length() - 1
    own_width = width // dp_size
    inner = reduce_weight.shape[0]
    me = lax.axis_index("head")
    core = jnp.reshape(me & 1, (1,))
    up_order = list(range(bits))
    down_order = up_order[1:] + up_order[:1]
    slopes = jnp.asarray(head_slopes(H), dtype=jnp.float32)

    own_tokens = rows_to_devices(tokens)
    own_cotangent = rows_to_devices(cotangent)
    row_count = own_tokens.shape[0]
    flat = lambda value: value.reshape(row_count * length, width)
    rowed = lambda value: value.reshape(row_count, length, width)
    labels = lax.dynamic_slice_in_dim(segment_labels, me * row_count, row_count)
    flat_tokens = flat(own_tokens)

    queries, keys, values, probs, attended = attend(own_tokens, labels, joint_projection, slopes)
    (
        normal,
        scale,
        hidden,
        gate_part,
        slope_part,
        active,
        output,
        back_two,
        back_mixed,
        second_gain_back,
        second_offset_back,
    ) = ahead(
        flat_tokens,
        flat(attended),
        output_projection,
        first_gain,
        first_offset,
        expand_weight,
        reduce_weight,
        second_gain,
        second_offset,
        flat(own_cotangent),
    )
    output_finish, output_sent = rows_from_devices(output, length)
    blocks = 8
    sent, kept = reduce_gradient(core, back_mixed, active, after=output_sent)
    by_device = lambda value: (
        value.reshape(blocks, width // 2, dp_size // blocks, inner // dp_size)
        .transpose(0, 2, 1, 3)
        .reshape(dp_size, width // 2, inner // dp_size)
    )
    reduce_sum = Sum(by_device(sent), by_device(kept))
    rest = (core, back_mixed, hidden, gate_part, slope_part, reduce_weight, expand_weight)
    cut = lambda value: value.reshape(value.shape[0], dp_size, own_width, value.shape[2])
    sent, kept, back_hidden = expand_gradient(*rest, back_two, 0)
    expand_first = Sum(cut(sent), cut(kept))
    moved = [reduce_sum.halve(up_order[0])]
    sent, kept, back_hidden = expand_gradient(*rest, back_hidden, 1, after=moved)
    expand_second = Sum(cut(sent), cut(kept))
    moved = [expand_first.halve(down_order[0])]
    back_one, back_attended, sent, kept, first_gain_back, first_offset_back = branch_back(
        core, back_hidden, normal, scale, first_gain, flat(attended), output_projection, after=moved
    )
    vectors = jnp.concatenate(
        (first_gain_back, first_offset_back, second_gain_back, second_offset_back)
    ).reshape(8, width // 2)
    vectors = jnp.broadcast_to(low(jnp.pad(vectors, ((0, 8), (0, 0)))), (dp_size, 16, width // 2))
    with_vectors = lambda value: jnp.concatenate(
        (value.reshape(dp_size, own_width, width // 2), vectors), axis=1
    )
    projection_sum = Sum(with_vectors(sent), with_vectors(kept))
    moved = [reduce_sum.halve(up_order[1]), expand_second.halve("y")]
    back_joint = attend_back(
        queries, keys, values, probs, attended, rowed(back_attended), after=moved
    ).reshape(3, -1, width)
    moved = [
        reduce_sum.halve(step) for step in up_order[2:]
    ] + [
        expand_first.halve(down_order[1]),
        expand_second.halve(up_order[0]),
        projection_sum.halve(up_order[0]),
    ]
    sent, kept = joint_gradient(core, flat_tokens, back_joint, after=moved)
    joint_sum = Sum(cut(sent), cut(kept))
    moved = [expand_second.halve(up_order[1]), projection_sum.halve(up_order[1])]
    gradient = tokens_gradient_of(back_joint, joint_projection, back_one, after=moved)
    gradient_finish, gradient_sent = rows_from_devices(gradient, length)
    joint_sum.halve(down_order[0])
    for step in down_order[2:]:
        expand_first.halve(step)
    for step in up_order[2:]:
        expand_second.halve(step)
        projection_sum.halve(step)
    for step in down_order[1:]:
        joint_sum.halve(step)

    reduce_grad = wide(join(sum_y(reduce_sum.own()), 1, 0).T)
    first_grad = join(sum_y(expand_first.own())[None], 1, 0)
    second_grad = join(join(expand_second.own(), 2, 0)[None], 1, 0)
    expand_grad = jnp.concatenate(
        [
            piece
            for side in range(2)
            for piece in (
                first_grad[side, 0],
                first_grad[side, 1],
                second_grad[side, 0],
                second_grad[side, 1],
            )
        ],
        axis=-1,
    )
    projection_own = sum_y(projection_sum.own())
    joint_grad = join(sum_y(joint_sum.own()), 1, 2)
    vectors = wide(projection_own[own_width : own_width + 8]).reshape(4, width)
    vectors = lax.dynamic_slice_in_dim(
        vectors, lax.axis_index("dp") * own_width, own_width, axis=1
    )
    return (
        output_finish(),
        gradient_finish(),
        wide(jnp.concatenate([joint_grad[0], joint_grad[1], joint_grad[2]], axis=-1)),
        wide(join(projection_own[:own_width], 1, 1)),
        vectors[0],
        vectors[1],
        wide(expand_grad),
        reduce_grad,
        vectors[2],
        vectors[3],
    )


def solution(mesh):
    placed = (
        P("dp", "head", None),
        P("dp", None),
        P(),
        P(),
        P(),
        P(),
        P(),
        P(),
        P(),
        P(),
        P("dp", "head", None),
    )
    return jax.shard_map(
        local,
        mesh=mesh,
        in_specs=placed,
        out_specs=(
            P("dp", "head", None),
            P("dp", "head", None),
            P("dp", None),
            P("dp", None),
            P("dp"),
            P("dp"),
            P("dp", None),
            P("dp", None),
            P("dp"),
            P("dp"),
        ),
        check_vma=False,
    )
```

```python
import functools
import math

import jax
import jax.numpy as jnp
import numpy as np
from jax import lax
from jax.experimental import pallas as pl
from jax.experimental.pallas import tpu as pltpu
from jax.sharding import PartitionSpec as P

H = 12
DH = 64


EPSILON = 1e-12
NEG_FILL = -1e30
LOG2E = 1.4426950408889634
NN = (((1,), (0,)), ((), ()))
NT = (((1,), (1,)), ((), ()))
TN = (((0,), (0,)), ((), ()))
VMEM_BYTES = 60 * 2**20
ANY = pl.BlockSpec(memory_space=pl.ANY)
SMEM = pl.BlockSpec(memory_space=pltpu.SMEM)


def head_slopes(heads_total):
    closest = 2 ** int(math.floor(math.log2(heads_total)))

    def power_slopes(number):
        first_slope = 2.0 ** (-8.0 / number)
        return [first_slope ** (counter + 1) for counter in range(number)]

    listed = power_slopes(closest)
    listed = listed + power_slopes(2 * closest)[0::2][: heads_total - closest]
    return np.array(listed, dtype=np.float32)


def low(value):
    return value.astype(jnp.bfloat16)


def wide(value):
    return value.astype(jnp.float32)


def dot(left, right, dims=NN):
    return lax.dot_general(left, right, dims, preferred_element_type=jnp.float32)


def shaped(shape, dtype=jnp.bfloat16):
    return jax.ShapeDtypeStruct(shape, dtype)


def whole(shape):
    return pl.BlockSpec(shape, lambda *_: (0,) * len(shape))


def call(kernel, name, grid, in_specs, out_specs, out_shape, scratch, operands, after, into=()):
    count = len(operands) - 1
    extra = len(after) + len(into)
    results = len(out_shape)

    def run(me, *refs):
        outs = refs[count + extra :]
        token = outs[results]
        token[...] = jnp.zeros_like(token)
        kernel(me, *refs[:count], *outs[:results], *outs[results + 1 :])

    return pl.pallas_call(
        run,
        grid_spec=pltpu.PrefetchScalarGridSpec(
            num_scalar_prefetch=1,
            grid=grid,
            in_specs=list(in_specs) + [ANY] * extra,
            out_specs=list(out_specs) + [whole((8, 128))],
            scratch_shapes=scratch,
        ),
        out_shape=list(out_shape) + [shaped((8, 128), jnp.float32)],
        input_output_aliases={count + 1 + number: number for number in range(len(into))},
        compiler_params=pltpu.CompilerParams(
            vmem_limit_bytes=VMEM_BYTES, dimension_semantics=("arbitrary",) * len(grid)
        ),
        cost_estimate=pl.CostEstimate(flops=10**6, bytes_accessed=0, transcendentals=0),
        name=name,
    )(*operands, *into, *after)


def normalize(value):
    center = value - jnp.mean(value, axis=-1, keepdims=True)
    scale = lax.rsqrt(jnp.mean(center * center, axis=-1, keepdims=True) + EPSILON)
    return center * scale, scale


def norm_back(scale, normal, back):
    return scale * (
        back
        - jnp.mean(back, axis=-1, keepdims=True)
        - normal * jnp.mean(back * normal, axis=-1, keepdims=True)
    )


def attend_kernel(
    me,
    slopes,
    labels,
    first,
    second,
    third,
    fourth,
    query_weight,
    key_weight,
    value_weight,
    tokens_out,
    queries_out,
    keys_out,
    values_out,
    probs_out,
    attended_out,
    bias,
    *,
    row,
    heads,
):
    group = pl.program_id(0)
    _, length, width = tokens_out.shape
    quarter = length // 4

    @pl.when(group == 0)
    def _():
        for step, piece in enumerate((first, second, third, fourth)):
            place = pl.multiple_of((me[0] ^ step) * quarter, quarter)
            tokens_out[0, pl.ds(place, quarter), :] = piece[0]
        label = labels[pl.ds(me[0] * 2 + row, 1), :]
        column = jnp.broadcast_to(label, (128, length)).T[:, :1]
        rows = lax.broadcasted_iota(jnp.int32, (length, length), 0)
        columns = lax.broadcasted_iota(jnp.int32, (length, length), 1)
        gap = -wide(jnp.abs(rows - columns))
        bias[...] = jnp.where(column == label, gap, NEG_FILL)

    tokens = tokens_out[0]
    queries = low(dot(tokens, query_weight[...]))
    keys = low(dot(tokens, key_weight[...]))
    values = low(dot(tokens, value_weight[...]))
    queries_out[0] = queries
    keys_out[0] = keys
    values_out[0] = values
    owner = lax.broadcasted_iota(jnp.int32, keys.shape, 1) // DH
    turned = values.T
    parts = []
    for head in range(heads):
        slope = slopes[group * heads + head] * LOG2E
        own_keys = jnp.where(owner == head, keys, jnp.zeros_like(keys))
        scores = dot(own_keys, queries, NT) * (DH**-0.5 * LOG2E) + bias[...] * slope
        exponent = jnp.exp2(scores - jnp.max(scores, axis=0, keepdims=True))
        probs = low(exponent * (1.0 / jnp.sum(exponent, axis=0, keepdims=True)))
        probs_out[0, head] = probs
        parts.append(dot(turned[head * DH : (head + 1) * DH], probs))
    attended_out[0] = low(jnp.concatenate(parts, axis=0).T)


def attend(me, slopes, labels, tokens, pieces, joint_projection, row, into=(), heads=4):
    _, quarter, width = tokens.shape
    length = labels.shape[1]
    rows = tokens.shape[0] // 4
    groups = H // heads
    group_width = heads * DH
    weight = [
        pl.BlockSpec((width, group_width), lambda g, me, which=which: (0, which * groups + g))
        for which in range(3)
    ]
    out = pl.BlockSpec((1, length, group_width), lambda g, me: (row, 0, g))
    like = shaped((rows, length, width))
    return call(
        functools.partial(attend_kernel, row=row, heads=heads),
        "attend",
        (groups,),
        [
            SMEM,
            whole(labels.shape),
            pl.BlockSpec((1, quarter, width), lambda g, me: (me[0] * rows + row, 0, 0)),
        ]
        + [whole((1, quarter, width))] * 3
        + weight,
        [pl.BlockSpec((1, length, width), lambda g, me: (row, 0, 0)), out, out, out]
        + [pl.BlockSpec((1, heads, length, length), lambda g, me: (row, g, 0, 0)), out],
        [like, like, like, like, shaped((rows, H, length, length)), like],
        [pltpu.VMEM((length, length), jnp.float32)],
        (me, slopes, labels, tokens, *pieces) + (joint_projection,) * 3,
        (),
        into,
    )


def attend_back_kernel(
    me, queries_ref, keys_ref, values_ref, probs_ref, attended, back_attended, back_joint, *, heads
):
    queries, keys, values = queries_ref[0], keys_ref[0], values_ref[0]
    back = back_attended[0]
    owner = lax.broadcasted_iota(jnp.int32, keys.shape, 1) // DH
    zero = jnp.zeros_like(keys)
    product = (wide(attended[0]) * wide(back)).T
    turned = keys.T
    probs_all, scores_all, back_all, queries_all, parts = [], [], [], [], []
    for head in range(heads):
        mine = owner == head
        lanes = slice(head * DH, (head + 1) * DH)
        inner = jnp.sum(product[lanes], axis=0, keepdims=True)
        back_probs = dot(jnp.where(mine, values, zero), back, NT)
        probs = probs_ref[0, head]
        back_scores = low(wide(probs) * (back_probs - inner))
        probs_all.append(probs)
        scores_all.append(back_scores)
        back_all.append(jnp.where(mine, back, zero))
        queries_all.append(jnp.where(mine, queries, zero))
        parts.append(dot(turned[lanes], back_scores))
    scale = DH**-0.5
    back_joint[2, 0] = low(dot(jnp.concatenate(probs_all, 1), jnp.concatenate(back_all, 0)))
    back_joint[1, 0] = low(
        dot(jnp.concatenate(scores_all, 1), jnp.concatenate(queries_all, 0)) * scale
    )
    back_joint[0, 0] = low(jnp.concatenate(parts, 0).T * scale)


def attend_back(me, queries, keys, values, probs, attended, back_attended, after=(), heads=4):
    rows, length, width = queries.shape
    groups = H // heads
    group_width = heads * DH
    spec = pl.BlockSpec((1, length, group_width), lambda r, g, me: (r, 0, g))
    return call(
        functools.partial(attend_back_kernel, heads=heads),
        "attend_back",
        (rows, groups),
        [spec] * 3
        + [pl.BlockSpec((1, heads, length, length), lambda r, g, me: (r, g, 0, 0)), spec, spec],
        [pl.BlockSpec((3, 1, length, group_width), lambda r, g, me: (0, r, 0, g))],
        [shaped((3, rows, length, width))],
        [],
        (me, queries, keys, values, probs, attended, back_attended),
        after,
    )


def send_piece(me, place, value, outs):
    for number, out in enumerate(outs):

        @pl.when((place % 4) ^ number == me[0])
        def _():
            out[place // 4] = value


def ahead_kernel(
    me,
    tokens,
    attended,
    output_projection,
    first_gain,
    first_offset,
    gate_weight,
    up_weight,
    reduce_weight,
    second_gain,
    second_offset,
    first,
    second,
    third,
    fourth,
    normal_out,
    scale_out,
    hidden_out,
    gate_out,
    slope_out,
    active_out,
    output_first,
    output_second,
    output_third,
    output_fourth,
    two_out,
    mixed_out,
    gain_out,
    offset_out,
    total,
    cotangent,
    *,
    block,
):
    step = pl.program_id(0)
    count, width = tokens.shape
    quarter = first.shape[1]
    blocks = [pl.ds(start, block) for start in range(0, count, block)]

    @pl.when(step == 0)
    def _():
        for number, piece in enumerate((first, second, third, fourth)):
            for row in range(piece.shape[0]):
                place = (row * 4 + (me[0] ^ number)) * quarter
                cotangent[pl.ds(pl.multiple_of(place, quarter), quarter), :] = piece[row]
        for rows in blocks:
            branch = dot(attended[rows, :], output_projection[...])
            normal, scale = normalize(wide(tokens[rows, :]) + branch)
            normal_out[rows, :] = normal
            scale_out[rows, :] = jnp.broadcast_to(scale, (block, scale_out.shape[1]))
            hidden = normal * first_gain[...][None] + first_offset[...][None]
            hidden_out[rows, :] = low(hidden)
            total[rows, :] = hidden

    for rows in blocks:
        hidden = hidden_out[rows, :]
        gate = dot(hidden, gate_weight[...])
        up = dot(hidden, up_weight[...])
        share = 0.5 * (1.0 + lax.erf(gate * 0.5**0.5))
        density = jnp.exp(gate * gate * -0.5) * (2.0 * math.pi) ** -0.5
        unit = gate * share
        active = low(unit * up)
        gate_out[rows, :] = low(unit)
        slope_out[rows, :] = low(up * (share + gate * density))
        active_out[rows, :] = active
        total[rows, :] += dot(active, reduce_weight[...])

    @pl.when(step == pl.num_programs(0) - 1)
    def _():
        gain = jnp.zeros((1, width), jnp.float32)
        offset = gain
        for start in range(0, count, quarter):
            rows = pl.ds(start, quarter)
            normal, scale = normalize(total[rows, :])
            send_piece(
                me,
                start // quarter,
                low(normal * second_gain[...][None] + second_offset[...][None]),
                (output_first, output_second, output_third, output_fourth),
            )
            back = wide(cotangent[rows, :])
            gain += jnp.sum(back * normal, axis=0, keepdims=True)
            offset += jnp.sum(back, axis=0, keepdims=True)
            two = norm_back(scale, normal, back * second_gain[...][None])
            two_out[rows, :] = two
            mixed_out[rows, :] = low(two)
        gain_out[...] = gain
        offset_out[...] = offset


def ahead(
    me,
    tokens,
    attended,
    output_projection,
    first_gain,
    first_offset,
    expand_weight,
    reduce_weight,
    second_gain,
    second_offset,
    cotangent,
    pieces,
    after=(),
    chunk=512,
    block=256,
):
    count, width = tokens.shape
    inner = reduce_weight.shape[0]
    steps = inner // chunk
    vector = whole((width,))
    rows = whole((count, width))
    column = pl.BlockSpec((count, chunk), lambda s, me: (0, s))
    piece = pieces[0].shape
    return call(
        functools.partial(ahead_kernel, block=block),
        "ahead",
        (steps,),
        [
            rows,
            rows,
            whole((width, width)),
            vector,
            vector,
            pl.BlockSpec((width, chunk), lambda s, me: (0, s)),
            pl.BlockSpec((width, chunk), lambda s, me: (0, s + steps)),
            pl.BlockSpec((chunk, width), lambda s, me: (s, 0)),
            vector,
            vector,
            pl.BlockSpec(piece, lambda s, me: (me[0], 0, 0)),
        ]
        + [whole(piece)] * 3,
        [rows, whole((count, 128)), rows, column, column, column]
        + [whole(piece)] * 4
        + [rows, rows, whole((1, width)), whole((1, width))],
        [
            shaped((count, width), jnp.float32),
            shaped((count, 128), jnp.float32),
            shaped((count, width)),
            shaped((count, inner)),
            shaped((count, inner)),
            shaped((count, inner)),
        ]
        + [shaped(piece)] * 4
        + [
            shaped((count, width), jnp.float32),
            shaped((count, width)),
            shaped((1, width), jnp.float32),
            shaped((1, width), jnp.float32),
        ],
        [pltpu.VMEM((count, width), jnp.float32), pltpu.VMEM((count, width), jnp.bfloat16)],
        (
            me,
            tokens,
            attended,
            output_projection,
            first_gain,
            first_offset,
            expand_weight,
            expand_weight,
            reduce_weight,
            second_gain,
            second_offset,
            cotangent,
            *pieces,
        ),
        after,
    )


def reduce_kernel(me, mixed, active, sent, kept, turned):
    half = turned.shape[0] // 2

    @pl.when(pl.program_id(0) == 0)
    def _():
        turned[...] = mixed[...].T

    core = me[0] & 1
    for out, place in ((sent, 1 - core), (kept, core)):
        left = turned[pl.ds(pl.multiple_of(place * half, half), half), :]
        part = low(dot(left, active[...]))
        columns = out.shape[2]
        for number in range(out.shape[0]):
            out[number] = part[:, number * columns : (number + 1) * columns]


def reduce_gradient(me, mixed, active, after=(), blocks=8, together=2):
    count, width = mixed.shape
    columns = active.shape[1] // blocks
    out = pl.BlockSpec((together, width // 2, columns), lambda s, me: (s, 0, 0))
    like = shaped((blocks, width // 2, columns))
    return call(
        reduce_kernel,
        "reduce_gradient",
        (blocks // together,),
        [
            whole((count, width)),
            pl.BlockSpec((count, columns * together), lambda s, me: (0, s)),
        ],
        [out, out],
        [like, like],
        [pltpu.VMEM((width, count), jnp.bfloat16)],
        (me, mixed, active),
        after,
    )


def expand_kernel(
    me,
    mixed,
    hidden,
    gate_part,
    slope_part,
    reduce_weight,
    gate_weight,
    up_weight,
    start,
    sent,
    kept,
    back,
    turned,
):
    @pl.when(pl.program_id(0) == 0)
    def _():
        turned[...] = hidden[...].T
        back[...] = start[...]

    weight = jnp.concatenate([gate_weight[...], up_weight[...]], 1)
    back_active = dot(mixed[...], reduce_weight[...], NT)
    both = jnp.concatenate(
        [low(back_active * wide(slope_part[...])), low(back_active * wide(gate_part[...]))], 1
    )
    back[...] += dot(both, weight, NT)
    gradient = low(dot(turned[...], both))
    chunk = gradient.shape[1] // 2
    first = me[0] & 1 == 0
    sent[0] = jnp.where(first, gradient[:, chunk:], gradient[:, :chunk])
    kept[0] = jnp.where(first, gradient[:, :chunk], gradient[:, chunk:])


def expand_gradient(
    me,
    mixed,
    hidden,
    gate_part,
    slope_part,
    reduce_weight,
    expand_weight,
    start,
    part,
    parts=2,
    after=(),
    chunk=768,
):
    count, width = mixed.shape
    inner = reduce_weight.shape[0]
    steps = inner // parts // chunk
    base = part * steps
    all_steps = inner // chunk
    rows = whole((count, width))
    column = pl.BlockSpec((count, chunk), lambda s, me: (0, base + s))
    out = pl.BlockSpec((1, width, chunk), lambda s, me: (s, 0, 0))
    like = shaped((steps, width, chunk))
    return call(
        expand_kernel,
        "expand_gradient",
        (steps,),
        [
            rows,
            rows,
            column,
            column,
            pl.BlockSpec((chunk, width), lambda s, me: (base + s, 0)),
            pl.BlockSpec((width, chunk), lambda s, me: (0, base + s)),
            pl.BlockSpec((width, chunk), lambda s, me: (0, all_steps + base + s)),
            rows,
        ],
        [out, out, rows],
        [like, like, shaped((count, width), jnp.float32)],
        [pltpu.VMEM((width, count), jnp.bfloat16)],
        (
            me,
            mixed,
            hidden,
            gate_part,
            slope_part,
            reduce_weight,
            expand_weight,
            expand_weight,
            start,
        ),
        after,
    )


def branch_kernel(
    me,
    back_hidden,
    normal,
    scale,
    first_gain,
    output_projection,
    one_out,
    back_attended,
    branch,
    gain_out,
    offset_out,
    *,
    block,
):
    count, width = back_hidden.shape
    gain = jnp.zeros((1, width), jnp.float32)
    offset = gain
    for start in range(0, count, block):
        rows = pl.ds(start, block)
        back = back_hidden[rows, :]
        gain += jnp.sum(back * normal[rows, :], axis=0, keepdims=True)
        offset += jnp.sum(back, axis=0, keepdims=True)
        one = norm_back(scale[rows, :1], normal[rows, :], back * first_gain[...][None])
        one_out[rows, :] = one
        branch[rows, :] = low(one)
        back_attended[rows, :] = low(dot(low(one), output_projection[...], NT))
    gain_out[...] = gain
    offset_out[...] = offset


def branch_back(me, back_hidden, normal, scale, first_gain, output_projection, after=(), block=256):
    count, width = back_hidden.shape
    rows = whole((count, width))
    vector = whole((1, width))
    return call(
        functools.partial(branch_kernel, block=block),
        "branch_back",
        (1,),
        [rows, rows, whole((count, 128)), whole((width,)), whole((width, width))],
        [rows, rows, rows, vector, vector],
        [
            shaped((count, width), jnp.float32),
            shaped((count, width)),
            shaped((count, width)),
            shaped((1, width), jnp.float32),
            shaped((1, width), jnp.float32),
        ],
        [],
        (me, back_hidden, normal, scale, first_gain, output_projection),
        after,
    )


def joint_kernel(me, tokens, attended, back_joint, branch, sent, kept, turned):
    step = pl.program_id(0)
    half = sent.shape[2]

    @pl.when(step == 0)
    def _():
        turned[...] = tokens[...].T

    @pl.when(step == 3)
    def _():
        turned[...] = attended[...].T

    def put(gradient):
        first = me[0] & 1 == 0
        sent[0] = jnp.where(first, gradient[:, half:], gradient[:, :half])
        kept[0] = jnp.where(first, gradient[:, :half], gradient[:, half:])

    @pl.when(step < 3)
    def _():
        put(low(dot(turned[...], back_joint[0])))

    @pl.when(step == 3)
    def _():
        put(low(dot(turned[...], branch[...])))


def joint_gradient(me, tokens, attended, back_joint, branch, after=()):
    count, width = tokens.shape
    rows = whole((count, width))
    out = pl.BlockSpec((1, width, width // 2), lambda s, me: (s, 0, 0))
    like = shaped((4, width, width // 2))
    return call(
        joint_kernel,
        "joint_gradient",
        (4,),
        [rows, rows, pl.BlockSpec((1, count, width), lambda s, me: (jnp.minimum(s, 2), 0, 0)), rows],
        [out, out],
        [like, like],
        [pltpu.VMEM((width, count), jnp.bfloat16)],
        (me, tokens, attended, back_joint, branch),
        after,
    )


def tokens_kernel(me, back_joint, weight, one, first, second, third, fourth, total):
    step = pl.program_id(0)
    part = dot(back_joint[0], weight[...], NT)

    @pl.when(step == 0)
    def _():
        total[...] = one[...] + part

    @pl.when(step == 1)
    def _():
        total[...] += part

    @pl.when(step == 2)
    def _():
        value = low(total[...] + part)
        quarter = first.shape[1]
        for place in range(value.shape[0] // quarter):
            rows = slice(place * quarter, (place + 1) * quarter)
            send_piece(me, place, value[rows], (first, second, third, fourth))


def tokens_gradient_of(me, back_joint, joint_projection, one, piece, after=()):
    _, count, width = back_joint.shape
    rows = whole((count, width))
    return call(
        tokens_kernel,
        "tokens_gradient",
        (3,),
        [
            pl.BlockSpec((1, count, width), lambda s, me: (s, 0, 0)),
            pl.BlockSpec((width, width), lambda s, me: (0, s)),
            rows,
        ],
        [whole(piece)] * 4,
        [shaped(piece)] * 4,
        [pltpu.VMEM((count, width), jnp.float32)],
        (me, back_joint, joint_projection, one),
        after,
    )


def exchange(value, axis, bit):
    sizes = (lax.axis_size("dp"), lax.axis_size("head"))
    pairs = []
    for dp in range(sizes[0]):
        for head in range(sizes[1]):
            target = (dp ^ bit, head) if axis == "dp" else (dp, head ^ bit)
            pairs.append((dp * sizes[1] + head, target[0] * sizes[1] + target[1]))
    return lax.ppermute(value, ("dp", "head"), pairs)


def pick(pieces, place):
    value = pieces[0]
    for number in range(1, len(pieces)):
        value = jnp.where(place == number, pieces[number], value)
    return value


def quarters_to_owners(values, row=None):
    groups = lax.axis_size("head")
    me = lax.axis_index("head")
    own = values.shape[0] // groups
    pieces = []
    for step in range(1, groups):
        start, size = (me ^ step) * own, own
        if row is not None:
            start, size = start + row, 1
        piece = lax.dynamic_slice_in_dim(values, start, size, axis=0)
        pieces.append(exchange(piece, "head", step))
    return pieces


def pieces_back(pieces):
    groups = lax.axis_size("head")
    me = lax.axis_index("head")
    come = [pieces[0]] + [exchange(pieces[step], "head", step) for step in range(1, groups)]
    return lambda: jnp.concatenate([pick(come, me ^ place) for place in range(groups)], axis=0)


class Sum:
    def __init__(self, sent, kept):
        self.bits = lax.axis_size("dp").bit_length() - 1
        self.lead = kept.ndim - 3
        self.tail = kept.shape[-2:]
        self.front = kept.shape[: self.lead]
        self.chosen = {}
        self.terms = [(self.split(kept), ())]
        self.coming = self.split(exchange(sent, "head", 1))

    def split(self, value):
        return value.reshape(self.front + (2,) * self.bits + self.tail)

    def total(self, wanted):
        value = None
        for term, cut in self.terms:
            starts = [0] * term.ndim
            sizes = list(term.shape)
            for axis, place in wanted.items():
                if axis not in cut:
                    starts[axis], sizes[axis] = place, 1
            piece = wide(lax.dynamic_slice(term, starts, sizes))
            value = piece if value is None else value + piece
        return value

    def arrive(self):
        if self.coming is not None:
            self.terms.append((self.coming, tuple(self.chosen)))
            self.coming = None

    def halve(self, step, token=None):
        self.arrive()
        if step == "y":
            axis, mine = 0, lax.axis_index("head") >> 1
        else:
            axis, mine = self.lead + self.bits - 1 - step, (lax.axis_index("dp") >> step) & 1
        away = dict(self.chosen)
        away[axis] = 1 - mine
        total = self.total(away)
        sent = low(total if token is None else total + token[0, 0])
        self.chosen[axis] = mine
        self.coming = exchange(sent, *(("head", 2) if step == "y" else ("dp", 1 << step)))
        return sent

    def own(self):
        self.arrive()
        value = low(self.total(self.chosen))
        return value.reshape(value.shape[: self.lead] + self.tail)


def sum_y(own):
    return low(wide(own) + wide(exchange(own, "head", 2)))


def join(own, bit, axis):
    other = exchange(own, "head", bit)
    first = lax.axis_index("head") & bit == 0
    return jnp.concatenate(
        (jnp.where(first, own, other), jnp.where(first, other, own)), axis=axis
    )


def local(
    tokens,
    segment_labels,
    joint_projection,
    output_projection,
    first_gain,
    first_offset,
    expand_weight,
    reduce_weight,
    second_gain,
    second_offset,
    cotangent,
):
    width = tokens.shape[2]
    length = segment_labels.shape[1]
    dp_size = lax.axis_size("dp")
    bits = dp_size.bit_length() - 1
    own_width = width // dp_size
    inner = reduce_weight.shape[0]
    me = lax.axis_index("head")
    group = jnp.reshape(me, (1,))
    up_order = list(range(bits))
    slopes = jnp.asarray(head_slopes(H), dtype=jnp.float32)
    row_count = tokens.shape[0] // lax.axis_size("head")
    flat = lambda value: value.reshape(row_count * length, width)
    rowed = lambda value: value.reshape(row_count, length, width)
    piece = (row_count,) + tokens.shape[1:]

    pieces = [quarters_to_owners(tokens, row) for row in range(row_count)]
    front = ()
    for row in range(row_count):
        front = attend(
            group, slopes, segment_labels, tokens, pieces[row], joint_projection, row, front
        )
        front, token = front[:-1], front[-1]
    own_tokens, queries, keys, values, probs, attended = front
    (
        normal,
        scale,
        hidden,
        gate_part,
        slope_part,
        active,
        *output,
        back_two,
        back_mixed,
        second_gain_back,
        second_offset_back,
        token,
    ) = ahead(
        group,
        flat(own_tokens),
        flat(attended),
        output_projection,
        first_gain,
        first_offset,
        expand_weight,
        reduce_weight,
        second_gain,
        second_offset,
        cotangent,
        quarters_to_owners(cotangent),
    )
    output = pieces_back(output)
    blocks = 8
    sent, kept, token = reduce_gradient(group, back_mixed, active)
    by_device = lambda value: (
        value.reshape(blocks, width // 2, dp_size // blocks, inner // dp_size)
        .transpose(0, 2, 1, 3)
        .reshape(dp_size, width // 2, inner // dp_size)
    )
    reduce_sum = Sum(by_device(sent), by_device(kept))
    reduce_order = up_order
    first_order = [1, 0] + up_order[2:]
    second_order = ["y"] + up_order
    rest = (group, back_mixed, hidden, gate_part, slope_part, reduce_weight, expand_weight)
    cut = lambda value: value.reshape(value.shape[0], dp_size, own_width, value.shape[2])
    sent, kept, back_hidden, token = expand_gradient(*rest, back_two, 0, after=[token])
    expand_first = Sum(cut(sent), cut(kept))
    moved = [reduce_sum.halve(reduce_order[0], token)]
    sent, kept, back_hidden, token = expand_gradient(*rest, back_hidden, 1, after=moved)
    expand_second = Sum(cut(sent), cut(kept))
    moved = [expand_first.halve(first_order[0], token)]
    back_one, back_attended, branch, first_gain_back, first_offset_back, token = branch_back(
        group, back_hidden, normal, scale, first_gain, output_projection, after=moved
    )
    moved = [
        expand_second.halve(second_order[0], token),
        reduce_sum.halve(reduce_order[1], token),
    ]
    back_joint, token = attend_back(
        group, queries, keys, values, probs, attended, rowed(back_attended), after=moved
    )
    back_joint = back_joint.reshape(3, -1, width)
    moved = [
        expand_first.halve(first_order[1], token),
        reduce_sum.halve(reduce_order[2], token),
    ]
    sent, kept, token = joint_gradient(
        group, flat(own_tokens), flat(attended), back_joint, branch, after=moved
    )
    vectors = jnp.concatenate(
        (first_gain_back, first_offset_back, second_gain_back, second_offset_back)
    ).reshape(8, width // 2)
    vectors = jnp.broadcast_to(
        low(jnp.pad(vectors, ((0, 8), (0, 0)))), (1, dp_size, 16, width // 2)
    )
    with_vectors = lambda value: jnp.concatenate((cut(value[2:]), jnp.pad(
        vectors, ((1, 0), (0, 0), (0, 0), (0, 0)))), axis=2)
    joint_sums = [Sum(cut(sent[:2]), cut(kept[:2])), Sum(with_vectors(sent), with_vectors(kept))]
    moved = [expand_second.halve(second_order[1], token)]
    *gradient, token = tokens_gradient_of(
        group, back_joint, joint_projection, back_one, piece, after=moved
    )
    gradient = pieces_back(gradient)
    joint_orders = [reduce_order, first_order]
    for place in range(bits):
        for number in range(2):
            joint_sums[number].halve(joint_orders[number][place], token)
        for step in reduce_order[3 + place : 4 + place]:
            reduce_sum.halve(step)
        for step in first_order[2 + place : 3 + place]:
            expand_first.halve(step)
        for step in second_order[2 + place : 3 + place]:
            expand_second.halve(step)

    reduce_grad = wide(join(sum_y(reduce_sum.own()), 1, 0).T)
    first_grad = join(sum_y(expand_first.own())[None], 1, 0)
    second_grad = join(join(expand_second.own(), 2, 0)[None], 1, 0)
    expand_grad = jnp.concatenate(
        [
            piece
            for side in range(2)
            for piece in (
                first_grad[side, 0],
                first_grad[side, 1],
                second_grad[side, 0],
                second_grad[side, 1],
            )
        ],
        axis=-1,
    )
    first_own = sum_y(joint_sums[0].own())
    second_own = sum_y(joint_sums[1].own())
    vectors = wide(second_own[1, own_width : own_width + 8]).reshape(4, width)
    joint_grad = join(
        jnp.concatenate((first_own, second_own[:, :own_width]), axis=0), 1, 2
    )
    vectors = lax.dynamic_slice_in_dim(
        vectors, lax.axis_index("dp") * own_width, own_width, axis=1
    )
    return (
        output(),
        gradient(),
        wide(jnp.concatenate([joint_grad[0], joint_grad[1], joint_grad[2]], axis=-1)),
        wide(joint_grad[3]),
        vectors[0],
        vectors[1],
        wide(expand_grad),
        reduce_grad,
        vectors[2],
        vectors[3],
    )


def solution(mesh):
    placed = (
        P("dp", "head", None),
        P("dp", None),
        P(),
        P(),
        P(),
        P(),
        P(),
        P(),
        P(),
        P(),
        P("dp", "head", None),
    )
    return jax.shard_map(
        local,
        mesh=mesh,
        in_specs=placed,
        out_specs=(
            P("dp", "head", None),
            P("dp", "head", None),
            P("dp", None),
            P("dp", None),
            P("dp"),
            P("dp"),
            P("dp", None),
            P("dp", None),
            P("dp"),
            P("dp"),
        ),
        check_vma=False,
    )
```

```python
import functools
import math

import jax
import jax.numpy as jnp
import numpy as np
from jax import lax
from jax.experimental import pallas as pl
from jax.experimental.pallas import tpu as pltpu
from jax.sharding import PartitionSpec as P

H = 12
DH = 64


EPSILON = 1e-12
NEG_FILL = -1e30
LOG2E = 1.4426950408889634
NN = (((1,), (0,)), ((), ()))
NT = (((1,), (1,)), ((), ()))
TN = (((0,), (0,)), ((), ()))
VMEM_BYTES = 63 * 2**20
ANY = pl.BlockSpec(memory_space=pl.ANY)
SMEM = pl.BlockSpec(memory_space=pltpu.SMEM)


def head_slopes(heads_total):
    closest = 2 ** int(math.floor(math.log2(heads_total)))

    def power_slopes(number):
        first_slope = 2.0 ** (-8.0 / number)
        return [first_slope ** (counter + 1) for counter in range(number)]

    listed = power_slopes(closest)
    listed = listed + power_slopes(2 * closest)[0::2][: heads_total - closest]
    return np.array(listed, dtype=np.float32)


def low(value):
    return value.astype(jnp.bfloat16)


def wide(value):
    return value.astype(jnp.float32)


def dot(left, right, dims=NN):
    return lax.dot_general(left, right, dims, preferred_element_type=jnp.float32)


def shaped(shape, dtype=jnp.bfloat16):
    return jax.ShapeDtypeStruct(shape, dtype)


def whole(shape):
    return pl.BlockSpec(shape, lambda *_: (0,) * len(shape))


def later(value, *arrays):
    if not arrays:
        return value
    token = lax.optimization_barrier((lax.create_token(), *arrays))[0]
    return lax.optimization_barrier((token, value))[1]


def call(kernel, name, grid, in_specs, out_specs, out_shape, scratch, operands, after, into=()):
    operands = (later(operands[0], *after),) + tuple(operands[1:])
    count = len(operands) - 1
    extra = len(into)

    def run(me, *refs):
        kernel(me, *refs[:count], *refs[count + extra :])

    return pl.pallas_call(
        run,
        grid_spec=pltpu.PrefetchScalarGridSpec(
            num_scalar_prefetch=1,
            grid=grid,
            in_specs=list(in_specs) + [ANY] * extra,
            out_specs=list(out_specs),
            scratch_shapes=scratch,
        ),
        out_shape=list(out_shape),
        input_output_aliases={count + 1 + number: number for number in range(len(into))},
        compiler_params=pltpu.CompilerParams(
            vmem_limit_bytes=VMEM_BYTES, dimension_semantics=("arbitrary",) * len(grid)
        ),
        cost_estimate=pl.CostEstimate(flops=10**12, bytes_accessed=0, transcendentals=0),
        name=name,
    )(*operands, *into)


def normalize(value):
    center = value - jnp.mean(value, axis=-1, keepdims=True)
    scale = lax.rsqrt(jnp.mean(center * center, axis=-1, keepdims=True) + EPSILON)
    return center * scale, scale


def norm_back(scale, normal, back):
    return scale * (
        back
        - jnp.mean(back, axis=-1, keepdims=True)
        - normal * jnp.mean(back * normal, axis=-1, keepdims=True)
    )


def attend_kernel(
    me,
    slopes,
    labels,
    first,
    second,
    third,
    fourth,
    query_weight,
    key_weight,
    value_weight,
    tokens_out,
    queries_out,
    keys_out,
    values_out,
    probs_out,
    attended_out,
    bias,
    *,
    row,
    heads,
):
    group = pl.program_id(0)
    _, length, width = tokens_out.shape
    quarter = length // 4

    @pl.when(group == 0)
    def _():
        for step, piece in enumerate((first, second, third, fourth)):
            place = pl.multiple_of((me[0] ^ step) * quarter, quarter)
            tokens_out[0, pl.ds(place, quarter), :] = piece[0]
        label = labels[pl.ds(me[0] * 2 + row, 1), :]
        column = jnp.broadcast_to(label, (128, length)).T[:, :1]
        rows = lax.broadcasted_iota(jnp.int32, (length, length), 0)
        columns = lax.broadcasted_iota(jnp.int32, (length, length), 1)
        gap = -wide(jnp.abs(rows - columns))
        bias[...] = jnp.where(column == label, gap, NEG_FILL)

    tokens = tokens_out[0]
    queries = low(dot(tokens, query_weight[...]))
    keys = low(dot(tokens, key_weight[...]))
    values = low(dot(tokens, value_weight[...]))
    queries_out[0] = queries
    keys_out[0] = keys
    values_out[0] = values
    owner = lax.broadcasted_iota(jnp.int32, keys.shape, 1) // DH
    turned = values.T
    parts = []
    for head in range(heads):
        slope = slopes[group * heads + head] * LOG2E
        own_keys = jnp.where(owner == head, keys, jnp.zeros_like(keys))
        scores = dot(own_keys, queries, NT) * (DH**-0.5 * LOG2E) + bias[...] * slope
        exponent = jnp.exp2(scores - jnp.max(scores, axis=0, keepdims=True))
        probs = low(exponent * (1.0 / jnp.sum(exponent, axis=0, keepdims=True)))
        probs_out[0, head] = probs
        parts.append(dot(turned[head * DH : (head + 1) * DH], probs))
    attended_out[0] = low(jnp.concatenate(parts, axis=0).T)


def attend(me, slopes, labels, tokens, pieces, joint_projection, row, into=(), heads=4):
    _, quarter, width = tokens.shape
    length = labels.shape[1]
    rows = tokens.shape[0] // 4
    groups = H // heads
    group_width = heads * DH
    weight = [
        pl.BlockSpec((width, group_width), lambda g, me, which=which: (0, which * groups + g))
        for which in range(3)
    ]
    out = pl.BlockSpec((1, length, group_width), lambda g, me: (row, 0, g))
    like = shaped((rows, length, width))
    return call(
        functools.partial(attend_kernel, row=row, heads=heads),
        "attend",
        (groups,),
        [
            SMEM,
            whole(labels.shape),
            pl.BlockSpec((1, quarter, width), lambda g, me: (me[0] * rows + row, 0, 0)),
        ]
        + [whole((1, quarter, width))] * 3
        + weight,
        [pl.BlockSpec((1, length, width), lambda g, me: (row, 0, 0)), out, out, out]
        + [pl.BlockSpec((1, heads, length, length), lambda g, me: (row, g, 0, 0)), out],
        [like, like, like, like, shaped((rows, H, length, length)), like],
        [pltpu.VMEM((length, length), jnp.float32)],
        (me, slopes, labels, tokens, *pieces) + (joint_projection,) * 3,
        (),
        into,
    )


def attend_back_kernel(
    me, queries_ref, keys_ref, values_ref, probs_ref, attended, back_attended, back_joint, *, heads
):
    queries, keys, values = queries_ref[0], keys_ref[0], values_ref[0]
    back = back_attended[0]
    owner = lax.broadcasted_iota(jnp.int32, keys.shape, 1) // DH
    zero = jnp.zeros_like(keys)
    product = (wide(attended[0]) * wide(back)).T
    turned = keys.T
    probs_all, scores_all, back_all, queries_all, parts = [], [], [], [], []
    for head in range(heads):
        mine = owner == head
        lanes = slice(head * DH, (head + 1) * DH)
        inner = jnp.sum(product[lanes], axis=0, keepdims=True)
        back_probs = dot(jnp.where(mine, values, zero), back, NT)
        probs = probs_ref[0, head]
        back_scores = low(wide(probs) * (back_probs - inner))
        probs_all.append(probs)
        scores_all.append(back_scores)
        back_all.append(jnp.where(mine, back, zero))
        queries_all.append(jnp.where(mine, queries, zero))
        parts.append(dot(turned[lanes], back_scores))
    scale = DH**-0.5
    back_joint[2, 0] = low(dot(jnp.concatenate(probs_all, 1), jnp.concatenate(back_all, 0)))
    back_joint[1, 0] = low(
        dot(jnp.concatenate(scores_all, 1), jnp.concatenate(queries_all, 0)) * scale
    )
    back_joint[0, 0] = low(jnp.concatenate(parts, 0).T * scale)


def attend_back(
    me, queries, keys, values, probs, attended, back_attended, base, groups, after=(), heads=4
):
    rows, length, _ = queries.shape
    group_width = heads * DH
    spec = pl.BlockSpec((1, length, group_width), lambda r, g, me: (r, 0, base + g))
    return call(
        functools.partial(attend_back_kernel, heads=heads),
        "attend_back",
        (rows, groups),
        [spec] * 3
        + [
            pl.BlockSpec((1, heads, length, length), lambda r, g, me: (r, base + g, 0, 0)),
            spec,
            spec,
        ],
        [pl.BlockSpec((3, 1, length, group_width), lambda r, g, me: (0, r, 0, g))],
        [shaped((3, rows, length, groups * group_width))],
        [],
        (me, queries, keys, values, probs, attended, back_attended),
        after,
    )


def send_piece(me, place, value, outs):
    for number, out in enumerate(outs):

        @pl.when((place % 4) ^ number == me[0])
        def _():
            out[place // 4] = value


def ahead_kernel(
    me,
    tokens,
    attended,
    output_projection,
    first_gain,
    first_offset,
    gate_weight,
    up_weight,
    reduce_weight,
    normal_out,
    scale_out,
    hidden_out,
    gate_out,
    slope_out,
    active_out,
    total,
    *,
    block,
):
    step = pl.program_id(0)
    count, width = tokens.shape
    blocks = [pl.ds(start, block) for start in range(0, count, block)]

    @pl.when(step == 0)
    def _():
        for rows in blocks:
            branch = dot(attended[rows, :], output_projection[...])
            normal, scale = normalize(wide(tokens[rows, :]) + branch)
            normal_out[rows, :] = normal
            scale_out[rows, :] = jnp.broadcast_to(scale, (block, scale_out.shape[1]))
            hidden = normal * first_gain[...][None] + first_offset[...][None]
            hidden_out[rows, :] = low(hidden)
            total[rows, :] = hidden

    for rows in blocks:
        hidden = hidden_out[rows, :]
        gate = dot(hidden, gate_weight[...])
        up = dot(hidden, up_weight[...])
        share = 0.5 * (1.0 + lax.erf(gate * 0.5**0.5))
        density = jnp.exp(gate * gate * -0.5) * (2.0 * math.pi) ** -0.5
        unit = gate * share
        active = low(unit * up)
        gate_out[rows, :] = low(unit)
        slope_out[rows, :] = low(up * (share + gate * density))
        active_out[rows, :] = active
        total[rows, :] += dot(active, reduce_weight[...])


def ahead(
    me,
    tokens,
    attended,
    output_projection,
    first_gain,
    first_offset,
    expand_weight,
    reduce_weight,
    after=(),
    chunk=512,
    block=256,
):
    count, width = tokens.shape
    inner = reduce_weight.shape[0]
    steps = inner // chunk
    vector = whole((width,))
    rows = whole((count, width))
    column = pl.BlockSpec((count, chunk), lambda s, me: (0, s))
    return call(
        functools.partial(ahead_kernel, block=block),
        "ahead",
        (steps,),
        [
            rows,
            rows,
            whole((width, width)),
            vector,
            vector,
            pl.BlockSpec((width, chunk), lambda s, me: (0, s)),
            pl.BlockSpec((width, chunk), lambda s, me: (0, s + steps)),
            pl.BlockSpec((chunk, width), lambda s, me: (s, 0)),
        ],
        [rows, whole((count, 128)), rows, column, column, column, rows],
        [
            shaped((count, width), jnp.float32),
            shaped((count, 128), jnp.float32),
            shaped((count, width)),
            shaped((count, inner)),
            shaped((count, inner)),
            shaped((count, inner)),
            shaped((count, width), jnp.float32),
        ],
        [],
        (
            me,
            tokens,
            attended,
            output_projection,
            first_gain,
            first_offset,
            expand_weight,
            expand_weight,
            reduce_weight,
        ),
        after,
    )


def reduce_kernel(
    me,
    total,
    second_gain,
    second_offset,
    first,
    second,
    third,
    fourth,
    active,
    output_first,
    output_second,
    output_third,
    output_fourth,
    two_out,
    mixed_out,
    gain_out,
    offset_out,
    sent,
    kept,
    cotangent,
    turned,
):
    half = turned.shape[0] // 2

    @pl.when(pl.program_id(0) == 0)
    def _():
        count, width = total.shape
        quarter = first.shape[1]
        for number, piece in enumerate((first, second, third, fourth)):
            for row in range(piece.shape[0]):
                place = (row * 4 + (me[0] ^ number)) * quarter
                cotangent[pl.ds(pl.multiple_of(place, quarter), quarter), :] = piece[row]
        gain = jnp.zeros((1, width), jnp.float32)
        offset = gain
        for start in range(0, count, quarter):
            rows = pl.ds(start, quarter)
            normal, scale = normalize(total[rows, :])
            send_piece(
                me,
                start // quarter,
                low(normal * second_gain[...][None] + second_offset[...][None]),
                (output_first, output_second, output_third, output_fourth),
            )
            back = wide(cotangent[rows, :])
            gain += jnp.sum(back * normal, axis=0, keepdims=True)
            offset += jnp.sum(back, axis=0, keepdims=True)
            two = norm_back(scale, normal, back * second_gain[...][None])
            two_out[rows, :] = two
            mixed_out[rows, :] = low(two)
        gain_out[...] = gain
        offset_out[...] = offset
        turned[...] = mixed_out[...].T

    core = me[0] & 1
    for out, place in ((sent, 1 - core), (kept, core)):
        left = turned[pl.ds(pl.multiple_of(place * half, half), half), :]
        part = low(dot(left, active[...]))
        columns = out.shape[2]
        for number in range(out.shape[0]):
            out[number] = part[:, number * columns : (number + 1) * columns]


def reduce_gradient(
    me,
    total,
    second_gain,
    second_offset,
    cotangent,
    pieces,
    active,
    after=(),
    blocks=8,
    together=2,
):
    count, width = total.shape
    columns = active.shape[1] // blocks
    piece = pieces[0].shape
    rows = whole((count, width))
    vector = whole((1, width))
    out = pl.BlockSpec((together, width // 2, columns), lambda s, me: (s, 0, 0))
    like = shaped((blocks, width // 2, columns))
    return call(
        reduce_kernel,
        "reduce_gradient",
        (blocks // together,),
        [
            rows,
            whole((width,)),
            whole((width,)),
            pl.BlockSpec(piece, lambda s, me: (me[0], 0, 0)),
        ]
        + [whole(piece)] * 3
        + [pl.BlockSpec((count, columns * together), lambda s, me: (0, s))],
        [whole(piece)] * 4 + [rows, rows, vector, vector, out, out],
        [shaped(piece)] * 4
        + [
            shaped((count, width), jnp.float32),
            shaped((count, width)),
            shaped((1, width), jnp.float32),
            shaped((1, width), jnp.float32),
            like,
            like,
        ],
        [pltpu.VMEM((count, width), jnp.bfloat16), pltpu.VMEM((width, count), jnp.bfloat16)],
        (me, total, second_gain, second_offset, cotangent, *pieces, active),
        after,
    )


def expand_kernel(
    me,
    mixed,
    hidden,
    gate_part,
    slope_part,
    reduce_weight,
    gate_weight,
    up_weight,
    start,
    sent,
    kept,
    back,
    turned,
):
    @pl.when(pl.program_id(0) == 0)
    def _():
        turned[...] = hidden[...].T
        back[...] = start[...]

    weight = jnp.concatenate([gate_weight[...], up_weight[...]], 1)
    back_active = dot(mixed[...], reduce_weight[...], NT)
    both = jnp.concatenate(
        [low(back_active * wide(slope_part[...])), low(back_active * wide(gate_part[...]))], 1
    )
    back[...] += dot(both, weight, NT)
    gradient = low(dot(turned[...], both))
    chunk = gradient.shape[1] // 2
    first = me[0] & 1 == 0
    sent[...] = jnp.where(first, gradient[:, chunk:], gradient[:, :chunk]).reshape(sent.shape)
    kept[...] = jnp.where(first, gradient[:, :chunk], gradient[:, chunk:]).reshape(kept.shape)


def expand_gradient(
    me,
    mixed,
    hidden,
    gate_part,
    slope_part,
    reduce_weight,
    expand_weight,
    start,
    part,
    lead,
    parts=2,
    after=(),
    chunk=768,
):
    count, width = mixed.shape
    inner = reduce_weight.shape[0]
    steps = inner // parts // chunk
    base = part * steps
    all_steps = inner // chunk
    rows = whole((count, width))
    column = pl.BlockSpec((count, chunk), lambda s, me: (0, base + s))
    if lead:
        out = pl.BlockSpec((1, width, chunk), lambda s, me: (s, 0, 0))
        like = shaped((steps, width, chunk))
    else:
        out = pl.BlockSpec((width, chunk), lambda s, me: (0, s))
        like = shaped((width, steps * chunk))
    return call(
        expand_kernel,
        "expand_gradient",
        (steps,),
        [
            rows,
            rows,
            column,
            column,
            pl.BlockSpec((chunk, width), lambda s, me: (base + s, 0)),
            pl.BlockSpec((width, chunk), lambda s, me: (0, base + s)),
            pl.BlockSpec((width, chunk), lambda s, me: (0, all_steps + base + s)),
            rows,
        ],
        [out, out, rows],
        [like, like, shaped((count, width), jnp.float32)],
        [pltpu.VMEM((width, count), jnp.bfloat16)],
        (
            me,
            mixed,
            hidden,
            gate_part,
            slope_part,
            reduce_weight,
            expand_weight,
            expand_weight,
            start,
        ),
        after,
    )


def branch_kernel(
    me,
    back_hidden,
    normal,
    scale,
    first_gain,
    output_projection,
    one_out,
    back_attended,
    branch,
    gain_out,
    offset_out,
    *,
    block,
):
    count, width = back_hidden.shape
    gain = jnp.zeros((1, width), jnp.float32)
    offset = gain
    for start in range(0, count, block):
        rows = pl.ds(start, block)
        back = back_hidden[rows, :]
        gain += jnp.sum(back * normal[rows, :], axis=0, keepdims=True)
        offset += jnp.sum(back, axis=0, keepdims=True)
        one = norm_back(scale[rows, :1], normal[rows, :], back * first_gain[...][None])
        one_out[rows, :] = one
        branch[rows, :] = low(one)
        back_attended[rows, :] = low(dot(low(one), output_projection[...], NT))
    gain_out[...] = gain
    offset_out[...] = offset


def branch_back(me, back_hidden, normal, scale, first_gain, output_projection, after=(), block=256):
    count, width = back_hidden.shape
    rows = whole((count, width))
    vector = whole((1, width))
    return call(
        functools.partial(branch_kernel, block=block),
        "branch_back",
        (1,),
        [rows, rows, whole((count, 128)), whole((width,)), whole((width, width))],
        [rows, rows, rows, vector, vector],
        [
            shaped((count, width), jnp.float32),
            shaped((count, width)),
            shaped((count, width)),
            shaped((1, width), jnp.float32),
            shaped((1, width), jnp.float32),
        ],
        [],
        (me, back_hidden, normal, scale, first_gain, output_projection),
        after,
    )


def joint_kernel(
    me, tokens, attended, back_joint, branch, vectors, sent, kept, turned
):
    step = pl.program_id(0)

    @pl.when(step == 0)
    def _():
        turned[...] = tokens[...].T

    @pl.when(step == 3)
    def _():
        turned[...] = attended[...].T

    def put(gradient, start):
        half = gradient.shape[1] // 2
        first = me[0] & 1 == 0
        place = slice(start, start + half)
        sent[:, place] = jnp.where(first, gradient[:, half:], gradient[:, :half])
        kept[:, place] = jnp.where(first, gradient[:, :half], gradient[:, half:])

    half = back_joint.shape[2] // 2
    for which in range(3):

        @pl.when(step == which)
        def _():
            put(low(dot(turned[...], back_joint[0])), which * half)

    @pl.when(step == 3)
    def _():
        put(low(dot(turned[...], branch[...])), 3 * half)
        rows = jnp.concatenate(
            [vectors[...], jnp.zeros((128 - vectors.shape[0], vectors.shape[1]), jnp.float32)]
        )
        columns = low(rows.T)
        sent[:, sent.shape[1] - 128 :] = columns
        kept[:, kept.shape[1] - 128 :] = columns


def joint_gradient(me, tokens, attended, back_joint, branch, vectors, after=()):
    count, width = tokens.shape
    columns = back_joint.shape[2]
    rows = whole((count, width))
    out = (width, 3 * columns // 2 + width // 2 + 128)
    return call(
        joint_kernel,
        "joint_gradient",
        (4,),
        [
            rows,
            rows,
            pl.BlockSpec((1, count, columns), lambda s, me: (jnp.minimum(s, 2), 0, 0)),
            rows,
            whole(vectors.shape),
        ],
        [whole(out)] * 2,
        [shaped(out)] * 2,
        [pltpu.VMEM((width, count), jnp.bfloat16)],
        (me, tokens, attended, back_joint, branch, vectors),
        after,
    )


def joint_end_kernel(me, tokens, back_joint, sent, kept):
    turned = tokens[...].T
    gradients = [low(dot(turned, back_joint[which])) for which in range(3)]
    half = back_joint.shape[2] // 2
    front = jnp.concatenate([gradient[:, :half] for gradient in gradients], axis=1)
    back = jnp.concatenate([gradient[:, half:] for gradient in gradients], axis=1)
    first = me[0] & 1 == 0
    sent[...] = jnp.where(first, back, front)
    kept[...] = jnp.where(first, front, back)


def joint_gradient_end(me, tokens, back_joint, after=()):
    count, width = tokens.shape
    columns = back_joint.shape[2]
    out = (width, 3 * columns // 2)
    return call(
        joint_end_kernel,
        "joint_gradient_end",
        (1,),
        [whole((count, width)), whole((3, count, columns))],
        [whole(out)] * 2,
        [shaped(out)] * 2,
        [],
        (me, tokens, back_joint),
        after,
    )


def tokens_kernel(me, front, back, weight, one, first, second, third, fourth, total):
    step = pl.program_id(0)
    columns = front.shape[2]
    part = dot(front[0], weight[:, :columns], NT) + dot(back[0], weight[:, columns:], NT)

    @pl.when(step == 0)
    def _():
        total[...] = one[...] + part

    @pl.when(step == 1)
    def _():
        total[...] += part

    @pl.when(step == 2)
    def _():
        value = low(total[...] + part)
        quarter = first.shape[1]
        for place in range(value.shape[0] // quarter):
            rows = slice(place * quarter, (place + 1) * quarter)
            send_piece(me, place, value[rows], (first, second, third, fourth))


def tokens_gradient_of(me, front, back, joint_projection, one, piece, after=()):
    count, width = one.shape
    rows = whole((count, width))
    return call(
        tokens_kernel,
        "tokens_gradient",
        (3,),
        [pl.BlockSpec((1, count, part.shape[2]), lambda s, me: (s, 0, 0)) for part in (front, back)]
        + [
            pl.BlockSpec((width, width), lambda s, me: (0, s)),
            rows,
        ],
        [whole(piece)] * 4,
        [shaped(piece)] * 4,
        [pltpu.VMEM((count, width), jnp.float32)],
        (me, front, back, joint_projection, one),
        after,
    )


def turn_kernel(me, own, other, out):
    half = own.shape[0]
    mine, others = wide(own[...]).T, wide(other[...]).T
    first = me[0] & 1 == 0
    out[:, :half] = jnp.where(first, mine, others)
    out[:, half:] = jnp.where(first, others, mine)


def turn(me, own, other):
    half, count = own.shape
    return call(
        turn_kernel,
        "turn",
        (1,),
        [whole((half, count))] * 2,
        [whole((count, 2 * half))],
        [shaped((count, 2 * half), jnp.float32)],
        [],
        (me, own, other),
        (),
    )[0]


def exchange(value, axis, bit):
    sizes = (lax.axis_size("dp"), lax.axis_size("head"))
    pairs = []
    for dp in range(sizes[0]):
        for head in range(sizes[1]):
            target = (dp ^ bit, head) if axis == "dp" else (dp, head ^ bit)
            pairs.append((dp * sizes[1] + head, target[0] * sizes[1] + target[1]))
    return lax.ppermute(value, ("dp", "head"), pairs)


def pick(pieces, place):
    value = pieces[0]
    for number in range(1, len(pieces)):
        value = jnp.where(place == number, pieces[number], value)
    return value


def quarters_to_owners(values, row=None):
    groups = lax.axis_size("head")
    me = lax.axis_index("head")
    own = values.shape[0] // groups
    pieces = []
    for step in range(1, groups):
        start, size = (me ^ step) * own, own
        if row is not None:
            start, size = start + row, 1
        pieces.append(lax.dynamic_slice_in_dim(values, start, size, axis=0))
    return pieces, lambda *after: [
        exchange(later(pieces[step - 1], *after), "head", step) for step in range(1, groups)
    ]


def pieces_back(pieces):
    groups = lax.axis_size("head")
    me = lax.axis_index("head")
    come = [pieces[0]] + [exchange(pieces[step], "head", step) for step in range(1, groups)]

    def finish(*after):
        ready = [later(piece, *after) for piece in come]
        return jnp.concatenate([pick(ready, me ^ place) for place in range(groups)], axis=0)

    return finish


class Sum:
    def __init__(self, sent, kept):
        self.bits = lax.axis_size("dp").bit_length() - 1
        self.lead = kept.ndim - 3
        self.tail = kept.shape[-2:]
        self.front = kept.shape[: self.lead]
        self.chosen = {}
        self.terms = [(self.split(kept), ())]
        self.coming = self.split(exchange(sent, "head", 1))

    def split(self, value):
        return value.reshape(self.front + (2,) * self.bits + self.tail)

    def total(self, wanted, after=()):
        value = None
        for term, cut in self.terms:
            term = later(term, *after)
            starts = [0] * term.ndim
            sizes = list(term.shape)
            for axis, place in wanted.items():
                if axis not in cut:
                    starts[axis], sizes[axis] = place, 1
            piece = wide(lax.dynamic_slice(term, starts, sizes))
            value = piece if value is None else value + piece
        return value

    def arrive(self):
        if self.coming is not None:
            self.terms.append((self.coming, tuple(self.chosen)))
            self.coming = None

    def halve(self, step, *after):
        self.arrive()
        if step == "y":
            axis, mine = 0, lax.axis_index("head") >> 1
        else:
            axis, mine = self.lead + self.bits - 1 - step, (lax.axis_index("dp") >> step) & 1
        away = dict(self.chosen)
        away[axis] = 1 - mine
        sent = low(self.total(away, after))
        self.chosen[axis] = mine
        self.coming = exchange(sent, *(("head", 2) if step == "y" else ("dp", 1 << step)))
        return sent

    def rest(self, steps, *after):
        for step in steps:
            self.halve(step, *after)
        return self.own(*after)

    def own(self, *after):
        self.arrive()
        value = low(self.total(self.chosen, after))
        return value.reshape(value.shape[: self.lead] + self.tail)


def sum_y(own, *after):
    other = exchange(own, "head", 2)
    return low(wide(later(own, *after)) + wide(other))


def join(own, bit, axis, *after):
    own = later(own, *after)
    other = exchange(own, "head", bit)
    first = lax.axis_index("head") & bit == 0
    return jnp.concatenate(
        (jnp.where(first, own, other), jnp.where(first, other, own)), axis=axis
    )


def local(
    tokens,
    segment_labels,
    joint_projection,
    output_projection,
    first_gain,
    first_offset,
    expand_weight,
    reduce_weight,
    second_gain,
    second_offset,
    cotangent,
):
    width = tokens.shape[2]
    length = segment_labels.shape[1]
    dp_size = lax.axis_size("dp")
    bits = dp_size.bit_length() - 1
    own_width = width // dp_size
    inner = reduce_weight.shape[0]
    me = lax.axis_index("head")
    group = jnp.reshape(me, (1,))
    up_order = list(range(bits))
    slopes = jnp.asarray(head_slopes(H), dtype=jnp.float32)
    row_count = tokens.shape[0] // lax.axis_size("head")
    flat = lambda value: value.reshape(row_count * length, width)
    rowed = lambda value: value.reshape(row_count, length, width)
    piece = (row_count,) + tokens.shape[1:]

    pieces = [quarters_to_owners(tokens, row)[1]() for row in range(row_count)]
    early, exchange_cotangent = quarters_to_owners(cotangent)
    front = ()
    for row in range(row_count):
        front = attend(
            later(group, *early),
            slopes,
            segment_labels,
            tokens,
            pieces[row],
            joint_projection,
            row,
            front,
        )
    own_tokens, queries, keys, values, probs, attended = front
    cotangent_pieces = exchange_cotangent(attended)
    normal, scale, hidden, gate_part, slope_part, active, total = ahead(
        group,
        flat(own_tokens),
        flat(attended),
        output_projection,
        first_gain,
        first_offset,
        expand_weight,
        reduce_weight,
    )
    blocks = 8
    *output, back_two, back_mixed, second_gain_back, second_offset_back, sent, kept = (
        reduce_gradient(
            group, total, second_gain, second_offset, cotangent, cotangent_pieces, active
        )
    )
    output = pieces_back(output)
    by_device = lambda value: (
        value.reshape(blocks, width // 2, dp_size // blocks, inner // dp_size)
        .transpose(0, 2, 1, 3)
        .reshape(dp_size, width // 2, inner // dp_size)
    )
    reduce_sum = Sum(by_device(sent), by_device(kept))
    reduce_order = up_order
    first_order = [1, 0] + up_order[2:]
    second_order = ["y"] + up_order
    rest = (group, back_mixed, hidden, gate_part, slope_part, reduce_weight, expand_weight)
    cut = lambda value: value.reshape(value.shape[0], dp_size, own_width, value.shape[2])
    sent, kept, back_hidden = expand_gradient(*rest, back_two, 0, False, after=[kept])
    slab = lambda value: value.reshape(dp_size, own_width, value.shape[1])
    expand_first = Sum(slab(sent), slab(kept))
    output = output(back_hidden)
    moved = [reduce_sum.halve(reduce_order[0], back_hidden), output]
    sent, kept, back_hidden = expand_gradient(*rest, back_hidden, 1, True, after=moved)
    expand_second = Sum(cut(sent), cut(kept))
    moved = [expand_first.halve(first_order[0], back_hidden)]
    back_one, back_attended, branch, first_gain_back, first_offset_back = branch_back(
        group, back_hidden, normal, scale, first_gain, output_projection, after=moved
    )
    moved = [
        expand_second.halve(second_order[0], back_one),
        reduce_sum.halve(reduce_order[1], back_one),
    ]
    heads = (group, queries, keys, values, probs, attended, rowed(back_attended))
    columns = lambda value: value.reshape(3, row_count * length, value.shape[3])
    front = columns(attend_back(*heads, 0, 2, after=moved)[0])
    moved = [
        expand_first.halve(first_order[1], front),
        reduce_sum.halve(reduce_order[2], front),
    ]
    vectors = jnp.concatenate(
        (first_gain_back, first_offset_back, second_gain_back, second_offset_back)
    )
    sent, kept = joint_gradient(
        group, flat(own_tokens), flat(attended), front, branch, vectors, after=moved
    )
    joint_first = Sum(slab(sent), slab(kept))
    moved = [expand_second.halve(second_order[1], kept)]
    back = columns(attend_back(*heads, 2, 1, after=moved)[0])
    joint_order = first_order
    last_order = reduce_order
    reduce_own = reduce_sum.rest(reduce_order[3:], back)
    moved = [joint_first.halve(joint_order[0], back), reduce_own]
    sent, kept = joint_gradient_end(group, flat(own_tokens), back, after=moved)
    joint_last = Sum(slab(sent), slab(kept))
    reduce_own = sum_y(reduce_own)
    moved = [expand_first.halve(first_order[2], kept)]
    gradient = tokens_gradient_of(
        group, front, back, joint_projection, back_one, piece, after=moved
    )
    done = gradient[0]
    gradient = pieces_back(gradient)
    moved = [joint_last.halve(last_order[0], done)]
    joint_first.halve(joint_order[1], *moved)
    expand_second.halve(second_order[2], *moved)
    moved = [joint_last.halve(last_order[1])]
    first_own = expand_first.rest(first_order[3:], *moved)
    joint_first.halve(joint_order[2], *moved)
    expand_second.halve(second_order[3], *moved)
    first_own = sum_y(first_own)
    moved = [joint_last.halve(last_order[2])]
    first_grad = join(first_own[None], 1, 0, *moved)
    joint_own = [joint_first.rest(joint_order[3:]), joint_last.rest(last_order[3:])]
    joint_own = [sum_y(part) for part in joint_own]
    second_own = expand_second.rest(second_order[4:], *joint_own)
    second_grad = join(join(second_own, 2, 0)[None], 1, 0)
    reduce_grad = turn(group, reduce_own, exchange(later(reduce_own, *joint_own), "head", 1))
    expand_grad = jnp.concatenate(
        [
            piece
            for side in range(2)
            for piece in (
                first_grad[side],
                second_grad[side, 0],
                second_grad[side, 1],
            )
        ],
        axis=-1,
    )
    joint_own[0] = joint_own[0].reshape(own_width, -1)
    vectors = wide(joint_own[0][:, -128:-124])
    both = join(jnp.concatenate((joint_own[0][:, :-128], joint_own[1]), axis=1)[None], 1, 0)
    size = front.shape[2] // 2
    last = back.shape[2] // 2
    start = 3 * size + width // 2
    joint_grad = []
    for which in range(3):
        for begin, count in ((which * size, size), (start + which * last, last)):
            joint_grad += [both[side, :, begin : begin + count] for side in range(2)]
    projection_grad = [both[side, :, 3 * size : start] for side in range(2)]
    return (
        output,
        gradient(),
        wide(jnp.concatenate(joint_grad, axis=-1)),
        wide(jnp.concatenate(projection_grad, axis=-1)),
        vectors[:, 0],
        vectors[:, 1],
        wide(expand_grad),
        reduce_grad,
        vectors[:, 2],
        vectors[:, 3],
    )


def solution(mesh):
    placed = (
        P("dp", "head", None),
        P("dp", None),
        P(),
        P(),
        P(),
        P(),
        P(),
        P(),
        P(),
        P(),
        P("dp", "head", None),
    )
    return jax.shard_map(
        local,
        mesh=mesh,
        in_specs=placed,
        out_specs=(
            P("dp", "head", None),
            P("dp", "head", None),
            P("dp", None),
            P("dp", None),
            P("dp"),
            P("dp"),
            P("dp", None),
            P("dp", None),
            P("dp"),
            P("dp"),
        ),
        check_vma=False,
    )
```

```python
import functools
import math

import jax
import jax.numpy as jnp
import numpy as np
from jax import lax
from jax.experimental import pallas as pl
from jax.experimental.pallas import tpu as pltpu
from jax.sharding import PartitionSpec as P

H = 12
DH = 64


EPSILON = 1e-12
NEG_FILL = -1e30
LOG2E = 1.4426950408889634
NN = (((1,), (0,)), ((), ()))
NT = (((1,), (1,)), ((), ()))
TN = (((0,), (0,)), ((), ()))
VMEM_BYTES = 63 * 2**20
ANY = pl.BlockSpec(memory_space=pl.ANY)
SMEM = pl.BlockSpec(memory_space=pltpu.SMEM)


def head_slopes(heads_total):
    closest = 2 ** int(math.floor(math.log2(heads_total)))

    def power_slopes(number):
        first_slope = 2.0 ** (-8.0 / number)
        return [first_slope ** (counter + 1) for counter in range(number)]

    listed = power_slopes(closest)
    listed = listed + power_slopes(2 * closest)[0::2][: heads_total - closest]
    return np.array(listed, dtype=np.float32)


def low(value):
    return value.astype(jnp.bfloat16)


def wide(value):
    return value.astype(jnp.float32)


def dot(left, right, dims=NN):
    return lax.dot_general(left, right, dims, preferred_element_type=jnp.float32)


def shaped(shape, dtype=jnp.bfloat16):
    return jax.ShapeDtypeStruct(shape, dtype)


def whole(shape):
    return pl.BlockSpec(shape, lambda *_: (0,) * len(shape))


def later(value, *arrays):
    if not arrays:
        return value
    token = lax.optimization_barrier((lax.create_token(), *arrays))[0]
    return lax.optimization_barrier((token, value))[1]


def call(kernel, name, grid, in_specs, out_specs, out_shape, scratch, operands, after, into=()):
    operands = (later(operands[0], *after),) + tuple(operands[1:])
    count = len(operands) - 1
    extra = len(into)

    def run(me, *refs):
        kernel(me, *refs[:count], *refs[count + extra :])

    return pl.pallas_call(
        run,
        grid_spec=pltpu.PrefetchScalarGridSpec(
            num_scalar_prefetch=1,
            grid=grid,
            in_specs=list(in_specs) + [ANY] * extra,
            out_specs=list(out_specs),
            scratch_shapes=scratch,
        ),
        out_shape=list(out_shape),
        input_output_aliases={count + 1 + number: number for number in range(len(into))},
        compiler_params=pltpu.CompilerParams(
            vmem_limit_bytes=VMEM_BYTES, dimension_semantics=("arbitrary",) * len(grid)
        ),
        cost_estimate=pl.CostEstimate(flops=10**12, bytes_accessed=0, transcendentals=0),
        name=name,
    )(*operands, *into)


def normalize(value):
    center = value - jnp.mean(value, axis=-1, keepdims=True)
    scale = lax.rsqrt(jnp.mean(center * center, axis=-1, keepdims=True) + EPSILON)
    return center * scale, scale


def norm_back(scale, normal, back):
    return scale * (
        back
        - jnp.mean(back, axis=-1, keepdims=True)
        - normal * jnp.mean(back * normal, axis=-1, keepdims=True)
    )


def attend_kernel(
    me,
    slopes,
    labels,
    first,
    second,
    third,
    fourth,
    query_weight,
    key_weight,
    value_weight,
    tokens_out,
    queries_out,
    keys_out,
    values_out,
    probs_out,
    attended_out,
    bias,
    *,
    row,
    heads,
):
    group = pl.program_id(0)
    _, length, width = tokens_out.shape
    quarter = length // 4

    @pl.when(group == 0)
    def _():
        for step, piece in enumerate((first, second, third, fourth)):
            place = pl.multiple_of((me[0] ^ step) * quarter, quarter)
            tokens_out[0, pl.ds(place, quarter), :] = piece[0]
        label = labels[pl.ds(me[0] * 2 + row, 1), :]
        column = jnp.broadcast_to(label, (128, length)).T[:, :1]
        rows = lax.broadcasted_iota(jnp.int32, (length, length), 0)
        columns = lax.broadcasted_iota(jnp.int32, (length, length), 1)
        gap = -wide(jnp.abs(rows - columns))
        bias[...] = jnp.where(column == label, gap, NEG_FILL)

    tokens = tokens_out[0]
    queries = low(dot(tokens, query_weight[...]))
    keys = low(dot(tokens, key_weight[...]))
    values = low(dot(tokens, value_weight[...]))
    queries_out[0] = queries
    keys_out[0] = keys
    values_out[0] = values
    owner = lax.broadcasted_iota(jnp.int32, keys.shape, 1) // DH
    turned = values.T
    raw = []
    for head in range(heads):
        own_keys = jnp.where(owner == head, keys, jnp.zeros_like(keys))
        raw.append(dot(own_keys, queries, NT))
    parts = []
    for head in range(heads):
        slope = slopes[group * heads + head] * LOG2E
        scores = raw[head] * (DH**-0.5 * LOG2E) + bias[...] * slope
        exponent = jnp.exp2(scores - jnp.max(scores, axis=0, keepdims=True))
        probs = low(exponent * (1.0 / jnp.sum(exponent, axis=0, keepdims=True)))
        probs_out[0, head] = probs
        parts.append(dot(turned[head * DH : (head + 1) * DH], probs))
    attended_out[0] = low(jnp.concatenate(parts, axis=0).T)


def attend(me, slopes, labels, tokens, pieces, joint_projection, row, into=(), heads=4):
    _, quarter, width = tokens.shape
    length = labels.shape[1]
    rows = tokens.shape[0] // 4
    groups = H // heads
    group_width = heads * DH
    weight = [
        pl.BlockSpec((width, group_width), lambda g, me, which=which: (0, which * groups + g))
        for which in range(3)
    ]
    out = pl.BlockSpec((1, length, group_width), lambda g, me: (row, 0, g))
    like = shaped((rows, length, width))
    return call(
        functools.partial(attend_kernel, row=row, heads=heads),
        "attend",
        (groups,),
        [
            SMEM,
            whole(labels.shape),
            pl.BlockSpec((1, quarter, width), lambda g, me: (me[0] * rows + row, 0, 0)),
        ]
        + [whole((1, quarter, width))] * 3
        + weight,
        [pl.BlockSpec((1, length, width), lambda g, me: (row, 0, 0)), out, out, out]
        + [pl.BlockSpec((1, heads, length, length), lambda g, me: (row, g, 0, 0)), out],
        [like, like, like, like, shaped((rows, H, length, length)), like],
        [pltpu.VMEM((length, length), jnp.float32)],
        (me, slopes, labels, tokens, *pieces) + (joint_projection,) * 3,
        (),
        into,
    )


def attend_back_kernel(
    me, queries_ref, keys_ref, values_ref, probs_ref, attended, back_attended, back_joint, *, heads
):
    queries, keys, values = queries_ref[0], keys_ref[0], values_ref[0]
    back = back_attended[0]
    owner = lax.broadcasted_iota(jnp.int32, keys.shape, 1) // DH
    zero = jnp.zeros_like(keys)
    product = (wide(attended[0]) * wide(back)).T
    turned = keys.T
    probs_all, scores_all, back_all, queries_all, parts = [], [], [], [], []
    back_probs = [dot(jnp.where(owner == head, values, zero), back, NT) for head in range(heads)]
    for head in range(heads):
        mine = owner == head
        lanes = slice(head * DH, (head + 1) * DH)
        inner = jnp.sum(product[lanes], axis=0, keepdims=True)
        probs = probs_ref[0, head]
        back_scores = low(wide(probs) * (back_probs[head] - inner))
        probs_all.append(probs)
        scores_all.append(back_scores)
        back_all.append(jnp.where(mine, back, zero))
        queries_all.append(jnp.where(mine, queries, zero))
        parts.append(dot(turned[lanes], back_scores))
    scale = DH**-0.5
    back_joint[2, 0] = low(dot(jnp.concatenate(probs_all, 1), jnp.concatenate(back_all, 0)))
    back_joint[1, 0] = low(
        dot(jnp.concatenate(scores_all, 1), jnp.concatenate(queries_all, 0)) * scale
    )
    back_joint[0, 0] = low(jnp.concatenate(parts, 0).T * scale)


def attend_back(
    me, queries, keys, values, probs, attended, back_attended, base, groups, after=(), heads=4
):
    rows, length, _ = queries.shape
    group_width = heads * DH
    spec = pl.BlockSpec((1, length, group_width), lambda r, g, me: (r, 0, base + g))
    return call(
        functools.partial(attend_back_kernel, heads=heads),
        "attend_back",
        (rows, groups),
        [spec] * 3
        + [
            pl.BlockSpec((1, heads, length, length), lambda r, g, me: (r, base + g, 0, 0)),
            spec,
            spec,
        ],
        [pl.BlockSpec((3, 1, length, group_width), lambda r, g, me: (0, r, 0, g))],
        [shaped((3, rows, length, groups * group_width))],
        [],
        (me, queries, keys, values, probs, attended, back_attended),
        after,
    )


def send_piece(me, place, value, outs):
    far = (place % 4) ^ me[0]
    for number, out in enumerate(outs):

        @pl.when(far == number)
        def _():
            out[place // 4] = value


def ahead_kernel(
    me,
    tokens,
    attended,
    output_projection,
    first_gain,
    first_offset,
    gate_weight,
    up_weight,
    reduce_weight,
    normal_out,
    scale_out,
    hidden_out,
    gate_out,
    slope_out,
    active_out,
    total,
    *,
    block,
):
    step = pl.program_id(0)
    count, width = tokens.shape
    blocks = [pl.ds(start, block) for start in range(0, count, block)]

    @pl.when(step == 0)
    def _():
        for rows in blocks:
            branch = dot(attended[rows, :], output_projection[...])
            normal, scale = normalize(wide(tokens[rows, :]) + branch)
            normal_out[rows, :] = normal
            scale_out[rows, :] = jnp.broadcast_to(scale, (block, scale_out.shape[1]))
            hidden = normal * first_gain[...][None] + first_offset[...][None]
            hidden_out[rows, :] = low(hidden)
            total[rows, :] = hidden

    blocks = [pl.ds(start, 2 * block) for start in range(0, count, 2 * block)]
    products = []
    for rows in blocks:
        hidden = hidden_out[rows, :]
        products.append((dot(hidden, gate_weight[...]), dot(hidden, up_weight[...])))
    for rows, (gate, up) in zip(blocks, products):
        share = 0.5 * (1.0 + lax.erf(gate * 0.5**0.5))
        density = jnp.exp(gate * gate * -0.5) * (2.0 * math.pi) ** -0.5
        unit = gate * share
        active = low(unit * up)
        gate_out[rows, :] = low(unit)
        slope_out[rows, :] = low(up * (share + gate * density))
        active_out[rows, :] = active
        total[rows, :] += dot(active, reduce_weight[...])


def ahead(
    me,
    tokens,
    attended,
    output_projection,
    first_gain,
    first_offset,
    expand_weight,
    reduce_weight,
    after=(),
    chunk=512,
    block=256,
):
    count, width = tokens.shape
    inner = reduce_weight.shape[0]
    steps = inner // chunk
    vector = whole((width,))
    rows = whole((count, width))
    column = pl.BlockSpec((count, chunk), lambda s, me: (0, s))
    return call(
        functools.partial(ahead_kernel, block=block),
        "ahead",
        (steps,),
        [
            rows,
            rows,
            whole((width, width)),
            vector,
            vector,
            pl.BlockSpec((width, chunk), lambda s, me: (0, s)),
            pl.BlockSpec((width, chunk), lambda s, me: (0, s + steps)),
            pl.BlockSpec((chunk, width), lambda s, me: (s, 0)),
        ],
        [rows, whole((count, 128)), rows, column, column, column, rows],
        [
            shaped((count, width), jnp.float32),
            shaped((count, 128), jnp.float32),
            shaped((count, width)),
            shaped((count, inner)),
            shaped((count, inner)),
            shaped((count, inner)),
            shaped((count, width), jnp.float32),
        ],
        [],
        (
            me,
            tokens,
            attended,
            output_projection,
            first_gain,
            first_offset,
            expand_weight,
            expand_weight,
            reduce_weight,
        ),
        after,
    )


def reduce_kernel(
    me,
    total,
    second_gain,
    second_offset,
    first,
    second,
    third,
    fourth,
    active,
    output_own,
    output_core,
    output_across,
    output_beyond,
    two_out,
    mixed_out,
    gain_out,
    offset_out,
    sent,
    kept,
    cotangent,
    turned,
):
    half = turned.shape[0] // 2
    outputs = (output_own, output_core, output_across, output_beyond)

    @pl.when(pl.program_id(0) == 0)
    def _():
        count, width = total.shape
        quarter = first.shape[1]
        for number, piece in enumerate((first, second, third, fourth)):
            for row in range(piece.shape[0]):
                place = (row * 4 + (me[0] ^ number)) * quarter
                cotangent[pl.ds(pl.multiple_of(place, quarter), quarter), :] = piece[row]
        gain = jnp.zeros((1, width), jnp.float32)
        offset = gain
        for start in range(0, count, quarter):
            rows = pl.ds(start, quarter)
            normal, scale = normalize(total[rows, :])
            send_piece(
                me,
                start // quarter,
                low(normal * second_gain[...][None] + second_offset[...][None]),
                outputs,
            )
            back = wide(cotangent[rows, :])
            gain += jnp.sum(back * normal, axis=0, keepdims=True)
            offset += jnp.sum(back, axis=0, keepdims=True)
            two = norm_back(scale, normal, back * second_gain[...][None])
            two_out[rows, :] = two
            mixed_out[rows, :] = low(two)
        gain_out[...] = gain
        offset_out[...] = offset
        turned[...] = mixed_out[...].T

    core = me[0] & 1
    for out, place in ((sent, 1 - core), (kept, core)):
        left = turned[pl.ds(pl.multiple_of(place * half, half), half), :]
        part = low(dot(left, active[...]))
        columns = out.shape[2]
        for number in range(out.shape[0]):
            out[number] = part[:, number * columns : (number + 1) * columns]


def reduce_gradient(
    me,
    total,
    second_gain,
    second_offset,
    cotangent,
    pieces,
    active,
    after=(),
    blocks=8,
    together=2,
):
    count, width = total.shape
    columns = active.shape[1] // blocks
    piece = pieces[0].shape
    rows = whole((count, width))
    vector = whole((1, width))
    out = pl.BlockSpec((together, width // 2, columns), lambda s, me: (s, 0, 0))
    like = shaped((blocks, width // 2, columns))
    return call(
        reduce_kernel,
        "reduce_gradient",
        (blocks // together,),
        [
            rows,
            whole((width,)),
            whole((width,)),
            pl.BlockSpec(piece, lambda s, me: (me[0], 0, 0)),
        ]
        + [whole(piece)] * 3
        + [pl.BlockSpec((count, columns * together), lambda s, me: (0, s))],
        [whole(piece)] * 4 + [rows, rows, vector, vector, out, out],
        [shaped(piece)] * 4
        + [
            shaped((count, width), jnp.float32),
            shaped((count, width)),
            shaped((1, width), jnp.float32),
            shaped((1, width), jnp.float32),
            like,
            like,
        ],
        [pltpu.VMEM((count, width), jnp.bfloat16), pltpu.VMEM((width, count), jnp.bfloat16)],
        (me, total, second_gain, second_offset, cotangent, *pieces, active),
        after,
    )


def expand_kernel(
    me,
    mixed,
    hidden,
    gate_part,
    slope_part,
    reduce_weight,
    gate_weight,
    up_weight,
    start,
    sent,
    kept,
    back,
    turned,
):
    @pl.when(pl.program_id(0) == 0)
    def _():
        turned[...] = hidden[...].T
        back[...] = start[...]

    weight = jnp.concatenate([gate_weight[...], up_weight[...]], 1)
    back_active = dot(mixed[...], reduce_weight[...], NT)
    both = jnp.concatenate(
        [low(back_active * wide(slope_part[...])), low(back_active * wide(gate_part[...]))], 1
    )
    back[...] += dot(both, weight, NT)
    gradient = low(dot(turned[...], both))
    chunk = gradient.shape[1] // 2
    first = me[0] & 1 == 0
    sent[...] = jnp.where(first, gradient[:, chunk:], gradient[:, :chunk]).reshape(sent.shape)
    kept[...] = jnp.where(first, gradient[:, :chunk], gradient[:, chunk:]).reshape(kept.shape)


def expand_gradient(
    me,
    mixed,
    hidden,
    gate_part,
    slope_part,
    reduce_weight,
    expand_weight,
    start,
    part,
    lead,
    parts=2,
    after=(),
    chunk=768,
):
    count, width = mixed.shape
    inner = reduce_weight.shape[0]
    steps = inner // parts // chunk
    base = part * steps
    all_steps = inner // chunk
    rows = whole((count, width))
    column = pl.BlockSpec((count, chunk), lambda s, me: (0, base + s))
    if lead:
        out = pl.BlockSpec((1, width, chunk), lambda s, me: (s, 0, 0))
        like = shaped((steps, width, chunk))
    else:
        out = pl.BlockSpec((width, chunk), lambda s, me: (0, s))
        like = shaped((width, steps * chunk))
    return call(
        expand_kernel,
        "expand_gradient",
        (steps,),
        [
            rows,
            rows,
            column,
            column,
            pl.BlockSpec((chunk, width), lambda s, me: (base + s, 0)),
            pl.BlockSpec((width, chunk), lambda s, me: (0, base + s)),
            pl.BlockSpec((width, chunk), lambda s, me: (0, all_steps + base + s)),
            rows,
        ],
        [out, out, rows],
        [like, like, shaped((count, width), jnp.float32)],
        [pltpu.VMEM((width, count), jnp.bfloat16)],
        (
            me,
            mixed,
            hidden,
            gate_part,
            slope_part,
            reduce_weight,
            expand_weight,
            expand_weight,
            start,
        ),
        after,
    )


def branch_kernel(
    me,
    back_hidden,
    normal,
    scale,
    first_gain,
    output_projection,
    one_out,
    back_attended,
    branch,
    gain_out,
    offset_out,
):
    back = back_hidden[...]
    gain = jnp.sum(back * normal[...], axis=0, keepdims=True)
    offset = jnp.sum(back, axis=0, keepdims=True)
    one = norm_back(scale[:, :1], normal[...], back * first_gain[...][None])
    one_out[...] = one
    branch[...] = low(one)
    back_attended[...] = low(dot(low(one), output_projection[...], NT))

    @pl.when(pl.program_id(0) == 0)
    def _():
        gain_out[...] = gain
        offset_out[...] = offset

    @pl.when(pl.program_id(0) > 0)
    def _():
        gain_out[...] += gain
        offset_out[...] += offset


def branch_back(me, back_hidden, normal, scale, first_gain, output_projection, after=(), block=256):
    count, width = back_hidden.shape
    rows = pl.BlockSpec((block, width), lambda s, me: (s, 0))
    vector = whole((1, width))
    return call(
        branch_kernel,
        "branch_back",
        (count // block,),
        [
            rows,
            rows,
            pl.BlockSpec((block, 128), lambda s, me: (s, 0)),
            whole((width,)),
            whole((width, width)),
        ],
        [rows, rows, rows, vector, vector],
        [
            shaped((count, width), jnp.float32),
            shaped((count, width)),
            shaped((count, width)),
            shaped((1, width), jnp.float32),
            shaped((1, width), jnp.float32),
        ],
        [],
        (me, back_hidden, normal, scale, first_gain, output_projection),
        after,
    )


def halves(gradients, me, outs):
    front, back = [], []
    for gradient in gradients:
        half = gradient.shape[1] // 2
        front.append(gradient[:, :half])
        back.append(gradient[:, half:])
    front, back = jnp.concatenate(front, axis=1), jnp.concatenate(back, axis=1)
    first = me[0] & 1 == 0
    outs[0][:, : front.shape[1]] = jnp.where(first, back, front)
    outs[1][:, : front.shape[1]] = jnp.where(first, front, back)


def joint_kernel(me, tokens, back_joint, sent, kept):
    turned = tokens[...].T
    halves([low(dot(turned, back_joint[which])) for which in range(3)], me, (sent, kept))


def joint_gradient(me, tokens, back_joint, after=()):
    count, width = tokens.shape
    out = (width, 3 * back_joint.shape[2] // 2)
    return call(
        joint_kernel,
        "joint_gradient",
        (1,),
        [whole((count, width)), whole(back_joint.shape)],
        [whole(out)] * 2,
        [shaped(out)] * 2,
        [],
        (me, tokens, back_joint),
        after,
    )


def joint_end_kernel(
    me, tokens, attended, back_joint, branch, first, second, third, fourth, sent, kept
):
    turned = tokens[...].T
    gradients = [low(dot(turned, back_joint[which])) for which in range(3)]
    gradients.append(low(dot(attended[...].T, branch[...])))
    halves(gradients, me, (sent, kept))
    rows = jnp.concatenate(
        [first[...], second[...], third[...], fourth[...]]
        + [jnp.zeros((124, first.shape[1]), jnp.float32)]
    )
    columns = low(rows.T)
    sent[:, sent.shape[1] - 128 :] = columns
    kept[:, kept.shape[1] - 128 :] = columns


def joint_gradient_end(me, tokens, attended, back_joint, branch, vectors, after=()):
    count, width = tokens.shape
    out = (width, 3 * back_joint.shape[2] // 2 + width // 2 + 128)
    rows = whole((count, width))
    return call(
        joint_end_kernel,
        "joint_gradient_end",
        (1,),
        [rows, rows, whole(back_joint.shape), rows] + [whole((1, width))] * 4,
        [whole(out)] * 2,
        [shaped(out)] * 2,
        [],
        (me, tokens, attended, back_joint, branch, *vectors),
        after,
    )


def tokens_kernel(me, front, back, weight, one, own, core, across, total):
    step = pl.program_id(0)
    part = dot(jnp.concatenate([front[0], back[0]], axis=1), weight[...], NT)

    @pl.when(step == 0)
    def _():
        total[...] = one[...] + part

    @pl.when(step == 1)
    def _():
        total[...] += part

    @pl.when(step == 2)
    def _():
        value = low(total[...] + part)
        quarter = own.shape[1]
        for place in range(value.shape[0] // quarter):
            rows = slice(place * quarter, (place + 1) * quarter)
            send_piece(me, place, value[rows], (own, core, across.at[0], across.at[1]))


def tokens_gradient_of(me, front, back, joint_projection, one, piece, after=()):
    count, width = one.shape
    rows = whole((count, width))
    return call(
        tokens_kernel,
        "tokens_gradient",
        (3,),
        [pl.BlockSpec((1, count, part.shape[2]), lambda s, me: (s, 0, 0)) for part in (front, back)]
        + [
            pl.BlockSpec((width, width), lambda s, me: (0, s)),
            rows,
        ],
        [whole(piece)] * 2 + [whole((2,) + piece)],
        [shaped(piece)] * 2 + [shaped((2,) + piece)],
        [pltpu.VMEM((count, width), jnp.float32)],
        (me, front, back, joint_projection, one),
        after,
    )


def turn_kernel(me, own, other, out):
    half = own.shape[0]
    mine, others = wide(own[...]).T, wide(other[...]).T
    first = me[0] & 1 == 0
    out[:, :half] = jnp.where(first, mine, others)
    out[:, half:] = jnp.where(first, others, mine)


def turn(me, own, other):
    half, count = own.shape
    return call(
        turn_kernel,
        "turn",
        (1,),
        [whole((half, count))] * 2,
        [whole((count, 2 * half))],
        [shaped((count, 2 * half), jnp.float32)],
        [],
        (me, own, other),
        (),
    )[0]


def exchange(value, axis, bit):
    sizes = (lax.axis_size("dp"), lax.axis_size("head"))
    pairs = []
    for dp in range(sizes[0]):
        for head in range(sizes[1]):
            target = (dp ^ bit, head) if axis == "dp" else (dp, head ^ bit)
            pairs.append((dp * sizes[1] + head, target[0] * sizes[1] + target[1]))
    return lax.ppermute(value, ("dp", "head"), pairs)


def pick(pieces, place):
    value = pieces[0]
    for number in range(1, len(pieces)):
        value = jnp.where(place == number, pieces[number], value)
    return value


def quarters_to_owners(values, row=None):
    groups = lax.axis_size("head")
    me = lax.axis_index("head")
    own = values.shape[0] // groups
    pieces = []
    for step in range(1, groups):
        start, size = (me ^ step) * own, own
        if row is not None:
            start, size = start + row, 1
        pieces.append(lax.dynamic_slice_in_dim(values, start, size, axis=0))
    return pieces, lambda *after: [
        exchange(later(pieces[step - 1], *after), "head", step) for step in range(1, groups)
    ]


class Pieces:
    def __init__(self, own, core, across):
        self.own = own
        self.core = core
        self.across = exchange(across, "head", 2)

    def pass_on(self, *after):
        across = later(self.across, *after)
        self.across = across[0]
        self.passed = exchange(across[1], "head", 1)
        self.core = exchange(later(self.core, *after), "head", 1)
        return [across]

    def finish(self, *after):
        pieces = [self.own, self.core, self.across, self.passed]
        pieces = [later(piece, *after) for piece in pieces]
        me = lax.axis_index("head")
        return jnp.concatenate([pick(pieces, me ^ place) for place in range(4)], axis=0)


class DirectPieces(Pieces):
    def __init__(self, own, core, across, beyond):
        self.own = own
        self.core = exchange(core, "head", 1)
        self.across = exchange(across, "head", 2)
        self.passed = exchange(beyond, "head", 3)

    def come(self):
        return [self.core, self.across, self.passed]


class Sum:
    def __init__(self, sent, kept):
        self.bits = lax.axis_size("dp").bit_length() - 1
        self.lead = kept.ndim - 3
        self.tail = kept.shape[-2:]
        self.front = kept.shape[: self.lead]
        self.chosen = {}
        self.terms = [(self.split(kept), ())]
        self.coming = self.split(exchange(sent, "head", 1))

    def split(self, value):
        return value.reshape(self.front + (2,) * self.bits + self.tail)

    def total(self, wanted, after=()):
        value = None
        for term, cut in self.terms:
            term = later(term, *after)
            starts = [0] * term.ndim
            sizes = list(term.shape)
            for axis, place in wanted.items():
                if axis not in cut:
                    starts[axis], sizes[axis] = place, 1
            piece = wide(lax.dynamic_slice(term, starts, sizes))
            value = piece if value is None else value + piece
        return value

    def arrive(self):
        if self.coming is not None:
            self.terms.append((self.coming, tuple(self.chosen)))
            self.coming = None

    def halve(self, step, *after):
        self.arrive()
        if step == "y":
            axis, mine = 0, lax.axis_index("head") >> 1
        else:
            axis, mine = self.lead + self.bits - 1 - step, (lax.axis_index("dp") >> step) & 1
        away = dict(self.chosen)
        away[axis] = 1 - mine
        sent = low(self.total(away, after))
        self.chosen[axis] = mine
        self.coming = exchange(sent, *(("head", 2) if step == "y" else ("dp", 1 << step)))
        return sent

    def rest(self, steps, *after):
        for step in steps:
            self.halve(step, *after)
        return self.own(*after)

    def own(self, *after):
        self.arrive()
        value = low(self.total(self.chosen, after))
        return value.reshape(value.shape[: self.lead] + self.tail)


def sum_y(own, *after):
    other = exchange(own, "head", 2)
    return low(wide(later(own, *after)) + wide(other))


def join(own, bit, axis, *after):
    own = later(own, *after)
    return join_parts(own, exchange(own, "head", bit), bit, axis)


def join_parts(own, other, bit, axis):
    first = lax.axis_index("head") & bit == 0
    return jnp.concatenate(
        (jnp.where(first, own, other), jnp.where(first, other, own)), axis=axis
    )


def local(
    tokens,
    segment_labels,
    joint_projection,
    output_projection,
    first_gain,
    first_offset,
    expand_weight,
    reduce_weight,
    second_gain,
    second_offset,
    cotangent,
):
    width = tokens.shape[2]
    length = segment_labels.shape[1]
    dp_size = lax.axis_size("dp")
    bits = dp_size.bit_length() - 1
    own_width = width // dp_size
    inner = reduce_weight.shape[0]
    me = lax.axis_index("head")
    group = jnp.reshape(me, (1,))
    up_order = list(range(bits))
    slopes = jnp.asarray(head_slopes(H), dtype=jnp.float32)
    row_count = tokens.shape[0] // lax.axis_size("head")
    flat = lambda value: value.reshape(row_count * length, width)
    rowed = lambda value: value.reshape(row_count, length, width)
    piece = (row_count,) + tokens.shape[1:]

    pieces = [quarters_to_owners(tokens, row)[1]() for row in range(row_count)]
    early, exchange_cotangent = quarters_to_owners(cotangent)
    front = ()
    for row in range(row_count):
        front = attend(
            later(group, *early),
            slopes,
            segment_labels,
            tokens,
            pieces[row],
            joint_projection,
            row,
            front,
        )
    own_tokens, queries, keys, values, probs, attended = front
    cotangent_pieces = exchange_cotangent(attended)
    normal, scale, hidden, gate_part, slope_part, active, total = ahead(
        group,
        flat(own_tokens),
        flat(attended),
        output_projection,
        first_gain,
        first_offset,
        expand_weight,
        reduce_weight,
    )
    blocks = 8
    *output, back_two, back_mixed, second_gain_back, second_offset_back, sent, kept = (
        reduce_gradient(
            group, total, second_gain, second_offset, cotangent, cotangent_pieces, active
        )
    )
    output = DirectPieces(*output)
    by_device = lambda value: (
        value.reshape(blocks, width // 2, dp_size // blocks, inner // dp_size)
        .transpose(0, 2, 1, 3)
        .reshape(dp_size, width // 2, inner // dp_size)
    )
    reduce_sum = Sum(by_device(sent), by_device(kept))
    across = [1, 0] + up_order[2:]
    rest = (group, back_mixed, hidden, gate_part, slope_part, reduce_weight, expand_weight)
    cut = lambda value: value.reshape(value.shape[0], dp_size, own_width, value.shape[2])
    slab = lambda value: value.reshape(dp_size, own_width, value.shape[1])
    sent, kept, back_hidden = expand_gradient(*rest, back_two, 0, True, after=[kept])
    expand_first = Sum(cut(sent), cut(kept))
    moved = [reduce_sum.halve(0, back_hidden)]
    moved += output.come()
    sent, kept, back_hidden = expand_gradient(*rest, back_hidden, 1, False, after=moved)
    expand_second = Sum(slab(sent), slab(kept))
    moved = [expand_first.halve("y", back_hidden)]
    moved = [reduce_sum.halve(1, *moved)]
    back_one, back_attended, branch, first_gain_back, first_offset_back = branch_back(
        group, back_hidden, normal, scale, first_gain, output_projection, after=moved
    )
    moved = [expand_second.halve(1, back_one)]
    heads = (group, queries, keys, values, probs, attended, rowed(back_attended))
    columns = lambda value: value.reshape(3, row_count * length, value.shape[3])
    front = columns(attend_back(*heads, 0, 2, after=moved)[0])
    moved = [expand_first.halve(0, front)]
    moved = [reduce_sum.halve(2, *moved)]
    vectors = (first_gain_back, first_offset_back, second_gain_back, second_offset_back)
    sent, kept = joint_gradient(group, flat(own_tokens), front, after=moved)
    joint_first = Sum(slab(sent), slab(kept))
    moved = [expand_second.halve(0, kept)]
    moved = [expand_first.halve(1, *moved)]
    back = columns(attend_back(*heads, 2, 1, after=moved)[0])
    moved = [joint_first.halve(1, back)]
    sent, kept = joint_gradient_end(
        group, flat(own_tokens), flat(attended), back, branch, vectors, after=moved
    )
    joint_last = Sum(slab(sent), slab(kept))
    moved = [joint_first.halve(0, kept)]
    gradient = tokens_gradient_of(
        group, front, back, joint_projection, back_one, piece, after=moved
    )

    moved = [joint_last.halve(0, gradient[0])]
    gradient = Pieces(*gradient)
    moved = [expand_first.halve(2, *moved)]
    moved = [expand_second.halve(2, *moved)]
    reduce_own = reduce_sum.rest(up_order[3:], *moved)
    output = output.finish(reduce_own)
    reduce_other = exchange(reduce_own, "head", 2)
    moved = [joint_last.halve(1, output)]
    first_own = expand_first.rest(up_order[3:], *moved)
    first_other = exchange(first_own, "head", 2)
    moved = [joint_first.halve(2, first_own)]
    reduce_own = low(wide(later(reduce_own, *moved)) + wide(reduce_other))
    reduce_other = exchange(reduce_own, "head", 1)
    moved = gradient.pass_on(reduce_own)
    second_own = expand_second.rest(up_order[3:], *moved)
    second_other = exchange(second_own, "head", 2)
    moved = [joint_last.halve(2, second_own)]
    first_grad = join(join_parts(later(first_own, *moved), first_other, 2, 0)[None], 1, 0)
    reduce_grad = turn(later(group, *moved), reduce_own, reduce_other)
    joint_own = [joint_first.rest(up_order[3:], first_grad)]
    joint_own = [sum_y(joint_own[0])]
    gradient = gradient.finish(reduce_grad)
    second_own = low(wide(later(second_own, gradient)) + wide(second_other))
    second_grad = join(second_own[None], 1, 0)
    joint_own += [sum_y(joint_last.rest(up_order[3:], second_own))]
    expand_grad = jnp.concatenate(
        [
            piece
            for side in range(2)
            for piece in (
                first_grad[side, 0],
                first_grad[side, 1],
                second_grad[side],
            )
        ],
        axis=-1,
    )
    vectors = wide(joint_own[1][:, -128:-124])
    both = join(jnp.concatenate((joint_own[0], joint_own[1][:, :-128]), axis=1)[None], 1, 0)
    size = front.shape[2] // 2
    last = back.shape[2] // 2
    joint_grad = []
    for which in range(3):
        for begin, count in ((which * size, size), (3 * size + which * last, last)):
            joint_grad += [both[side, :, begin : begin + count] for side in range(2)]
    projection_grad = [both[side, :, 3 * (size + last) :] for side in range(2)]
    return (
        output,
        gradient,
        wide(jnp.concatenate(joint_grad, axis=-1)),
        wide(jnp.concatenate(projection_grad, axis=-1)),
        vectors[:, 0],
        vectors[:, 1],
        wide(expand_grad),
        reduce_grad,
        vectors[:, 2],
        vectors[:, 3],
    )


def solution(mesh):
    placed = (
        P("dp", "head", None),
        P("dp", None),
        P(),
        P(),
        P(),
        P(),
        P(),
        P(),
        P(),
        P(),
        P("dp", "head", None),
    )
    return jax.shard_map(
        local,
        mesh=mesh,
        in_specs=placed,
        out_specs=(
            P("dp", "head", None),
            P("dp", "head", None),
            P("dp", None),
            P("dp", None),
            P("dp"),
            P("dp"),
            P("dp", None),
            P("dp", None),
            P("dp"),
            P("dp"),
        ),
        check_vma=False,
    )
```

```python
import functools
import math

import jax
import jax.numpy as jnp
import numpy as np
from jax import lax
from jax.experimental import pallas as pl
from jax.experimental.pallas import tpu as pltpu
from jax.sharding import PartitionSpec as P

H = 12
DH = 64


EPSILON = 1e-12
NEG_FILL = -1e30
LOG2E = 1.4426950408889634
NN = (((1,), (0,)), ((), ()))
NT = (((1,), (1,)), ((), ()))
TN = (((0,), (0,)), ((), ()))
VMEM_BYTES = 48 * 2**20
ANY = pl.BlockSpec(memory_space=pl.ANY)
SMEM = pl.BlockSpec(memory_space=pltpu.SMEM)


def head_slopes(heads_total):
    closest = 2 ** int(math.floor(math.log2(heads_total)))

    def power_slopes(number):
        first_slope = 2.0 ** (-8.0 / number)
        return [first_slope ** (counter + 1) for counter in range(number)]

    listed = power_slopes(closest)
    listed = listed + power_slopes(2 * closest)[0::2][: heads_total - closest]
    return np.array(listed, dtype=np.float32)


def low(value):
    return value.astype(jnp.bfloat16)


def wide(value):
    return value.astype(jnp.float32)


def dot(left, right, dims=NN):
    return lax.dot_general(left, right, dims, preferred_element_type=jnp.float32)


def shaped(shape, dtype=jnp.bfloat16):
    return jax.ShapeDtypeStruct(shape, dtype)


def whole(shape):
    return pl.BlockSpec(shape, lambda *_: (0,) * len(shape))


def later(value, *arrays):
    if not arrays:
        return value
    token = lax.optimization_barrier((lax.create_token(), *arrays))[0]
    return lax.optimization_barrier((token, value))[1]


def once(spec, operand):
    if spec.block_shape is not None and tuple(spec.block_shape) == operand.shape:
        return pl.BlockSpec(spec.block_shape, spec.index_map, pipeline_mode=pl.Buffered(1))
    return spec


def call(kernel, name, grid, in_specs, out_specs, out_shape, scratch, operands, after, into=()):
    operands = (later(operands[0], *after),) + tuple(operands[1:])
    count = len(operands) - 1
    extra = len(into)

    def run(me, *refs):
        kernel(me, *refs[:count], *refs[count + extra :])

    return pl.pallas_call(
        run,
        grid_spec=pltpu.PrefetchScalarGridSpec(
            num_scalar_prefetch=1,
            grid=grid,
            in_specs=[once(spec, operand) for spec, operand in zip(in_specs, operands[1:])]
            + [ANY] * extra,
            out_specs=list(out_specs),
            scratch_shapes=scratch,
        ),
        out_shape=list(out_shape),
        input_output_aliases={count + 1 + number: number for number in range(len(into))},
        compiler_params=pltpu.CompilerParams(
            vmem_limit_bytes=VMEM_BYTES, dimension_semantics=("arbitrary",) * len(grid)
        ),
        cost_estimate=pl.CostEstimate(flops=10**12, bytes_accessed=0, transcendentals=0),
        name=name,
    )(*operands, *into)


def near_bit(dp_size):
    return 0 if dp_size <= 8 else dp_size.bit_length() - 3


def arranged(blocks, swapped, low_bit=0):
    near, far = 1 << low_bit, 2 << low_bit
    result = []
    for number, block in enumerate(blocks):
        if bool(number & near) != bool(number & far):
            block = jnp.where(swapped, blocks[number ^ near ^ far], block)
        result.append(block)
    return result


def arranged_rows(value, swapped, dp_size):
    count = dp_size >> near_bit(dp_size)
    rows = value.shape[0] // count
    blocks = [value[number * rows : (number + 1) * rows] for number in range(count)]
    return jnp.concatenate(arranged(blocks, swapped), axis=0)


def normalize(value):
    center = value - jnp.mean(value, axis=-1, keepdims=True)
    scale = lax.rsqrt(jnp.mean(center * center, axis=-1, keepdims=True) + EPSILON)
    return center * scale, scale


def norm_back(scale, normal, back):
    return scale * (
        back
        - jnp.mean(back, axis=-1, keepdims=True)
        - normal * jnp.mean(back * normal, axis=-1, keepdims=True)
    )


def attend_kernel(
    me,
    slopes,
    labels,
    first,
    second,
    third,
    fourth,
    query_weight,
    key_weight,
    value_weight,
    tokens_out,
    queries_out,
    keys_out,
    values_out,
    probs_out,
    attended_out,
    bias,
    *,
    row,
    heads,
):
    group = pl.program_id(0)
    _, length, width = tokens_out.shape
    quarter = length // 4

    @pl.when(group == 0)
    def _():
        for step, piece in enumerate((first, second, third, fourth)):
            place = pl.multiple_of((me[0] ^ step) * quarter, quarter)
            tokens_out[0, pl.ds(place, quarter), :] = piece[0]
        label = labels[pl.ds(me[0] * 2 + row, 1), :]
        column = jnp.broadcast_to(label, (128, length)).T[:, :1]
        rows = lax.broadcasted_iota(jnp.int32, (length, length), 0)
        columns = lax.broadcasted_iota(jnp.int32, (length, length), 1)
        gap = -wide(jnp.abs(rows - columns))
        bias[...] = jnp.where(column == label, gap, NEG_FILL)

    tokens = tokens_out[0]
    queries = low(dot(tokens, query_weight[...]))
    keys = low(dot(tokens, key_weight[...]))
    values = low(dot(tokens, value_weight[...]))
    queries_out[0] = queries
    keys_out[0] = keys
    values_out[0] = values
    owner = lax.broadcasted_iota(jnp.int32, keys.shape, 1) // DH
    turned = values.T
    raw = []
    for head in range(heads):
        own_keys = jnp.where(owner == head, keys, jnp.zeros_like(keys))
        raw.append(dot(own_keys, queries, NT))
    parts = []
    for head in range(heads):
        slope = slopes[group * heads + head] * LOG2E
        scores = raw[head] * (DH**-0.5 * LOG2E) + bias[...] * slope
        exponent = jnp.exp2(scores - jnp.max(scores, axis=0, keepdims=True))
        probs = low(exponent * (1.0 / jnp.sum(exponent, axis=0, keepdims=True)))
        probs_out[0, head] = probs
        parts.append(dot(turned[head * DH : (head + 1) * DH], probs))
    attended_out[0] = low(jnp.concatenate(parts, axis=0).T)


def attend(me, slopes, labels, tokens, pieces, joint_projection, row, into=(), heads=4):
    _, quarter, width = tokens.shape
    length = labels.shape[1]
    rows = tokens.shape[0] // 4
    groups = H // heads
    group_width = heads * DH
    weight = [
        pl.BlockSpec((width, group_width), lambda g, me, which=which: (0, which * groups + g))
        for which in range(3)
    ]
    out = pl.BlockSpec((1, length, group_width), lambda g, me: (row, 0, g))
    like = shaped((rows, length, width))
    return call(
        functools.partial(attend_kernel, row=row, heads=heads),
        "attend",
        (groups,),
        [
            SMEM,
            whole(labels.shape),
            pl.BlockSpec((1, quarter, width), lambda g, me: (me[0] * rows + row, 0, 0)),
        ]
        + [whole((1, quarter, width))] * 3
        + weight,
        [pl.BlockSpec((1, length, width), lambda g, me: (row, 0, 0)), out, out, out]
        + [pl.BlockSpec((1, heads, length, length), lambda g, me: (row, g, 0, 0)), out],
        [like, like, like, like, shaped((rows, H, length, length)), like],
        [pltpu.VMEM((length, length), jnp.float32)],
        (me, slopes, labels, tokens, *pieces) + (joint_projection,) * 3,
        (),
        into,
    )


def attend_back_kernel(
    me, queries_ref, keys_ref, values_ref, probs_ref, attended, back_attended, back_joint, *, heads
):
    queries, keys, values = queries_ref[0], keys_ref[0], values_ref[0]
    back = back_attended[0]
    owner = lax.broadcasted_iota(jnp.int32, keys.shape, 1) // DH
    zero = jnp.zeros_like(keys)
    product = (wide(attended[0]) * wide(back)).T
    turned = keys.T
    probs_all, scores_all, back_all, queries_all, parts = [], [], [], [], []
    back_probs = [dot(jnp.where(owner == head, values, zero), back, NT) for head in range(heads)]
    for head in range(heads):
        mine = owner == head
        lanes = slice(head * DH, (head + 1) * DH)
        inner = jnp.sum(product[lanes], axis=0, keepdims=True)
        probs = probs_ref[0, head]
        back_scores = low(wide(probs) * (back_probs[head] - inner))
        probs_all.append(probs)
        scores_all.append(back_scores)
        back_all.append(jnp.where(mine, back, zero))
        queries_all.append(jnp.where(mine, queries, zero))
        parts.append(dot(turned[lanes], back_scores))
    scale = DH**-0.5
    back_joint[2, 0] = low(dot(jnp.concatenate(probs_all, 1), jnp.concatenate(back_all, 0)))
    back_joint[1, 0] = low(
        dot(jnp.concatenate(scores_all, 1), jnp.concatenate(queries_all, 0)) * scale
    )
    back_joint[0, 0] = low(jnp.concatenate(parts, 0).T * scale)


def attend_back(
    me, queries, keys, values, probs, attended, back_attended, base, groups, after=(), heads=4
):
    rows, length, _ = queries.shape
    group_width = heads * DH
    spec = pl.BlockSpec((1, length, group_width), lambda r, g, me: (r, 0, base + g))
    return call(
        functools.partial(attend_back_kernel, heads=heads),
        "attend_back",
        (rows, groups),
        [spec] * 3
        + [
            pl.BlockSpec((1, heads, length, length), lambda r, g, me: (r, base + g, 0, 0)),
            spec,
            spec,
        ],
        [pl.BlockSpec((3, 1, length, group_width), lambda r, g, me: (0, r, 0, g))],
        [shaped((3, rows, length, groups * group_width))],
        [],
        (me, queries, keys, values, probs, attended, back_attended),
        after,
    )


def send_piece(me, place, value, outs):
    far = (place % 4) ^ me[0]
    for number, out in enumerate(outs):

        @pl.when(far == number)
        def _():
            out[place // 4] = value


def ahead_kernel(
    me,
    tokens,
    attended,
    output_projection,
    first_gain,
    first_offset,
    gate_weight,
    up_weight,
    reduce_weight,
    normal_out,
    scale_out,
    hidden_out,
    gate_out,
    slope_out,
    active_out,
    total,
    *,
    block,
):
    step = pl.program_id(0)
    count, width = tokens.shape
    blocks = [pl.ds(start, block) for start in range(0, count, block)]

    @pl.when(step == 0)
    def _():
        for rows in blocks:
            branch = dot(attended[rows, :], output_projection[...])
            normal, scale = normalize(wide(tokens[rows, :]) + branch)
            normal_out[rows, :] = normal
            scale_out[rows, :] = jnp.broadcast_to(scale, (block, scale_out.shape[1]))
            hidden = normal * first_gain[...][None] + first_offset[...][None]
            hidden_out[rows, :] = low(hidden)
            total[rows, :] = hidden

    blocks = [pl.ds(start, 2 * block) for start in range(0, count, 2 * block)]
    products = []
    for rows in blocks:
        hidden = hidden_out[rows, :]
        products.append((dot(hidden, gate_weight[...]), dot(hidden, up_weight[...])))
    for rows, (gate, up) in zip(blocks, products):
        share = 0.5 * (1.0 + lax.erf(gate * 0.5**0.5))
        density = jnp.exp(gate * gate * -0.5) * (2.0 * math.pi) ** -0.5
        unit = gate * share
        active = low(unit * up)
        gate_out[rows, :] = low(unit)
        slope_out[rows, :] = low(up * (share + gate * density))
        active_out[rows, :] = active
        total[rows, :] += dot(active, reduce_weight[...])


def ahead(
    me,
    tokens,
    attended,
    output_projection,
    first_gain,
    first_offset,
    expand_weight,
    reduce_weight,
    after=(),
    chunk=512,
    block=256,
):
    count, width = tokens.shape
    inner = reduce_weight.shape[0]
    steps = inner // chunk
    vector = whole((width,))
    rows = whole((count, width))
    column = pl.BlockSpec((count, chunk), lambda s, me: (0, s))
    return call(
        functools.partial(ahead_kernel, block=block),
        "ahead",
        (steps,),
        [
            rows,
            rows,
            whole((width, width)),
            vector,
            vector,
            pl.BlockSpec((width, chunk), lambda s, me: (0, s)),
            pl.BlockSpec((width, chunk), lambda s, me: (0, s + steps)),
            pl.BlockSpec((chunk, width), lambda s, me: (s, 0)),
        ],
        [rows, whole((count, 128)), rows, column, column, column, rows],
        [
            shaped((count, width), jnp.float32),
            shaped((count, 128), jnp.float32),
            shaped((count, width)),
            shaped((count, inner)),
            shaped((count, inner)),
            shaped((count, inner)),
            shaped((count, width), jnp.float32),
        ],
        [],
        (
            me,
            tokens,
            attended,
            output_projection,
            first_gain,
            first_offset,
            expand_weight,
            expand_weight,
            reduce_weight,
        ),
        after,
    )


def reduce_kernel(
    me,
    total,
    second_gain,
    second_offset,
    first,
    second,
    third,
    fourth,
    active,
    output_own,
    output_core,
    output_across,
    output_beyond,
    two_out,
    mixed_out,
    gain_out,
    offset_out,
    sent,
    kept,
    cotangent,
    turned,
    *,
    low_bit,
):
    half = turned.shape[0] // 2
    outputs = (output_own, output_core, output_across, output_beyond)

    @pl.when(pl.program_id(0) == 0)
    def _():
        count, width = total.shape
        quarter = first.shape[1]
        for number, piece in enumerate((first, second, third, fourth)):
            for row in range(piece.shape[0]):
                place = (row * 4 + (me[0] ^ number)) * quarter
                cotangent[pl.ds(pl.multiple_of(place, quarter), quarter), :] = piece[row]
        gain = jnp.zeros((1, width), jnp.float32)
        offset = gain
        for start in range(0, count, quarter):
            rows = pl.ds(start, quarter)
            normal, scale = normalize(total[rows, :])
            send_piece(
                me,
                start // quarter,
                low(normal * second_gain[...][None] + second_offset[...][None]),
                outputs,
            )
            back = wide(cotangent[rows, :])
            gain += jnp.sum(back * normal, axis=0, keepdims=True)
            offset += jnp.sum(back, axis=0, keepdims=True)
            two = norm_back(scale, normal, back * second_gain[...][None])
            two_out[rows, :] = two
            mixed_out[rows, :] = low(two)
        gain_out[...] = gain
        offset_out[...] = offset
        turned[...] = mixed_out[...].T

    core = me[0] & 1
    for out, place in ((sent, 1 - core), (kept, core)):
        left = turned[pl.ds(pl.multiple_of(place * half, half), half), :]
        part = low(dot(left, active[...]))
        columns = out.shape[2]
        blocks = [
            part[:, number * columns : (number + 1) * columns] for number in range(out.shape[0])
        ]
        for number, block in enumerate(arranged(blocks, place == 1, low_bit)):
            out[number] = block


def reduce_gradient(
    me,
    total,
    second_gain,
    second_offset,
    cotangent,
    pieces,
    active,
    after=(),
    blocks=8,
    dp_size=8,
):
    count, width = total.shape
    columns = active.shape[1] // blocks
    together = 4 if dp_size <= blocks else blocks
    piece = pieces[0].shape
    rows = whole((count, width))
    vector = whole((1, width))
    out = pl.BlockSpec((together, width // 2, columns), lambda s, me: (s, 0, 0))
    like = shaped((blocks, width // 2, columns))
    return call(
        functools.partial(reduce_kernel, low_bit=together // 4 - 1),
        "reduce_gradient",
        (blocks // together,),
        [
            rows,
            whole((width,)),
            whole((width,)),
            pl.BlockSpec(piece, lambda s, me: (me[0], 0, 0)),
        ]
        + [whole(piece)] * 3
        + [pl.BlockSpec((count, columns * together), lambda s, me: (0, s))],
        [whole(piece)] * 4 + [rows, rows, vector, vector, out, out],
        [shaped(piece)] * 4
        + [
            shaped((count, width), jnp.float32),
            shaped((count, width)),
            shaped((1, width), jnp.float32),
            shaped((1, width), jnp.float32),
            like,
            like,
        ],
        [pltpu.VMEM((count, width), jnp.bfloat16), pltpu.VMEM((width, count), jnp.bfloat16)],
        (me, total, second_gain, second_offset, cotangent, *pieces, active),
        after,
    )


def expand_kernel(
    me,
    mixed,
    hidden,
    gate_part,
    slope_part,
    reduce_weight,
    gate_weight,
    up_weight,
    start,
    sent,
    kept,
    back,
    turned,
    *,
    dp_size,
):
    @pl.when(pl.program_id(0) == 0)
    def _():
        turned[...] = hidden[...].T
        back[...] = start[...]

    weight = jnp.concatenate([gate_weight[...], up_weight[...]], 1)
    back_active = dot(mixed[...], reduce_weight[...], NT)
    both = jnp.concatenate(
        [low(back_active * wide(slope_part[...])), low(back_active * wide(gate_part[...]))], 1
    )
    back[...] += dot(both, weight, NT)
    gradient = low(dot(turned[...], both))
    chunk = gradient.shape[1] // 2
    first = me[0] & 1 == 0
    away = jnp.where(first, gradient[:, chunk:], gradient[:, :chunk])
    mine = jnp.where(first, gradient[:, :chunk], gradient[:, chunk:])
    if dp_size:
        away = arranged_rows(away, first, dp_size)
        mine = arranged_rows(mine, jnp.logical_not(first), dp_size)
    sent[...] = away.reshape(sent.shape)
    kept[...] = mine.reshape(kept.shape)


def expand_gradient(
    me,
    mixed,
    hidden,
    gate_part,
    slope_part,
    reduce_weight,
    expand_weight,
    start,
    part,
    lead,
    dp_size,
    parts=2,
    after=(),
    chunk=768,
):
    count, width = mixed.shape
    inner = reduce_weight.shape[0]
    steps = inner // parts // chunk
    base = part * steps
    all_steps = inner // chunk
    rows = whole((count, width))
    column = pl.BlockSpec((count, chunk), lambda s, me: (0, base + s))
    if lead:
        out = pl.BlockSpec((1, width, chunk), lambda s, me: (s, 0, 0))
        like = shaped((steps, width, chunk))
    else:
        out = pl.BlockSpec((width, chunk), lambda s, me: (0, s))
        like = shaped((width, steps * chunk))
    return call(
        functools.partial(expand_kernel, dp_size=0 if lead else dp_size),
        "expand_gradient",
        (steps,),
        [
            rows,
            rows,
            column,
            column,
            pl.BlockSpec((chunk, width), lambda s, me: (base + s, 0)),
            pl.BlockSpec((width, chunk), lambda s, me: (0, base + s)),
            pl.BlockSpec((width, chunk), lambda s, me: (0, all_steps + base + s)),
            rows,
        ],
        [out, out, rows],
        [like, like, shaped((count, width), jnp.float32)],
        [pltpu.VMEM((width, count), jnp.bfloat16)],
        (
            me,
            mixed,
            hidden,
            gate_part,
            slope_part,
            reduce_weight,
            expand_weight,
            expand_weight,
            start,
        ),
        after,
    )


def branch_kernel(
    me,
    back_hidden,
    normal,
    scale,
    first_gain,
    output_projection,
    one_out,
    back_attended,
    branch,
    gain_out,
    offset_out,
):
    back = back_hidden[...]
    gain = jnp.sum(back * normal[...], axis=0, keepdims=True)
    offset = jnp.sum(back, axis=0, keepdims=True)
    one = norm_back(scale[:, :1], normal[...], back * first_gain[...][None])
    one_out[...] = one
    branch[...] = low(one)
    back_attended[...] = low(dot(low(one), output_projection[...], NT))

    @pl.when(pl.program_id(0) == 0)
    def _():
        gain_out[...] = gain
        offset_out[...] = offset

    @pl.when(pl.program_id(0) > 0)
    def _():
        gain_out[...] += gain
        offset_out[...] += offset


def branch_back(me, back_hidden, normal, scale, first_gain, output_projection, after=(), block=256):
    count, width = back_hidden.shape
    rows = pl.BlockSpec((block, width), lambda s, me: (s, 0))
    vector = whole((1, width))
    return call(
        branch_kernel,
        "branch_back",
        (count // block,),
        [
            rows,
            rows,
            pl.BlockSpec((block, 128), lambda s, me: (s, 0)),
            whole((width,)),
            whole((width, width)),
        ],
        [rows, rows, rows, vector, vector],
        [
            shaped((count, width), jnp.float32),
            shaped((count, width)),
            shaped((count, width)),
            shaped((1, width), jnp.float32),
            shaped((1, width), jnp.float32),
        ],
        [],
        (me, back_hidden, normal, scale, first_gain, output_projection),
        after,
    )


def halves(gradients, me, outs, dp_size):
    front, back = [], []
    for gradient in gradients:
        half = gradient.shape[1] // 2
        front.append(gradient[:, :half])
        back.append(gradient[:, half:])
    front, back = jnp.concatenate(front, axis=1), jnp.concatenate(back, axis=1)
    first = me[0] & 1 == 0
    away, mine = jnp.where(first, back, front), jnp.where(first, front, back)
    outs[0][...] = arranged_rows(away, first, dp_size)
    outs[1][...] = arranged_rows(mine, jnp.logical_not(first), dp_size)


def joint_end_kernel(me, tokens, back_joint, sent, kept, *, dp_size):
    turned = tokens[...].T
    gradients = [low(dot(turned, back_joint[which])) for which in range(3)]
    halves(gradients, me, (sent, kept), dp_size)


def joint_gradient_end(me, tokens, back_joint, dp_size, after=()):
    count, width = tokens.shape
    out = (width, 3 * back_joint.shape[2] // 2)
    return call(
        functools.partial(joint_end_kernel, dp_size=dp_size),
        "joint_gradient_end",
        (1,),
        [whole((count, width)), whole(back_joint.shape)],
        [whole(out)] * 2,
        [shaped(out)] * 2,
        [],
        (me, tokens, back_joint),
        after,
    )


def joint_kernel(
    me, tokens, attended, back_joint, branch, first, second, third, fourth, sent, kept, *, dp_size
):
    turned = tokens[...].T
    gradients = [low(dot(turned, back_joint[which])) for which in range(3)]
    gradients.append(low(dot(attended[...].T, branch[...])))
    rows = jnp.concatenate(
        [first[...], second[...], third[...], fourth[...]]
        + [jnp.zeros((124, first.shape[1]), jnp.float32)]
    )
    columns = low(rows.T)
    gradients.append(jnp.concatenate([columns, columns], axis=1))
    halves(gradients, me, (sent, kept), dp_size)


def joint_gradient(me, tokens, attended, back_joint, branch, vectors, dp_size, after=()):
    count, width = tokens.shape
    out = (width, 3 * back_joint.shape[2] // 2 + width // 2 + 128)
    rows = whole((count, width))
    return call(
        functools.partial(joint_kernel, dp_size=dp_size),
        "joint_gradient",
        (1,),
        [rows, rows, whole(back_joint.shape), rows] + [whole((1, width))] * 4,
        [whole(out)] * 2,
        [shaped(out)] * 2,
        [],
        (me, tokens, attended, back_joint, branch, *vectors),
        after,
    )


def tokens_kernel(me, front, back, weight, one, own, core, across, total):
    step = pl.program_id(0)
    part = dot(jnp.concatenate([front[0], back[0]], axis=1), weight[...], NT)

    @pl.when(step == 0)
    def _():
        total[...] = one[...] + part

    @pl.when(step == 1)
    def _():
        total[...] += part

    @pl.when(step == 2)
    def _():
        value = low(total[...] + part)
        quarter = own.shape[1]
        for place in range(value.shape[0] // quarter):
            rows = slice(place * quarter, (place + 1) * quarter)
            send_piece(me, place, value[rows], (own, core, across.at[0], across.at[1]))


def tokens_gradient_of(me, front, back, joint_projection, one, piece, after=()):
    count, width = one.shape
    rows = whole((count, width))
    return call(
        tokens_kernel,
        "tokens_gradient",
        (3,),
        [pl.BlockSpec((1, count, part.shape[2]), lambda s, me: (s, 0, 0)) for part in (front, back)]
        + [
            pl.BlockSpec((width, width), lambda s, me: (0, s)),
            rows,
        ],
        [whole(piece)] * 2 + [whole((2,) + piece)],
        [shaped(piece)] * 2 + [shaped((2,) + piece)],
        [pltpu.VMEM((count, width), jnp.float32)],
        (me, front, back, joint_projection, one),
        after,
    )


def turn_kernel(me, own, other, out):
    half = own.shape[0]
    mine, others = wide(own[...]).T, wide(other[...]).T
    first = me[0] & 1 == 0
    out[:, :half] = jnp.where(first, mine, others)
    out[:, half:] = jnp.where(first, others, mine)


def turn(me, own, other):
    half, count = own.shape
    return call(
        turn_kernel,
        "turn",
        (1,),
        [whole((half, count))] * 2,
        [whole((count, 2 * half))],
        [shaped((count, 2 * half), jnp.float32)],
        [],
        (me, own, other),
        (),
    )[0]


def exchange(value, axis, bit):
    sizes = (lax.axis_size("dp"), lax.axis_size("head"))
    pairs = []
    for dp in range(sizes[0]):
        for head in range(sizes[1]):
            if axis == "head":
                target = (dp, head ^ bit)
            else:
                target = (dp ^ bit[head & 1], head)
            pairs.append((dp * sizes[1] + head, target[0] * sizes[1] + target[1]))
    return lax.ppermute(value, ("dp", "head"), pairs)


def pick(pieces, place):
    value = pieces[0]
    for number in range(1, len(pieces)):
        value = jnp.where(place == number, pieces[number], value)
    return value


def quarters_to_owners(values, row=None, after=()):
    groups = lax.axis_size("head")
    me = lax.axis_index("head")
    own = values.shape[0] // groups
    values = later(values, *after)
    pieces = []
    for step in range(1, groups):
        start, size = (me ^ step) * own, own
        if row is not None:
            start, size = start + row, 1
        pieces.append(lax.dynamic_slice_in_dim(values, start, size, axis=0))
    return pieces, lambda *after: [
        exchange(later(pieces[step - 1], *after), "head", step) for step in range(1, groups)
    ]


class Pieces:
    def __init__(self, own, core, across):
        self.own = own
        self.core = core
        self.across = exchange(across, "head", 2)

    def pass_on(self, *after):
        across = later(self.across, *after)
        self.across = across[0]
        self.passed = exchange(across[1], "head", 1)
        self.core = exchange(later(self.core, *after), "head", 1)
        return [across]

    def finish(self, *after):
        pieces = [self.own, self.core, self.across, self.passed]
        pieces = [later(piece, *after) for piece in pieces]
        me = lax.axis_index("head")
        return jnp.concatenate([pick(pieces, me ^ place) for place in range(4)], axis=0)


class DirectPieces(Pieces):
    def __init__(self, own, core, across, beyond):
        self.own = own
        self.core = exchange(core, "head", 1)
        self.across = exchange(across, "head", 2)
        self.passed = exchange(beyond, "head", 3)

    def come(self):
        return [self.core, self.across, self.passed]


class Sum:
    def __init__(self, sent, kept):
        self.bits = lax.axis_size("dp").bit_length() - 1
        self.lead = kept.ndim - 3
        self.tail = kept.shape[-2:]
        self.front = kept.shape[: self.lead]
        self.chosen = {}
        self.terms = [(self.split(kept), ())]
        self.coming = self.split(exchange(sent, "head", 1))

    def split(self, value):
        return value.reshape(self.front + (2,) * self.bits + self.tail)

    def total(self, wanted, after=()):
        value = None
        for term, cut in self.terms:
            term = later(term, *after)
            starts = [0] * term.ndim
            sizes = list(term.shape)
            for axis, place in wanted.items():
                if axis not in cut:
                    starts[axis], sizes[axis] = place, 1
            piece = wide(lax.dynamic_slice(term, starts, sizes))
            value = piece if value is None else value + piece
        return value

    def arrive(self):
        if self.coming is not None:
            self.terms.append((self.coming, tuple(self.chosen)))
            self.coming = None

    def halve(self, step, *after):
        self.arrive()
        low_bit = near_bit(1 << self.bits)
        if step == "y":
            axis, mine = 0, lax.axis_index("head") >> 1
        else:
            steps = {"near": (low_bit, low_bit + 1), "far": (low_bit + 1, low_bit)}
            steps = steps.get(step, (step, step))
            axis = self.lead + self.bits - 1 - steps[0]
            step = jnp.where(lax.axis_index("head") & 1 == 0, *steps)
            mine = (lax.axis_index("dp") >> step) & 1
        away = dict(self.chosen)
        away[axis] = 1 - mine
        sent = low(self.total(away, after))
        self.chosen[axis] = mine
        if axis == 0 and self.lead:
            self.coming = exchange(sent, "head", 2)
        else:
            self.coming = exchange(sent, "dp", [1 << step for step in steps])
        return sent

    def rest(self, steps, *after):
        for step in steps:
            self.halve(step, *after)
        return self.own(*after)

    def own(self, *after):
        self.arrive()
        value = low(self.total(self.chosen, after))
        return value.reshape(value.shape[: self.lead] + self.tail)


def sum_y(own, *after):
    other = exchange(own, "head", 2)
    return low(wide(later(own, *after)) + wide(other))


def join(own, bit, axis, *after):
    own = later(own, *after)
    return join_parts(own, exchange(own, "head", bit), bit, axis)


def join_parts(own, other, bit, axis):
    first = lax.axis_index("head") & bit == 0
    return jnp.concatenate(
        (jnp.where(first, own, other), jnp.where(first, other, own)), axis=axis
    )


def local(
    tokens,
    segment_labels,
    joint_projection,
    output_projection,
    first_gain,
    first_offset,
    expand_weight,
    reduce_weight,
    second_gain,
    second_offset,
    cotangent,
):
    width = tokens.shape[2]
    length = segment_labels.shape[1]
    dp_size = lax.axis_size("dp")
    bits = dp_size.bit_length() - 1
    own_width = width // dp_size
    inner = reduce_weight.shape[0]
    me = lax.axis_index("head")
    group = jnp.reshape(me, (1,))
    up_order = list(range(bits))
    slopes = jnp.asarray(head_slopes(H), dtype=jnp.float32)
    row_count = tokens.shape[0] // lax.axis_size("head")
    flat = lambda value: value.reshape(row_count * length, width)
    rowed = lambda value: value.reshape(row_count, length, width)
    piece = (row_count,) + tokens.shape[1:]

    pieces, early = [], ()
    for row in range(row_count):
        early, exchange_tokens = quarters_to_owners(tokens, row, early)
        pieces.append(exchange_tokens())
    early, exchange_cotangent = quarters_to_owners(cotangent, after=early)
    front = ()
    for row in range(row_count):
        front = attend(
            later(group, *early),
            slopes,
            segment_labels,
            tokens,
            pieces[row],
            joint_projection,
            row,
            front,
        )
    own_tokens, queries, keys, values, probs, attended = front
    cotangent_pieces = exchange_cotangent(attended)
    normal, scale, hidden, gate_part, slope_part, active, total = ahead(
        group,
        flat(own_tokens),
        flat(attended),
        output_projection,
        first_gain,
        first_offset,
        expand_weight,
        reduce_weight,
    )
    blocks = 8
    *output, back_two, back_mixed, second_gain_back, second_offset_back, sent, kept = (
        reduce_gradient(
            group,
            total,
            second_gain,
            second_offset,
            cotangent,
            cotangent_pieces,
            active,
            dp_size=dp_size,
        )
    )
    output = DirectPieces(*output)
    by_device = lambda value: (
        value.reshape(blocks, width // 2, dp_size // blocks, inner // dp_size)
        .transpose(0, 2, 1, 3)
        .reshape(dp_size, width // 2, inner // dp_size)
    )
    reduce_sum = Sum(by_device(sent), by_device(kept))
    low_bit = near_bit(dp_size)
    others = [step for step in up_order if step not in (low_bit, low_bit + 1)]
    rest = (group, back_mixed, hidden, gate_part, slope_part, reduce_weight, expand_weight)
    cut = lambda value: value.reshape(value.shape[0], dp_size, own_width, value.shape[2])
    slab = lambda value: value.reshape(dp_size, own_width, value.shape[1])
    sent, kept, back_hidden = expand_gradient(*rest, back_two, 0, True, dp_size, after=[kept])
    expand_first = Sum(cut(sent), cut(kept))
    moved = [reduce_sum.halve("near", back_hidden)]
    moved += output.come()
    sent, kept, back_hidden = expand_gradient(*rest, back_hidden, 1, False, dp_size, after=moved)
    expand_second = Sum(slab(sent), slab(kept))
    moved = [expand_first.halve("y", back_hidden)]
    moved = [reduce_sum.halve("far", *moved)]
    back_one, back_attended, branch, first_gain_back, first_offset_back = branch_back(
        group, back_hidden, normal, scale, first_gain, output_projection, after=moved
    )
    moved = [expand_second.halve("near", back_one)]
    moved = [reduce_sum.halve(others[0], *moved)]
    heads = (group, queries, keys, values, probs, attended, rowed(back_attended))
    columns = lambda value: value.reshape(3, row_count * length, value.shape[3])
    front = columns(attend_back(*heads, 0, 2, after=moved)[0])
    moved = [expand_first.halve(1, front)]
    moved = [expand_second.halve("far", *moved)]
    vectors = (first_gain_back, first_offset_back, second_gain_back, second_offset_back)
    sent, kept = joint_gradient(
        group, flat(own_tokens), flat(attended), front, branch, vectors, dp_size, after=moved
    )
    joint_first = Sum(slab(sent), slab(kept))
    moved = [expand_first.halve(0, kept)]
    moved = [expand_second.halve(others[0], *moved)]
    back = columns(attend_back(*heads, 2, 1, after=moved)[0])
    moved = [joint_first.halve("near", back)]
    sent, kept = joint_gradient_end(group, flat(own_tokens), back, dp_size, after=moved)
    joint_last = Sum(slab(sent), slab(kept))
    moved = [expand_first.halve(2, kept)]
    gradient = tokens_gradient_of(
        group, front, back, joint_projection, back_one, piece, after=moved
    )

    moved = [joint_last.halve("near", gradient[0])]
    moved = [joint_first.halve("far", *moved)]
    gradient = Pieces(*[later(part, *moved) for part in gradient])
    reduce_own = reduce_sum.rest(others[1:], *moved)
    reduce_other = exchange(reduce_own, "head", 2)
    moved = [joint_last.halve("far", reduce_own)]
    moved = [joint_first.halve(others[0], *moved)]
    first_own = expand_first.rest(up_order[3:], *moved)
    first_other = exchange(first_own, "head", 2)
    moved = [joint_last.halve(others[0], first_own)]
    output = output.finish(*moved)
    first_own = later(first_own, output)
    reduce_own = low(wide(later(reduce_own, first_own)) + wide(reduce_other))
    reduce_other = exchange(reduce_own, "head", 1)
    second_own = expand_second.rest(others[1:], reduce_own)
    second_other = exchange(second_own, "head", 2)
    moved = gradient.pass_on(second_own)
    first_grad = join_parts(later(first_own, *moved), first_other, 2, 0)
    first_other = exchange(first_grad, "head", 1)
    joint_own = [joint_first.rest(others[1:], first_grad)]
    joint_other = [exchange(joint_own[0], "head", 2)]
    joint_own += [joint_last.rest(others[1:], *joint_own)]
    joint_other += [exchange(joint_own[1], "head", 2)]
    reduce_grad = turn(later(group, joint_own[1]), reduce_own, reduce_other)
    gradient = gradient.finish(reduce_grad)
    second_own = low(wide(later(second_own, gradient)) + wide(second_other))
    second_grad = join(second_own[None], 1, 0)
    first_grad = join_parts(later(first_grad, second_own)[None], first_other[None], 1, 0)
    joint_own = [
        low(wide(later(own, second_own)) + wide(other))
        for own, other in zip(joint_own, joint_other)
    ]
    expand_grad = jnp.concatenate(
        [
            piece
            for side in range(2)
            for piece in (
                first_grad[side, 0],
                first_grad[side, 1],
                second_grad[side],
            )
        ],
        axis=-1,
    )
    vectors = wide(joint_own[0][:, -128:-124])
    both = join(jnp.concatenate((joint_own[0][:, :-128], joint_own[1]), axis=1)[None], 1, 0)
    size = front.shape[2] // 2
    last = back.shape[2] // 2
    start = 3 * size + width // 2
    joint_grad = []
    for which in range(3):
        for begin, count in ((which * size, size), (start + which * last, last)):
            joint_grad += [both[side, :, begin : begin + count] for side in range(2)]
    projection_grad = [both[side, :, 3 * size : start] for side in range(2)]
    return (
        output,
        gradient,
        wide(jnp.concatenate(joint_grad, axis=-1)),
        wide(jnp.concatenate(projection_grad, axis=-1)),
        vectors[:, 0],
        vectors[:, 1],
        wide(expand_grad),
        reduce_grad,
        vectors[:, 2],
        vectors[:, 3],
    )


def solution(mesh):
    placed = (
        P("dp", "head", None),
        P("dp", None),
        P(),
        P(),
        P(),
        P(),
        P(),
        P(),
        P(),
        P(),
        P("dp", "head", None),
    )
    return jax.shard_map(
        local,
        mesh=mesh,
        in_specs=placed,
        out_specs=(
            P("dp", "head", None),
            P("dp", "head", None),
            P("dp", None),
            P("dp", None),
            P("dp"),
            P("dp"),
            P("dp", None),
            P("dp", None),
            P("dp"),
            P("dp"),
        ),
        check_vma=False,
    )
```

```python
import functools
import math

import jax
import jax.numpy as jnp
import numpy as np
from jax import lax
from jax.experimental import pallas as pl
from jax.experimental.pallas import tpu as pltpu
from jax.sharding import PartitionSpec as P

H = 12
DH = 64


EPSILON = 1e-12
NEG_FILL = -1e30
LOG2E = 1.4426950408889634
NN = (((1,), (0,)), ((), ()))
NT = (((1,), (1,)), ((), ()))
TN = (((0,), (0,)), ((), ()))
VMEM_BYTES = 48 * 2**20
ANY = pl.BlockSpec(memory_space=pl.ANY)
SMEM = pl.BlockSpec(memory_space=pltpu.SMEM)


def head_slopes(heads_total):
    closest = 2 ** int(math.floor(math.log2(heads_total)))

    def power_slopes(number):
        first_slope = 2.0 ** (-8.0 / number)
        return [first_slope ** (counter + 1) for counter in range(number)]

    listed = power_slopes(closest)
    listed = listed + power_slopes(2 * closest)[0::2][: heads_total - closest]
    return np.array(listed, dtype=np.float32)


def low(value):
    return value.astype(jnp.bfloat16)


def wide(value):
    return value.astype(jnp.float32)


def dot(left, right, dims=NN):
    return lax.dot_general(left, right, dims, preferred_element_type=jnp.float32)


def shaped(shape, dtype=jnp.bfloat16):
    return jax.ShapeDtypeStruct(shape, dtype)


def whole(shape):
    return pl.BlockSpec(shape, lambda *_: (0,) * len(shape))


def later(value, *arrays):
    if not arrays:
        return value
    token = lax.optimization_barrier((lax.create_token(), *arrays))[0]
    return lax.optimization_barrier((token, value))[1]


def once(spec, operand):
    if spec.block_shape is not None and tuple(spec.block_shape) == operand.shape:
        return pl.BlockSpec(spec.block_shape, spec.index_map, pipeline_mode=pl.Buffered(1))
    return spec


def call(kernel, name, grid, in_specs, out_specs, out_shape, scratch, operands, after, into=()):
    operands = (later(operands[0], *after),) + tuple(operands[1:])
    count = len(operands) - 1
    extra = len(into)

    def run(me, *refs):
        kernel(me, *refs[:count], *refs[count + extra :])

    return pl.pallas_call(
        run,
        grid_spec=pltpu.PrefetchScalarGridSpec(
            num_scalar_prefetch=1,
            grid=grid,
            in_specs=[once(spec, operand) for spec, operand in zip(in_specs, operands[1:])]
            + [ANY] * extra,
            out_specs=list(out_specs),
            scratch_shapes=scratch,
        ),
        out_shape=list(out_shape),
        input_output_aliases={count + 1 + number: number for number in range(len(into))},
        compiler_params=pltpu.CompilerParams(
            vmem_limit_bytes=VMEM_BYTES, dimension_semantics=("arbitrary",) * len(grid)
        ),
        cost_estimate=pl.CostEstimate(flops=10**12, bytes_accessed=0, transcendentals=0),
        name=name,
    )(*operands, *into)


def near_bit(dp_size):
    return 0 if dp_size <= 8 else dp_size.bit_length() - 3


def arranged(blocks, swapped, low_bit=0):
    near, far = 1 << low_bit, 2 << low_bit
    result = []
    for number, block in enumerate(blocks):
        if bool(number & near) != bool(number & far):
            block = jnp.where(swapped, blocks[number ^ near ^ far], block)
        result.append(block)
    return result


def arranged_rows(value, swapped, dp_size):
    count = dp_size >> near_bit(dp_size)
    rows = value.shape[0] // count
    blocks = [value[number * rows : (number + 1) * rows] for number in range(count)]
    return jnp.concatenate(arranged(blocks, swapped), axis=0)


def normalize(value):
    center = value - jnp.mean(value, axis=-1, keepdims=True)
    scale = lax.rsqrt(jnp.mean(center * center, axis=-1, keepdims=True) + EPSILON)
    return center * scale, scale


def norm_back(scale, normal, back):
    return scale * (
        back
        - jnp.mean(back, axis=-1, keepdims=True)
        - normal * jnp.mean(back * normal, axis=-1, keepdims=True)
    )


def attend_kernel(
    me,
    slopes,
    labels,
    first,
    second,
    third,
    fourth,
    query_weight,
    key_weight,
    value_weight,
    tokens_out,
    queries_out,
    keys_out,
    values_out,
    probs_out,
    attended_out,
    bias,
    *,
    row,
    heads,
):
    group = pl.program_id(0)
    _, length, width = tokens_out.shape
    quarter = length // 4

    @pl.when(group == 0)
    def _():
        for step, piece in enumerate((first, second, third, fourth)):
            place = pl.multiple_of((me[0] ^ step) * quarter, quarter)
            tokens_out[0, pl.ds(place, quarter), :] = piece[0]
        label = labels[pl.ds(me[0] * 2 + row, 1), :]
        column = jnp.broadcast_to(label, (128, length)).T[:, :1]
        rows = lax.broadcasted_iota(jnp.int32, (length, length), 0)
        columns = lax.broadcasted_iota(jnp.int32, (length, length), 1)
        gap = -wide(jnp.abs(rows - columns))
        bias[...] = jnp.where(column == label, gap, NEG_FILL)

    tokens = tokens_out[0]
    queries = low(dot(tokens, query_weight[...]))
    keys = low(dot(tokens, key_weight[...]))
    values = low(dot(tokens, value_weight[...]))
    queries_out[0] = queries
    keys_out[0] = keys
    values_out[0] = values
    owner = lax.broadcasted_iota(jnp.int32, keys.shape, 1) // DH
    turned = values.T
    raw = []
    for head in range(heads):
        own_keys = jnp.where(owner == head, keys, jnp.zeros_like(keys))
        raw.append(dot(own_keys, queries, NT))
    parts = []
    for head in range(heads):
        slope = slopes[group * heads + head] * LOG2E
        scores = raw[head] * (DH**-0.5 * LOG2E) + bias[...] * slope
        exponent = jnp.exp2(scores - jnp.max(scores, axis=0, keepdims=True))
        probs = low(exponent * (1.0 / jnp.sum(exponent, axis=0, keepdims=True)))
        probs_out[0, head] = probs
        parts.append(dot(turned[head * DH : (head + 1) * DH], probs))
    attended_out[0] = low(jnp.concatenate(parts, axis=0).T)


def attend(me, slopes, labels, tokens, pieces, joint_projection, row, into=(), heads=4):
    _, quarter, width = tokens.shape
    length = labels.shape[1]
    rows = tokens.shape[0] // 4
    groups = H // heads
    group_width = heads * DH
    weight = [
        pl.BlockSpec((width, group_width), lambda g, me, which=which: (0, which * groups + g))
        for which in range(3)
    ]
    out = pl.BlockSpec((1, length, group_width), lambda g, me: (row, 0, g))
    like = shaped((rows, length, width))
    return call(
        functools.partial(attend_kernel, row=row, heads=heads),
        "attend",
        (groups,),
        [
            SMEM,
            whole(labels.shape),
            pl.BlockSpec((1, quarter, width), lambda g, me: (me[0] * rows + row, 0, 0)),
        ]
        + [whole((1, quarter, width))] * 3
        + weight,
        [pl.BlockSpec((1, length, width), lambda g, me: (row, 0, 0)), out, out, out]
        + [pl.BlockSpec((1, heads, length, length), lambda g, me: (row, g, 0, 0)), out],
        [like, like, like, like, shaped((rows, H, length, length)), like],
        [pltpu.VMEM((length, length), jnp.float32)],
        (me, slopes, labels, tokens, *pieces) + (joint_projection,) * 3,
        (),
        into,
    )


def attend_back_kernel(
    me, queries_ref, keys_ref, values_ref, probs_ref, attended, back_attended, back_joint, *, heads
):
    queries, keys, values = queries_ref[0], keys_ref[0], values_ref[0]
    back = back_attended[0]
    owner = lax.broadcasted_iota(jnp.int32, keys.shape, 1) // DH
    zero = jnp.zeros_like(keys)
    product = (wide(attended[0]) * wide(back)).T
    turned = keys.T
    probs_all, scores_all, back_all, queries_all, parts = [], [], [], [], []
    back_probs = [dot(jnp.where(owner == head, values, zero), back, NT) for head in range(heads)]
    for head in range(heads):
        mine = owner == head
        lanes = slice(head * DH, (head + 1) * DH)
        inner = jnp.sum(product[lanes], axis=0, keepdims=True)
        probs = probs_ref[0, head]
        back_scores = low(wide(probs) * (back_probs[head] - inner))
        probs_all.append(probs)
        scores_all.append(back_scores)
        back_all.append(jnp.where(mine, back, zero))
        queries_all.append(jnp.where(mine, queries, zero))
        parts.append(dot(turned[lanes], back_scores))
    scale = DH**-0.5
    back_joint[2, 0] = low(dot(jnp.concatenate(probs_all, 1), jnp.concatenate(back_all, 0)))
    back_joint[1, 0] = low(
        dot(jnp.concatenate(scores_all, 1), jnp.concatenate(queries_all, 0)) * scale
    )
    back_joint[0, 0] = low(jnp.concatenate(parts, 0).T * scale)


def attend_back(
    me, queries, keys, values, probs, attended, back_attended, base, groups, after=(), heads=4
):
    rows, length, _ = queries.shape
    group_width = heads * DH
    spec = pl.BlockSpec((1, length, group_width), lambda r, g, me: (r, 0, base + g))
    return call(
        functools.partial(attend_back_kernel, heads=heads),
        "attend_back",
        (rows, groups),
        [spec] * 3
        + [
            pl.BlockSpec((1, heads, length, length), lambda r, g, me: (r, base + g, 0, 0)),
            spec,
            spec,
        ],
        [pl.BlockSpec((3, 1, length, group_width), lambda r, g, me: (0, r, 0, g))],
        [shaped((3, rows, length, groups * group_width))],
        [],
        (me, queries, keys, values, probs, attended, back_attended),
        after,
    )


def send_piece(me, place, value, outs):
    far = (place % 4) ^ me[0]
    for number, out in enumerate(outs):

        @pl.when(far == number)
        def _():
            out[place // 4] = value


def ahead_kernel(
    me,
    tokens,
    attended,
    output_projection,
    first_gain,
    first_offset,
    gate_weight,
    up_weight,
    reduce_weight,
    normal_out,
    scale_out,
    hidden_out,
    gate_out,
    slope_out,
    active_out,
    total,
    *,
    block,
):
    step = pl.program_id(0)
    count, width = tokens.shape
    blocks = [pl.ds(start, block) for start in range(0, count, block)]

    @pl.when(step == 0)
    def _():
        for rows in blocks:
            branch = dot(attended[rows, :], output_projection[...])
            normal, scale = normalize(wide(tokens[rows, :]) + branch)
            normal_out[rows, :] = normal
            scale_out[rows, :] = jnp.broadcast_to(scale, (block, scale_out.shape[1]))
            hidden = normal * first_gain[...][None] + first_offset[...][None]
            hidden_out[rows, :] = low(hidden)
            total[rows, :] = hidden

    blocks = [pl.ds(start, 2 * block) for start in range(0, count, 2 * block)]
    products = []
    for rows in blocks:
        hidden = hidden_out[rows, :]
        products.append((dot(hidden, gate_weight[...]), dot(hidden, up_weight[...])))
    for rows, (gate, up) in zip(blocks, products):
        share = 0.5 * (1.0 + lax.erf(gate * 0.5**0.5))
        density = jnp.exp(gate * gate * -0.5) * (2.0 * math.pi) ** -0.5
        unit = gate * share
        active = low(unit * up)
        gate_out[rows, :] = low(unit)
        slope_out[rows, :] = low(up * (share + gate * density))
        active_out[rows, :] = active
        total[rows, :] += dot(active, reduce_weight[...])


def ahead(
    me,
    tokens,
    attended,
    output_projection,
    first_gain,
    first_offset,
    expand_weight,
    reduce_weight,
    after=(),
    chunk=512,
    block=256,
):
    count, width = tokens.shape
    inner = reduce_weight.shape[0]
    steps = inner // chunk
    vector = whole((width,))
    rows = whole((count, width))
    column = pl.BlockSpec((count, chunk), lambda s, me: (0, s))
    return call(
        functools.partial(ahead_kernel, block=block),
        "ahead",
        (steps,),
        [
            rows,
            rows,
            whole((width, width)),
            vector,
            vector,
            pl.BlockSpec((width, chunk), lambda s, me: (0, s)),
            pl.BlockSpec((width, chunk), lambda s, me: (0, s + steps)),
            pl.BlockSpec((chunk, width), lambda s, me: (s, 0)),
        ],
        [rows, whole((count, 128)), rows, column, column, column, rows],
        [
            shaped((count, width), jnp.float32),
            shaped((count, 128), jnp.float32),
            shaped((count, width)),
            shaped((count, inner)),
            shaped((count, inner)),
            shaped((count, inner)),
            shaped((count, width), jnp.float32),
        ],
        [],
        (
            me,
            tokens,
            attended,
            output_projection,
            first_gain,
            first_offset,
            expand_weight,
            expand_weight,
            reduce_weight,
        ),
        after,
    )


def reduce_kernel(
    me,
    total,
    second_gain,
    second_offset,
    first,
    second,
    third,
    fourth,
    active,
    output_own,
    output_core,
    output_across,
    output_beyond,
    two_out,
    mixed_out,
    gain_out,
    offset_out,
    sent,
    kept,
    cotangent,
    turned,
    *,
    low_bit,
):
    half = turned.shape[0] // 2
    outputs = (output_own, output_core, output_across, output_beyond)

    @pl.when(pl.program_id(0) == 0)
    def _():
        count, width = total.shape
        quarter = first.shape[1]
        for number, piece in enumerate((first, second, third, fourth)):
            for row in range(piece.shape[0]):
                place = (row * 4 + (me[0] ^ number)) * quarter
                cotangent[pl.ds(pl.multiple_of(place, quarter), quarter), :] = piece[row]
        gain = jnp.zeros((1, width), jnp.float32)
        offset = gain
        for start in range(0, count, quarter):
            rows = pl.ds(start, quarter)
            normal, scale = normalize(total[rows, :])
            send_piece(
                me,
                start // quarter,
                low(normal * second_gain[...][None] + second_offset[...][None]),
                outputs,
            )
            back = wide(cotangent[rows, :])
            gain += jnp.sum(back * normal, axis=0, keepdims=True)
            offset += jnp.sum(back, axis=0, keepdims=True)
            two = norm_back(scale, normal, back * second_gain[...][None])
            two_out[rows, :] = two
            mixed_out[rows, :] = low(two)
        gain_out[...] = gain
        offset_out[...] = offset
        turned[...] = mixed_out[...].T

    core = me[0] & 1
    for out, place in ((sent, 1 - core), (kept, core)):
        left = turned[pl.ds(pl.multiple_of(place * half, half), half), :]
        part = low(dot(left, active[...]))
        columns = out.shape[2]
        blocks = [
            part[:, number * columns : (number + 1) * columns] for number in range(out.shape[0])
        ]
        for number, block in enumerate(arranged(blocks, place == 1, low_bit)):
            out[number] = block


def reduce_gradient(
    me,
    total,
    second_gain,
    second_offset,
    cotangent,
    pieces,
    active,
    after=(),
    blocks=8,
    dp_size=8,
):
    count, width = total.shape
    columns = active.shape[1] // blocks
    together = 4 if dp_size <= blocks else blocks
    piece = pieces[0].shape
    rows = whole((count, width))
    vector = whole((1, width))
    out = pl.BlockSpec((together, width // 2, columns), lambda s, me: (s, 0, 0))
    like = shaped((blocks, width // 2, columns))
    return call(
        functools.partial(reduce_kernel, low_bit=together // 4 - 1),
        "reduce_gradient",
        (blocks // together,),
        [
            rows,
            whole((width,)),
            whole((width,)),
            pl.BlockSpec(piece, lambda s, me: (me[0], 0, 0)),
        ]
        + [whole(piece)] * 3
        + [pl.BlockSpec((count, columns * together), lambda s, me: (0, s))],
        [whole(piece)] * 4 + [rows, rows, vector, vector, out, out],
        [shaped(piece)] * 4
        + [
            shaped((count, width), jnp.float32),
            shaped((count, width)),
            shaped((1, width), jnp.float32),
            shaped((1, width), jnp.float32),
            like,
            like,
        ],
        [pltpu.VMEM((count, width), jnp.bfloat16), pltpu.VMEM((width, count), jnp.bfloat16)],
        (me, total, second_gain, second_offset, cotangent, *pieces, active),
        after,
    )


def expand_kernel(
    me,
    mixed,
    hidden,
    gate_part,
    slope_part,
    reduce_weight,
    gate_weight,
    up_weight,
    start,
    sent,
    kept,
    back,
    turned,
    *,
    dp_size,
):
    @pl.when(pl.program_id(0) == 0)
    def _():
        turned[...] = hidden[...].T
        back[...] = start[...]

    weight = jnp.concatenate([gate_weight[...], up_weight[...]], 1)
    back_active = dot(mixed[...], reduce_weight[...], NT)
    both = jnp.concatenate(
        [low(back_active * wide(slope_part[...])), low(back_active * wide(gate_part[...]))], 1
    )
    back[...] += dot(both, weight, NT)
    gradient = low(dot(turned[...], both))
    chunk = gradient.shape[1] // 2
    first = me[0] & 1 == 0
    away = jnp.where(first, gradient[:, chunk:], gradient[:, :chunk])
    mine = jnp.where(first, gradient[:, :chunk], gradient[:, chunk:])
    if dp_size:
        away = arranged_rows(away, first, dp_size)
        mine = arranged_rows(mine, jnp.logical_not(first), dp_size)
    sent[...] = away.reshape(sent.shape)
    kept[...] = mine.reshape(kept.shape)


def expand_gradient(
    me,
    mixed,
    hidden,
    gate_part,
    slope_part,
    reduce_weight,
    expand_weight,
    start,
    part,
    lead,
    dp_size,
    parts=2,
    after=(),
    chunk=768,
):
    count, width = mixed.shape
    inner = reduce_weight.shape[0]
    steps = inner // parts // chunk
    base = part * steps
    all_steps = inner // chunk
    rows = whole((count, width))
    column = pl.BlockSpec((count, chunk), lambda s, me: (0, base + s))
    if lead:
        out = pl.BlockSpec((1, width, chunk), lambda s, me: (s, 0, 0))
        like = shaped((steps, width, chunk))
    else:
        out = pl.BlockSpec((width, chunk), lambda s, me: (0, s))
        like = shaped((width, steps * chunk))
    return call(
        functools.partial(expand_kernel, dp_size=0 if lead else dp_size),
        "expand_gradient",
        (steps,),
        [
            rows,
            rows,
            column,
            column,
            pl.BlockSpec((chunk, width), lambda s, me: (base + s, 0)),
            pl.BlockSpec((width, chunk), lambda s, me: (0, base + s)),
            pl.BlockSpec((width, chunk), lambda s, me: (0, all_steps + base + s)),
            rows,
        ],
        [out, out, rows],
        [like, like, shaped((count, width), jnp.float32)],
        [pltpu.VMEM((width, count), jnp.bfloat16)],
        (
            me,
            mixed,
            hidden,
            gate_part,
            slope_part,
            reduce_weight,
            expand_weight,
            expand_weight,
            start,
        ),
        after,
    )


def branch_kernel(
    me,
    back_hidden,
    normal,
    scale,
    first_gain,
    output_projection,
    one_out,
    back_attended,
    branch,
    gain_out,
    offset_out,
):
    back = back_hidden[...]
    gain = jnp.sum(back * normal[...], axis=0, keepdims=True)
    offset = jnp.sum(back, axis=0, keepdims=True)
    one = norm_back(scale[:, :1], normal[...], back * first_gain[...][None])
    one_out[...] = one
    branch[...] = low(one)
    back_attended[...] = low(dot(low(one), output_projection[...], NT))

    @pl.when(pl.program_id(0) == 0)
    def _():
        gain_out[...] = gain
        offset_out[...] = offset

    @pl.when(pl.program_id(0) > 0)
    def _():
        gain_out[...] += gain
        offset_out[...] += offset


def branch_back(me, back_hidden, normal, scale, first_gain, output_projection, after=(), block=256):
    count, width = back_hidden.shape
    rows = pl.BlockSpec((block, width), lambda s, me: (s, 0))
    vector = whole((1, width))
    return call(
        branch_kernel,
        "branch_back",
        (count // block,),
        [
            rows,
            rows,
            pl.BlockSpec((block, 128), lambda s, me: (s, 0)),
            whole((width,)),
            whole((width, width)),
        ],
        [rows, rows, rows, vector, vector],
        [
            shaped((count, width), jnp.float32),
            shaped((count, width)),
            shaped((count, width)),
            shaped((1, width), jnp.float32),
            shaped((1, width), jnp.float32),
        ],
        [],
        (me, back_hidden, normal, scale, first_gain, output_projection),
        after,
    )


def halves(gradients, me, outs, dp_size):
    front, back = [], []
    for gradient in gradients:
        half = gradient.shape[1] // 2
        front.append(gradient[:, :half])
        back.append(gradient[:, half:])
    front, back = jnp.concatenate(front, axis=1), jnp.concatenate(back, axis=1)
    first = me[0] & 1 == 0
    away, mine = jnp.where(first, back, front), jnp.where(first, front, back)
    outs[0][...] = arranged_rows(away, first, dp_size)
    outs[1][...] = arranged_rows(mine, jnp.logical_not(first), dp_size)


def joint_end_kernel(me, tokens, back_joint, sent, kept, *, dp_size):
    turned = tokens[...].T
    gradients = [low(dot(turned, back_joint[which])) for which in range(3)]
    halves(gradients, me, (sent, kept), dp_size)


def joint_gradient_end(me, tokens, back_joint, dp_size, after=()):
    count, width = tokens.shape
    out = (width, 3 * back_joint.shape[2] // 2)
    return call(
        functools.partial(joint_end_kernel, dp_size=dp_size),
        "joint_gradient_end",
        (1,),
        [whole((count, width)), whole(back_joint.shape)],
        [whole(out)] * 2,
        [shaped(out)] * 2,
        [],
        (me, tokens, back_joint),
        after,
    )


def joint_kernel(
    me, tokens, attended, back_joint, branch, first, second, third, fourth, sent, kept, *, dp_size
):
    turned = tokens[...].T
    gradients = [low(dot(turned, back_joint[which])) for which in range(3)]
    gradients.append(low(dot(attended[...].T, branch[...])))
    rows = jnp.concatenate(
        [first[...], second[...], third[...], fourth[...]]
        + [jnp.zeros((124, first.shape[1]), jnp.float32)]
    )
    columns = low(rows.T)
    gradients.append(jnp.concatenate([columns, columns], axis=1))
    halves(gradients, me, (sent, kept), dp_size)


def joint_gradient(me, tokens, attended, back_joint, branch, vectors, dp_size, after=()):
    count, width = tokens.shape
    out = (width, 3 * back_joint.shape[2] // 2 + width // 2 + 128)
    rows = whole((count, width))
    return call(
        functools.partial(joint_kernel, dp_size=dp_size),
        "joint_gradient",
        (1,),
        [rows, rows, whole(back_joint.shape), rows] + [whole((1, width))] * 4,
        [whole(out)] * 2,
        [shaped(out)] * 2,
        [],
        (me, tokens, attended, back_joint, branch, *vectors),
        after,
    )


def tokens_kernel(me, front, back, weight, one, own, core, across, total):
    step = pl.program_id(0)
    part = dot(jnp.concatenate([front[0], back[0]], axis=1), weight[...], NT)

    @pl.when(step == 0)
    def _():
        total[...] = one[...] + part

    @pl.when(step == 1)
    def _():
        total[...] += part

    @pl.when(step == 2)
    def _():
        value = low(total[...] + part)
        quarter = own.shape[1]
        for place in range(value.shape[0] // quarter):
            rows = slice(place * quarter, (place + 1) * quarter)
            send_piece(me, place, value[rows], (own, core, across.at[0], across.at[1]))


def tokens_gradient_of(me, front, back, joint_projection, one, piece, after=()):
    count, width = one.shape
    rows = whole((count, width))
    return call(
        tokens_kernel,
        "tokens_gradient",
        (3,),
        [pl.BlockSpec((1, count, part.shape[2]), lambda s, me: (s, 0, 0)) for part in (front, back)]
        + [
            pl.BlockSpec((width, width), lambda s, me: (0, s)),
            rows,
        ],
        [whole(piece)] * 2 + [whole((2,) + piece)],
        [shaped(piece)] * 2 + [shaped((2,) + piece)],
        [pltpu.VMEM((count, width), jnp.float32)],
        (me, front, back, joint_projection, one),
        after,
    )


def turn_kernel(me, own, other, out):
    half = own.shape[0]
    mine, others = wide(own[...]).T, wide(other[...]).T
    first = me[0] & 1 == 0
    out[:, :half] = jnp.where(first, mine, others)
    out[:, half:] = jnp.where(first, others, mine)


def turn(me, own, other):
    half, count = own.shape
    return call(
        turn_kernel,
        "turn",
        (1,),
        [whole((half, count))] * 2,
        [whole((count, 2 * half))],
        [shaped((count, 2 * half), jnp.float32)],
        [],
        (me, own, other),
        (),
    )[0]


def exchange(value, axis, bit):
    sizes = (lax.axis_size("dp"), lax.axis_size("head"))
    pairs = []
    for dp in range(sizes[0]):
        for head in range(sizes[1]):
            if axis == "head":
                target = (dp, head ^ bit)
            else:
                target = (dp ^ bit[head & 1], head)
            pairs.append((dp * sizes[1] + head, target[0] * sizes[1] + target[1]))
    return lax.ppermute(value, ("dp", "head"), pairs)


def pick(pieces, place):
    value = pieces[0]
    for number in range(1, len(pieces)):
        value = jnp.where(place == number, pieces[number], value)
    return value


def quarters_to_owners(values, row=None, after=()):
    groups = lax.axis_size("head")
    me = lax.axis_index("head")
    own = values.shape[0] // groups
    values = later(values, *after)
    pieces = []
    for step in range(1, groups):
        start, size = (me ^ step) * own, own
        if row is not None:
            start, size = start + row, 1
        pieces.append(lax.dynamic_slice_in_dim(values, start, size, axis=0))
    return pieces, lambda *after: [
        exchange(later(pieces[step - 1], *after), "head", step) for step in range(1, groups)
    ]


class Pieces:
    def __init__(self, own, core, across):
        self.own = own
        self.core = core
        self.across = exchange(across, "head", 2)

    def pass_on(self, *after):
        across = later(self.across, *after)
        self.across = across[0]
        self.passed = exchange(across[1], "head", 1)
        self.core = exchange(later(self.core, *after), "head", 1)
        return [across]

    def finish(self, *after):
        pieces = [self.own, self.core, self.across, self.passed]
        pieces = [later(piece, *after) for piece in pieces]
        me = lax.axis_index("head")
        return jnp.concatenate([pick(pieces, me ^ place) for place in range(4)], axis=0)


class DirectPieces(Pieces):
    def __init__(self, own, core, across, beyond):
        self.own = own
        self.core = exchange(core, "head", 1)
        self.across = exchange(across, "head", 2)
        self.passed = exchange(beyond, "head", 3)

    def come(self):
        return [self.core, self.across, self.passed]


class Sum:
    def __init__(self, sent, kept):
        self.bits = lax.axis_size("dp").bit_length() - 1
        self.lead = kept.ndim - 3
        self.tail = kept.shape[-2:]
        self.front = kept.shape[: self.lead]
        self.chosen = {}
        self.terms = [(self.split(kept), ())]
        self.coming = self.split(exchange(sent, "head", 1))

    def split(self, value):
        return value.reshape(self.front + (2,) * self.bits + self.tail)

    def total(self, wanted, after=()):
        value = None
        for term, cut in self.terms:
            term = later(term, *after)
            starts = [0] * term.ndim
            sizes = list(term.shape)
            for axis, place in wanted.items():
                if axis not in cut:
                    starts[axis], sizes[axis] = place, 1
            piece = wide(lax.dynamic_slice(term, starts, sizes))
            value = piece if value is None else value + piece
        return value

    def arrive(self):
        if self.coming is not None:
            self.terms.append((self.coming, tuple(self.chosen)))
            self.coming = None

    def halve(self, step, *after):
        self.arrive()
        low_bit = near_bit(1 << self.bits)
        if step == "y":
            axis, mine = 0, lax.axis_index("head") >> 1
        else:
            steps = {"near": (low_bit, low_bit + 1), "far": (low_bit + 1, low_bit)}
            steps = steps.get(step, (step, step))
            axis = self.lead + self.bits - 1 - steps[0]
            step = jnp.where(lax.axis_index("head") & 1 == 0, *steps)
            mine = (lax.axis_index("dp") >> step) & 1
        away = dict(self.chosen)
        away[axis] = 1 - mine
        sent = low(self.total(away, after))
        self.chosen[axis] = mine
        if axis == 0 and self.lead:
            self.coming = exchange(sent, "head", 2)
        else:
            self.coming = exchange(sent, "dp", [1 << step for step in steps])
        return sent

    def rest(self, steps, *after):
        for step in steps:
            self.halve(step, *after)
        return self.own(*after)

    def own(self, *after):
        self.arrive()
        value = low(self.total(self.chosen, after))
        return value.reshape(value.shape[: self.lead] + self.tail)


def sum_y(own, *after):
    other = exchange(own, "head", 2)
    return low(wide(later(own, *after)) + wide(other))


def join(own, bit, axis, *after):
    own = later(own, *after)
    return join_parts(own, exchange(own, "head", bit), bit, axis)


def join_parts(own, other, bit, axis):
    first = lax.axis_index("head") & bit == 0
    return jnp.concatenate(
        (jnp.where(first, own, other), jnp.where(first, other, own)), axis=axis
    )


def local(
    tokens,
    segment_labels,
    joint_projection,
    output_projection,
    first_gain,
    first_offset,
    expand_weight,
    reduce_weight,
    second_gain,
    second_offset,
    cotangent,
):
    width = tokens.shape[2]
    length = segment_labels.shape[1]
    dp_size = lax.axis_size("dp")
    bits = dp_size.bit_length() - 1
    own_width = width // dp_size
    inner = reduce_weight.shape[0]
    me = lax.axis_index("head")
    group = jnp.reshape(me, (1,))
    up_order = list(range(bits))
    slopes = jnp.asarray(head_slopes(H), dtype=jnp.float32)
    row_count = tokens.shape[0] // lax.axis_size("head")
    flat = lambda value: value.reshape(row_count * length, width)
    rowed = lambda value: value.reshape(row_count, length, width)
    piece = (row_count,) + tokens.shape[1:]

    pieces, early = [], ()
    for row in range(row_count):
        early, exchange_tokens = quarters_to_owners(tokens, row, early)
        pieces.append(exchange_tokens())
    early, exchange_cotangent = quarters_to_owners(cotangent, after=early)
    front = ()
    for row in range(row_count):
        front = attend(
            later(group, *early),
            slopes,
            segment_labels,
            tokens,
            pieces[row],
            joint_projection,
            row,
            front,
        )
    own_tokens, queries, keys, values, probs, attended = front
    cotangent_pieces = exchange_cotangent(attended)
    normal, scale, hidden, gate_part, slope_part, active, total = ahead(
        group,
        flat(own_tokens),
        flat(attended),
        output_projection,
        first_gain,
        first_offset,
        expand_weight,
        reduce_weight,
    )
    blocks = 8
    *output, back_two, back_mixed, second_gain_back, second_offset_back, sent, kept = (
        reduce_gradient(
            group,
            total,
            second_gain,
            second_offset,
            cotangent,
            cotangent_pieces,
            active,
            dp_size=dp_size,
        )
    )
    output = DirectPieces(*output)
    by_device = lambda value: (
        value.reshape(blocks, width // 2, dp_size // blocks, inner // dp_size)
        .transpose(0, 2, 1, 3)
        .reshape(dp_size, width // 2, inner // dp_size)
    )
    reduce_sum = Sum(by_device(sent), by_device(kept))
    low_bit = near_bit(dp_size)
    others = [step for step in up_order if step not in (low_bit, low_bit + 1)]
    rest = (group, back_mixed, hidden, gate_part, slope_part, reduce_weight, expand_weight)
    cut = lambda value: value.reshape(value.shape[0], dp_size, own_width, value.shape[2])
    slab = lambda value: value.reshape(dp_size, own_width, value.shape[1])
    sent, kept, back_hidden = expand_gradient(*rest, back_two, 0, True, dp_size, after=[kept])
    expand_first = Sum(cut(sent), cut(kept))
    moved = [reduce_sum.halve("near", back_hidden)]
    moved += output.come()
    sent, kept, back_hidden = expand_gradient(*rest, back_hidden, 1, False, dp_size, after=moved)
    expand_second = Sum(slab(sent), slab(kept))
    moved = [expand_first.halve("y", back_hidden)]
    moved = [reduce_sum.halve("far", *moved)]
    back_one, back_attended, branch, first_gain_back, first_offset_back = branch_back(
        group, back_hidden, normal, scale, first_gain, output_projection, after=moved
    )
    moved = [expand_second.halve("near", back_one)]
    moved = [reduce_sum.halve(others[0], *moved)]
    heads = (group, queries, keys, values, probs, attended, rowed(back_attended))
    columns = lambda value: value.reshape(3, row_count * length, value.shape[3])
    front = columns(attend_back(*heads, 0, 2, after=moved)[0])
    moved = [expand_first.halve(1, front)]
    moved = [expand_second.halve("far", *moved)]
    vectors = (first_gain_back, first_offset_back, second_gain_back, second_offset_back)
    sent, kept = joint_gradient(
        group, flat(own_tokens), flat(attended), front, branch, vectors, dp_size, after=moved
    )
    joint_first = Sum(slab(sent), slab(kept))
    reduce_own = reduce_sum.rest(others[1:], kept)
    reduce_other = exchange(reduce_own, "head", 2)
    moved = [reduce_own]
    back = columns(attend_back(*heads, 2, 1, after=moved)[0])
    moved = [joint_first.halve("near", back)]
    moved = [expand_first.halve(0, *moved)]
    sent, kept = joint_gradient_end(group, flat(own_tokens), back, dp_size, after=moved)
    joint_last = Sum(slab(sent), slab(kept))
    moved = [expand_second.halve(others[0], kept)]
    reduce_own = low(wide(later(reduce_own, *moved)) + wide(reduce_other))
    reduce_other = exchange(reduce_own, "head", 1)
    moved = [reduce_own]
    gradient = tokens_gradient_of(
        group, front, back, joint_projection, back_one, piece, after=moved
    )

    moved = [joint_last.halve("near", gradient[0])]
    moved = [joint_first.halve("far", *moved)]
    moved = [expand_first.halve(2, *moved)]
    second_own = expand_second.rest(others[1:], *moved)
    second_other = exchange(second_own, "head", 2)
    gradient = Pieces(*[later(part, second_own) for part in gradient])
    moved = [joint_last.halve("far", second_own)]
    moved = [joint_first.halve(others[0], *moved)]
    first_own = expand_first.rest(up_order[3:], *moved)
    first_other = exchange(first_own, "head", 2)
    moved = [joint_last.halve(others[0], first_own)]
    output = output.finish(*moved)
    second_own = low(wide(later(second_own, output)) + wide(second_other))
    second_other = exchange(second_own, "head", 1)
    reduce_grad = turn(later(group, second_own), reduce_own, reduce_other)
    moved = gradient.pass_on(reduce_grad)
    first_grad = join_parts(later(first_own, *moved), first_other, 2, 0)
    first_other = exchange(first_grad, "head", 1)
    joint_own = [joint_first.rest(others[1:], first_grad)]
    joint_other = [exchange(joint_own[0], "head", 2)]
    joint_own += [joint_last.rest(others[1:], *joint_own)]
    joint_other += [exchange(joint_own[1], "head", 2)]
    gradient = gradient.finish(joint_own[1])
    second_grad = join_parts(later(second_own, gradient)[None], second_other[None], 1, 0)
    first_grad = join_parts(later(first_grad, gradient)[None], first_other[None], 1, 0)
    joint_own = [
        low(wide(later(own, gradient)) + wide(other))
        for own, other in zip(joint_own, joint_other)
    ]
    expand_grad = jnp.concatenate(
        [
            piece
            for side in range(2)
            for piece in (
                first_grad[side, 0],
                first_grad[side, 1],
                second_grad[side],
            )
        ],
        axis=-1,
    )
    vectors = wide(joint_own[0][:, -128:-124])
    both = join(jnp.concatenate((joint_own[0][:, :-128], joint_own[1]), axis=1)[None], 1, 0)
    size = front.shape[2] // 2
    last = back.shape[2] // 2
    start = 3 * size + width // 2
    joint_grad = []
    for which in range(3):
        for begin, count in ((which * size, size), (start + which * last, last)):
            joint_grad += [both[side, :, begin : begin + count] for side in range(2)]
    projection_grad = [both[side, :, 3 * size : start] for side in range(2)]
    return (
        output,
        gradient,
        wide(jnp.concatenate(joint_grad, axis=-1)),
        wide(jnp.concatenate(projection_grad, axis=-1)),
        vectors[:, 0],
        vectors[:, 1],
        wide(expand_grad),
        reduce_grad,
        vectors[:, 2],
        vectors[:, 3],
    )


def solution(mesh):
    placed = (
        P("dp", "head", None),
        P("dp", None),
        P(),
        P(),
        P(),
        P(),
        P(),
        P(),
        P(),
        P(),
        P("dp", "head", None),
    )
    return jax.shard_map(
        local,
        mesh=mesh,
        in_specs=placed,
        out_specs=(
            P("dp", "head", None),
            P("dp", "head", None),
            P("dp", None),
            P("dp", None),
            P("dp"),
            P("dp"),
            P("dp", None),
            P("dp", None),
            P("dp"),
            P("dp"),
        ),
        check_vma=False,
    )
```

```python
import functools
import math

import jax
import jax.numpy as jnp
import numpy as np
from jax import lax
from jax.experimental import pallas as pl
from jax.experimental.pallas import tpu as pltpu
from jax.sharding import PartitionSpec as P

H = 12
DH = 64


EPSILON = 1e-12
NEG_FILL = -1e30
LOG2E = 1.4426950408889634
NN = (((1,), (0,)), ((), ()))
NT = (((1,), (1,)), ((), ()))
TN = (((0,), (0,)), ((), ()))
VMEM_MIB = {"attend": 56, "ahead": 56, "reduce_gradient": 56}
ANY = pl.BlockSpec(memory_space=pl.ANY)
SMEM = pl.BlockSpec(memory_space=pltpu.SMEM)


def head_slopes(heads_total):
    closest = 2 ** int(math.floor(math.log2(heads_total)))

    def power_slopes(number):
        first_slope = 2.0 ** (-8.0 / number)
        return [first_slope ** (counter + 1) for counter in range(number)]

    listed = power_slopes(closest)
    listed = listed + power_slopes(2 * closest)[0::2][: heads_total - closest]
    return np.array(listed, dtype=np.float32)


def low(value):
    return value.astype(jnp.bfloat16)


def wide(value):
    return value.astype(jnp.float32)


def dot(left, right, dims=NN):
    return lax.dot_general(left, right, dims, preferred_element_type=jnp.float32)


def shaped(shape, dtype=jnp.bfloat16):
    return jax.ShapeDtypeStruct(shape, dtype)


def whole(shape):
    return pl.BlockSpec(shape, lambda *_: (0,) * len(shape))


def later(value, *arrays):
    if not arrays:
        return value
    token = lax.optimization_barrier((lax.create_token(), *arrays))[0]
    return lax.optimization_barrier((token, value))[1]


def once(spec, operand):
    if spec.block_shape is not None and tuple(spec.block_shape) == operand.shape:
        return pl.BlockSpec(spec.block_shape, spec.index_map, pipeline_mode=pl.Buffered(1))
    return spec


def call(kernel, name, grid, in_specs, out_specs, out_shape, scratch, operands, after, into=()):
    operands = (later(operands[0], *after),) + tuple(operands[1:])
    count = len(operands) - 1
    extra = len(into)

    def run(me, *refs):
        kernel(me, *refs[:count], *refs[count + extra :])

    return pl.pallas_call(
        run,
        grid_spec=pltpu.PrefetchScalarGridSpec(
            num_scalar_prefetch=1,
            grid=grid,
            in_specs=[once(spec, operand) for spec, operand in zip(in_specs, operands[1:])]
            + [ANY] * extra,
            out_specs=list(out_specs),
            scratch_shapes=scratch,
        ),
        out_shape=list(out_shape),
        input_output_aliases={count + 1 + number: number for number in range(len(into))},
        compiler_params=pltpu.CompilerParams(
            vmem_limit_bytes=VMEM_MIB.get(name, 48) * 2**20, dimension_semantics=("arbitrary",) * len(grid)
        ),
        cost_estimate=pl.CostEstimate(flops=10**12, bytes_accessed=0, transcendentals=0),
        name=name,
    )(*operands, *into)


def near_bit(dp_size):
    return 0 if dp_size <= 8 else dp_size.bit_length() - 3


def arranged(blocks, swapped, low_bit=0):
    near, far = 1 << low_bit, 2 << low_bit
    result = []
    for number, block in enumerate(blocks):
        if bool(number & near) != bool(number & far):
            block = jnp.where(swapped, blocks[number ^ near ^ far], block)
        result.append(block)
    return result


def arranged_rows(value, swapped, dp_size):
    count = dp_size >> near_bit(dp_size)
    rows = value.shape[0] // count
    blocks = [value[number * rows : (number + 1) * rows] for number in range(count)]
    return jnp.concatenate(arranged(blocks, swapped), axis=0)


def normalize(value):
    center = value - jnp.mean(value, axis=-1, keepdims=True)
    scale = lax.rsqrt(jnp.mean(center * center, axis=-1, keepdims=True) + EPSILON)
    return center * scale, scale


def norm_back(scale, normal, back):
    return scale * (
        back
        - jnp.mean(back, axis=-1, keepdims=True)
        - normal * jnp.mean(back * normal, axis=-1, keepdims=True)
    )


def attend_kernel(
    me,
    slopes,
    labels,
    first,
    second,
    third,
    fourth,
    query_weight,
    key_weight,
    value_weight,
    tokens_out,
    queries_out,
    keys_out,
    values_out,
    probs_out,
    attended_out,
    bias,
    *,
    row,
    heads,
):
    group = pl.program_id(0)
    _, length, width = tokens_out.shape
    quarter = length // 4

    @pl.when(group == 0)
    def _():
        for step, piece in enumerate((first, second, third, fourth)):
            place = pl.multiple_of((me[0] ^ step) * quarter, quarter)
            tokens_out[0, pl.ds(place, quarter), :] = piece[0]
        label = labels[pl.ds(me[0] * 2 + row, 1), :]
        column = jnp.broadcast_to(label, (128, length)).T[:, :1]
        rows = lax.broadcasted_iota(jnp.int32, (length, length), 0)
        columns = lax.broadcasted_iota(jnp.int32, (length, length), 1)
        gap = -wide(jnp.abs(rows - columns))
        bias[...] = jnp.where(column == label, gap, NEG_FILL)

    tokens = tokens_out[0]
    queries = low(dot(tokens, query_weight[...]))
    keys = low(dot(tokens, key_weight[...]))
    values = low(dot(tokens, value_weight[...]))
    queries_out[0] = queries
    keys_out[0] = keys
    values_out[0] = values
    owner = lax.broadcasted_iota(jnp.int32, keys.shape, 1) // DH
    turned = values.T
    raw = []
    for head in range(heads):
        own_keys = jnp.where(owner == head, keys, jnp.zeros_like(keys))
        raw.append(dot(own_keys, queries, NT))
    parts = []
    for head in range(heads):
        slope = slopes[group * heads + head] * LOG2E
        scores = raw[head] * (DH**-0.5 * LOG2E) + bias[...] * slope
        exponent = jnp.exp2(scores - jnp.max(scores, axis=0, keepdims=True))
        probs = low(exponent * (1.0 / jnp.sum(exponent, axis=0, keepdims=True)))
        probs_out[0, head] = probs
        parts.append(dot(turned[head * DH : (head + 1) * DH], probs))
    attended_out[0] = low(jnp.concatenate(parts, axis=0).T)


def attend(me, slopes, labels, tokens, pieces, joint_projection, row, into=(), heads=4):
    _, quarter, width = tokens.shape
    length = labels.shape[1]
    rows = tokens.shape[0] // 4
    groups = H // heads
    group_width = heads * DH
    weight = [
        pl.BlockSpec((width, group_width), lambda g, me, which=which: (0, which * groups + g))
        for which in range(3)
    ]
    out = pl.BlockSpec((1, length, group_width), lambda g, me: (row, 0, g))
    like = shaped((rows, length, width))
    return call(
        functools.partial(attend_kernel, row=row, heads=heads),
        "attend",
        (groups,),
        [
            SMEM,
            whole(labels.shape),
            pl.BlockSpec((1, quarter, width), lambda g, me: (me[0] * rows + row, 0, 0)),
        ]
        + [whole((1, quarter, width))] * 3
        + weight,
        [pl.BlockSpec((1, length, width), lambda g, me: (row, 0, 0)), out, out, out]
        + [pl.BlockSpec((1, heads, length, length), lambda g, me: (row, g, 0, 0)), out],
        [like, like, like, like, shaped((rows, H, length, length)), like],
        [pltpu.VMEM((length, length), jnp.float32)],
        (me, slopes, labels, tokens, *pieces) + (joint_projection,) * 3,
        (),
        into,
    )


def attend_back_kernel(
    me, queries_ref, keys_ref, values_ref, probs_ref, attended, back_attended, back_joint, *, heads
):
    queries, keys, values = queries_ref[0], keys_ref[0], values_ref[0]
    back = back_attended[0]
    owner = lax.broadcasted_iota(jnp.int32, keys.shape, 1) // DH
    zero = jnp.zeros_like(keys)
    product = (wide(attended[0]) * wide(back)).T
    turned = keys.T
    probs_all, scores_all, back_all, queries_all, parts = [], [], [], [], []
    back_probs = [dot(jnp.where(owner == head, values, zero), back, NT) for head in range(heads)]
    for head in range(heads):
        mine = owner == head
        lanes = slice(head * DH, (head + 1) * DH)
        inner = jnp.sum(product[lanes], axis=0, keepdims=True)
        probs = probs_ref[0, head]
        back_scores = low(wide(probs) * (back_probs[head] - inner))
        probs_all.append(probs)
        scores_all.append(back_scores)
        back_all.append(jnp.where(mine, back, zero))
        queries_all.append(jnp.where(mine, queries, zero))
        parts.append(dot(turned[lanes], back_scores))
    scale = DH**-0.5
    back_joint[2, 0] = low(dot(jnp.concatenate(probs_all, 1), jnp.concatenate(back_all, 0)))
    back_joint[1, 0] = low(
        dot(jnp.concatenate(scores_all, 1), jnp.concatenate(queries_all, 0)) * scale
    )
    back_joint[0, 0] = low(jnp.concatenate(parts, 0).T * scale)


def attend_back(
    me, queries, keys, values, probs, attended, back_attended, base, groups, after=(), heads=4
):
    rows, length, _ = queries.shape
    group_width = heads * DH
    spec = pl.BlockSpec((1, length, group_width), lambda r, g, me: (r, 0, base + g))
    return call(
        functools.partial(attend_back_kernel, heads=heads),
        "attend_back",
        (rows, groups),
        [spec] * 3
        + [
            pl.BlockSpec((1, heads, length, length), lambda r, g, me: (r, base + g, 0, 0)),
            spec,
            spec,
        ],
        [pl.BlockSpec((3, 1, length, group_width), lambda r, g, me: (0, r, 0, g))],
        [shaped((3, rows, length, groups * group_width))],
        [],
        (me, queries, keys, values, probs, attended, back_attended),
        after,
    )


def send_piece(me, place, value, outs):
    far = (place % 4) ^ me[0]
    for number, out in enumerate(outs):

        @pl.when(far == number)
        def _():
            out[place // 4] = value


def ahead_kernel(
    me,
    tokens,
    attended,
    output_projection,
    first_gain,
    first_offset,
    gate_weight,
    up_weight,
    reduce_weight,
    normal_out,
    scale_out,
    hidden_out,
    gate_out,
    slope_out,
    active_out,
    total,
    *,
    block,
):
    step = pl.program_id(0)
    count, width = tokens.shape
    blocks = [pl.ds(start, block) for start in range(0, count, block)]

    @pl.when(step == 0)
    def _():
        for rows in blocks:
            branch = dot(attended[rows, :], output_projection[...])
            normal, scale = normalize(wide(tokens[rows, :]) + branch)
            normal_out[rows, :] = low(normal)
            scale_out[rows, :] = jnp.broadcast_to(scale, (block, scale_out.shape[1]))
            hidden = normal * first_gain[...][None] + first_offset[...][None]
            hidden_out[rows, :] = low(hidden)
            total[rows, :] = hidden

    blocks = [pl.ds(start, 2 * block) for start in range(0, count, 2 * block)]
    products = []
    for rows in blocks:
        hidden = hidden_out[rows, :]
        products.append((dot(hidden, gate_weight[...]), dot(hidden, up_weight[...])))
    for rows, (gate, up) in zip(blocks, products):
        share = 0.5 * (1.0 + lax.erf(gate * 0.5**0.5))
        density = jnp.exp(gate * gate * -0.5) * (2.0 * math.pi) ** -0.5
        unit = gate * share
        active = low(unit * up)
        gate_out[rows, :] = low(unit)
        slope_out[rows, :] = low(up * (share + gate * density))
        active_out[rows, :] = active
        total[rows, :] += dot(active, reduce_weight[...])


def ahead(
    me,
    tokens,
    attended,
    output_projection,
    first_gain,
    first_offset,
    expand_weight,
    reduce_weight,
    after=(),
    chunk=512,
    block=256,
):
    count, width = tokens.shape
    inner = reduce_weight.shape[0]
    steps = inner // chunk
    vector = whole((width,))
    rows = whole((count, width))
    column = pl.BlockSpec((count, chunk), lambda s, me: (0, s))
    return call(
        functools.partial(ahead_kernel, block=block),
        "ahead",
        (steps,),
        [
            rows,
            rows,
            whole((width, width)),
            vector,
            vector,
            pl.BlockSpec((width, chunk), lambda s, me: (0, s)),
            pl.BlockSpec((width, chunk), lambda s, me: (0, s + steps)),
            pl.BlockSpec((chunk, width), lambda s, me: (s, 0)),
        ],
        [rows, whole((count, 128)), rows, column, column, column, rows],
        [
            shaped((count, width)),
            shaped((count, 128), jnp.float32),
            shaped((count, width)),
            shaped((count, inner)),
            shaped((count, inner)),
            shaped((count, inner)),
            shaped((count, width), jnp.float32),
        ],
        [],
        (
            me,
            tokens,
            attended,
            output_projection,
            first_gain,
            first_offset,
            expand_weight,
            expand_weight,
            reduce_weight,
        ),
        after,
    )


def reduce_kernel(
    me,
    total,
    second_gain,
    second_offset,
    first,
    second,
    third,
    fourth,
    active,
    output_own,
    output_core,
    output_across,
    output_beyond,
    mixed_out,
    gain_out,
    offset_out,
    sent,
    kept,
    cotangent,
    turned,
    *,
    low_bit,
):
    half = turned.shape[0] // 2
    outputs = (output_own, output_core, output_across, output_beyond)

    @pl.when(pl.program_id(0) == 0)
    def _():
        count, width = total.shape
        quarter = first.shape[1]
        for number, piece in enumerate((first, second, third, fourth)):
            for row in range(piece.shape[0]):
                place = (row * 4 + (me[0] ^ number)) * quarter
                cotangent[pl.ds(pl.multiple_of(place, quarter), quarter), :] = piece[row]
        gain = jnp.zeros((1, width), jnp.float32)
        offset = gain
        for start in range(0, count, quarter):
            rows = pl.ds(start, quarter)
            normal, scale = normalize(total[rows, :])
            send_piece(
                me,
                start // quarter,
                low(normal * second_gain[...][None] + second_offset[...][None]),
                outputs,
            )
            back = wide(cotangent[rows, :])
            gain += jnp.sum(back * normal, axis=0, keepdims=True)
            offset += jnp.sum(back, axis=0, keepdims=True)
            two = norm_back(scale, normal, back * second_gain[...][None])
            mixed_out[rows, :] = low(two)
        gain_out[...] = gain
        offset_out[...] = offset
        turned[...] = mixed_out[...].T

    core = me[0] & 1
    for out, place in ((sent, 1 - core), (kept, core)):
        left = turned[pl.ds(pl.multiple_of(place * half, half), half), :]
        part = low(dot(left, active[...]))
        columns = out.shape[2]
        blocks = [
            part[:, number * columns : (number + 1) * columns] for number in range(out.shape[0])
        ]
        for number, block in enumerate(arranged(blocks, place == 1, low_bit)):
            out[number] = block


def reduce_gradient(
    me,
    total,
    second_gain,
    second_offset,
    cotangent,
    pieces,
    active,
    after=(),
    blocks=8,
    dp_size=8,
):
    count, width = total.shape
    columns = active.shape[1] // blocks
    together = 4 if dp_size <= blocks else blocks
    piece = pieces[0].shape
    rows = whole((count, width))
    vector = whole((1, width))
    out = pl.BlockSpec((together, width // 2, columns), lambda s, me: (s, 0, 0))
    like = shaped((blocks, width // 2, columns))
    return call(
        functools.partial(reduce_kernel, low_bit=together // 4 - 1),
        "reduce_gradient",
        (blocks // together,),
        [
            rows,
            whole((width,)),
            whole((width,)),
            pl.BlockSpec(piece, lambda s, me: (me[0], 0, 0)),
        ]
        + [whole(piece)] * 3
        + [pl.BlockSpec((count, columns * together), lambda s, me: (0, s))],
        [whole(piece)] * 4 + [rows, vector, vector, out, out],
        [shaped(piece)] * 4
        + [
            shaped((count, width)),
            shaped((1, width), jnp.float32),
            shaped((1, width), jnp.float32),
            like,
            like,
        ],
        [pltpu.VMEM((count, width), jnp.bfloat16), pltpu.VMEM((width, count), jnp.bfloat16)],
        (me, total, second_gain, second_offset, cotangent, *pieces, active),
        after,
    )


def expand_kernel(
    me,
    mixed,
    hidden,
    gate_part,
    slope_part,
    reduce_weight,
    gate_weight,
    up_weight,
    start,
    sent,
    kept,
    back,
    turned,
    *,
    dp_size,
):
    @pl.when(pl.program_id(0) == 0)
    def _():
        turned[...] = hidden[...].T
        back[...] = wide(mixed[...]) if start is None else start[...]

    weight = jnp.concatenate([gate_weight[...], up_weight[...]], 1)
    back_active = dot(mixed[...], reduce_weight[...], NT)
    both = jnp.concatenate(
        [low(back_active * wide(slope_part[...])), low(back_active * wide(gate_part[...]))], 1
    )
    back[...] += dot(both, weight, NT)
    gradient = low(dot(turned[...], both))
    chunk = gradient.shape[1] // 2
    first = me[0] & 1 == 0
    away = jnp.where(first, gradient[:, chunk:], gradient[:, :chunk])
    mine = jnp.where(first, gradient[:, :chunk], gradient[:, chunk:])
    sent[...] = arranged_rows(away, first, dp_size)
    kept[...] = arranged_rows(mine, jnp.logical_not(first), dp_size)


def without_start(kernel):
    return lambda *refs: kernel(*refs[:8], None, *refs[8:])


def expand_gradient(
    me,
    mixed,
    hidden,
    gate_part,
    slope_part,
    reduce_weight,
    expand_weight,
    start,
    part,
    dp_size,
    parts=2,
    after=(),
    chunk=768,
):
    count, width = mixed.shape
    inner = reduce_weight.shape[0]
    steps = inner // parts // chunk
    base = part * steps
    all_steps = inner // chunk
    rows = whole((count, width))
    column = pl.BlockSpec((count, chunk), lambda s, me: (0, base + s))
    out = pl.BlockSpec((width, chunk), lambda s, me: (0, s))
    like = shaped((width, steps * chunk))
    kernel = functools.partial(expand_kernel, dp_size=dp_size)
    if start is None:
        kernel = without_start(kernel)
    return call(
        kernel,
        "expand_gradient",
        (steps,),
        [
            rows,
            rows,
            column,
            column,
            pl.BlockSpec((chunk, width), lambda s, me: (base + s, 0)),
            pl.BlockSpec((width, chunk), lambda s, me: (0, base + s)),
            pl.BlockSpec((width, chunk), lambda s, me: (0, all_steps + base + s)),
        ]
        + [rows] * (start is not None),
        [out, out, rows],
        [like, like, shaped((count, width), jnp.float32)],
        [pltpu.VMEM((width, count), jnp.bfloat16)],
        (
            me,
            mixed,
            hidden,
            gate_part,
            slope_part,
            reduce_weight,
            expand_weight,
            expand_weight,
        )
        + (() if start is None else (start,)),
        after,
    )


def branch_kernel(
    me,
    back_hidden,
    normal,
    scale,
    first_gain,
    output_projection,
    back_attended,
    branch,
    gain_out,
    offset_out,
):
    back, normal = back_hidden[...], wide(normal[...])
    gain = jnp.sum(back * normal, axis=0, keepdims=True)
    offset = jnp.sum(back, axis=0, keepdims=True)
    one = norm_back(scale[:, :1], normal, back * first_gain[...][None])
    branch[...] = low(one)
    back_attended[...] = low(dot(low(one), output_projection[...], NT))

    @pl.when(pl.program_id(0) == 0)
    def _():
        gain_out[...] = gain
        offset_out[...] = offset

    @pl.when(pl.program_id(0) > 0)
    def _():
        gain_out[...] += gain
        offset_out[...] += offset


def branch_back(me, back_hidden, normal, scale, first_gain, output_projection, after=(), block=256):
    count, width = back_hidden.shape
    rows = pl.BlockSpec((block, width), lambda s, me: (s, 0))
    vector = whole((1, width))
    return call(
        branch_kernel,
        "branch_back",
        (count // block,),
        [
            rows,
            rows,
            pl.BlockSpec((block, 128), lambda s, me: (s, 0)),
            whole((width,)),
            whole((width, width)),
        ],
        [rows, rows, vector, vector],
        [
            shaped((count, width)),
            shaped((count, width)),
            shaped((1, width), jnp.float32),
            shaped((1, width), jnp.float32),
        ],
        [],
        (me, back_hidden, normal, scale, first_gain, output_projection),
        after,
    )


def halves(gradients, me, outs, dp_size):
    front, back = [], []
    for gradient in gradients:
        half = gradient.shape[1] // 2
        front.append(gradient[:, :half])
        back.append(gradient[:, half:])
    front, back = jnp.concatenate(front, axis=1), jnp.concatenate(back, axis=1)
    first = me[0] & 1 == 0
    away, mine = jnp.where(first, back, front), jnp.where(first, front, back)
    outs[0][...] = arranged_rows(away, first, dp_size)
    outs[1][...] = arranged_rows(mine, jnp.logical_not(first), dp_size)


def joint_end_kernel(me, tokens, back_joint, sent, kept, *, dp_size):
    turned = tokens[...].T
    gradients = [low(dot(turned, back_joint[which])) for which in range(3)]
    halves(gradients, me, (sent, kept), dp_size)


def joint_gradient_end(me, tokens, back_joint, dp_size, after=()):
    count, width = tokens.shape
    out = (width, 3 * back_joint.shape[2] // 2)
    return call(
        functools.partial(joint_end_kernel, dp_size=dp_size),
        "joint_gradient_end",
        (1,),
        [whole((count, width)), whole(back_joint.shape)],
        [whole(out)] * 2,
        [shaped(out)] * 2,
        [],
        (me, tokens, back_joint),
        after,
    )


def joint_kernel(
    me, tokens, attended, back_joint, branch, first, second, third, fourth, sent, kept, *, dp_size
):
    turned = tokens[...].T
    gradients = [low(dot(turned, back_joint[which])) for which in range(3)]
    gradients.append(low(dot(attended[...].T, branch[...])))
    rows = jnp.concatenate(
        [first[...], second[...], third[...], fourth[...]]
        + [jnp.zeros((124, first.shape[1]), jnp.float32)]
    )
    columns = low(rows.T)
    gradients.append(jnp.concatenate([columns, columns], axis=1))
    halves(gradients, me, (sent, kept), dp_size)


def joint_gradient(me, tokens, attended, back_joint, branch, vectors, dp_size, after=()):
    count, width = tokens.shape
    out = (width, 3 * back_joint.shape[2] // 2 + width // 2 + 128)
    rows = whole((count, width))
    return call(
        functools.partial(joint_kernel, dp_size=dp_size),
        "joint_gradient",
        (1,),
        [rows, rows, whole(back_joint.shape), rows] + [whole((1, width))] * 4,
        [whole(out)] * 2,
        [shaped(out)] * 2,
        [],
        (me, tokens, attended, back_joint, branch, *vectors),
        after,
    )


def tokens_kernel(me, front, back, weight, one, own, core, across, total):
    step = pl.program_id(0)
    part = dot(jnp.concatenate([front[0], back[0]], axis=1), weight[...], NT)

    @pl.when(step == 0)
    def _():
        total[...] = wide(one[...]) + part

    @pl.when(step == 1)
    def _():
        total[...] += part

    @pl.when(step == 2)
    def _():
        value = low(total[...] + part)
        quarter = own.shape[1]
        for place in range(value.shape[0] // quarter):
            rows = slice(place * quarter, (place + 1) * quarter)
            send_piece(me, place, value[rows], (own, core, across.at[0], across.at[1]))


def tokens_gradient_of(me, front, back, joint_projection, one, piece, after=()):
    count, width = one.shape
    rows = whole((count, width))
    return call(
        tokens_kernel,
        "tokens_gradient",
        (3,),
        [pl.BlockSpec((1, count, part.shape[2]), lambda s, me: (s, 0, 0)) for part in (front, back)]
        + [
            pl.BlockSpec((width, width), lambda s, me: (0, s)),
            rows,
        ],
        [whole(piece)] * 2 + [whole((2,) + piece)],
        [shaped(piece)] * 2 + [shaped((2,) + piece)],
        [pltpu.VMEM((count, width), jnp.float32)],
        (me, front, back, joint_projection, one),
        after,
    )


def turn_kernel(me, own, other, out):
    half = own.shape[0]
    mine, others = wide(own[...]).T, wide(other[...]).T
    first = me[0] & 1 == 0
    out[:, :half] = jnp.where(first, mine, others)
    out[:, half:] = jnp.where(first, others, mine)


def turn(me, own, other):
    half, count = own.shape
    return call(
        turn_kernel,
        "turn",
        (1,),
        [whole((half, count))] * 2,
        [whole((count, 2 * half))],
        [shaped((count, 2 * half), jnp.float32)],
        [],
        (me, own, other),
        (),
    )[0]


def exchange(value, axis, bit):
    sizes = (lax.axis_size("dp"), lax.axis_size("head"))
    pairs = []
    for dp in range(sizes[0]):
        for head in range(sizes[1]):
            if axis == "head":
                target = (dp, head ^ bit)
            else:
                target = (dp ^ bit[head & 1], head)
            pairs.append((dp * sizes[1] + head, target[0] * sizes[1] + target[1]))
    return lax.ppermute(value, ("dp", "head"), pairs)


def pick(pieces, place):
    value = pieces[0]
    for number in range(1, len(pieces)):
        value = jnp.where(place == number, pieces[number], value)
    return value


def quarters_to_owners(values, row=None, after=()):
    groups = lax.axis_size("head")
    me = lax.axis_index("head")
    own = values.shape[0] // groups
    values = later(values, *after)
    pieces = []
    for step in range(1, groups):
        start, size = (me ^ step) * own, own
        if row is not None:
            start, size = start + row, 1
        pieces.append(lax.dynamic_slice_in_dim(values, start, size, axis=0))
    return pieces, lambda *after: [
        exchange(later(pieces[step - 1], *after), "head", step) for step in range(1, groups)
    ]


class Pieces:
    def __init__(self, own, core, across):
        self.own = own
        self.core = core
        self.across = exchange(across, "head", 2)

    def pass_on(self, *after):
        across = later(self.across, *after)
        self.across = across[0]
        self.passed = exchange(across[1], "head", 1)
        self.core = exchange(later(self.core, *after), "head", 1)
        return [across]

    def finish(self, *after):
        pieces = [self.own, self.core, self.across, self.passed]
        pieces = [later(piece, *after) for piece in pieces]
        me = lax.axis_index("head")
        return jnp.concatenate([pick(pieces, me ^ place) for place in range(4)], axis=0)


class DirectPieces(Pieces):
    def __init__(self, own, core, across, beyond):
        self.own = own
        self.core = exchange(core, "head", 1)
        self.across = exchange(across, "head", 2)
        self.passed = exchange(beyond, "head", 3)

    def come(self):
        return [self.core, self.across, self.passed]


class Sum:
    def __init__(self, sent, kept):
        self.bits = lax.axis_size("dp").bit_length() - 1
        self.tail = kept.shape[-2:]
        self.chosen = {}
        self.terms = [(self.split(kept), ())]
        self.coming = self.split(exchange(sent, "head", 1))

    def split(self, value):
        return value.reshape((2,) * self.bits + self.tail)

    def total(self, wanted, after=()):
        value = None
        for term, cut in self.terms:
            term = later(term, *after)
            starts = [0] * term.ndim
            sizes = list(term.shape)
            for axis, place in wanted.items():
                if axis not in cut:
                    starts[axis], sizes[axis] = place, 1
            piece = wide(lax.dynamic_slice(term, starts, sizes))
            value = piece if value is None else value + piece
        return value

    def arrive(self):
        if self.coming is not None:
            self.terms.append((self.coming, tuple(self.chosen)))
            self.coming = None

    def halve(self, step, *after):
        self.arrive()
        low_bit = near_bit(1 << self.bits)
        steps = {"near": (low_bit, low_bit + 1), "far": (low_bit + 1, low_bit)}
        steps = steps.get(step, (step, step))
        axis = self.bits - 1 - steps[0]
        step = jnp.where(lax.axis_index("head") & 1 == 0, *steps)
        mine = (lax.axis_index("dp") >> step) & 1
        away = dict(self.chosen)
        away[axis] = 1 - mine
        sent = low(self.total(away, after))
        self.chosen[axis] = mine
        self.coming = exchange(sent, "dp", [1 << step for step in steps])
        return sent

    def rest(self, steps, *after):
        for step in steps:
            self.halve(step, *after)
        return self.own(*after)

    def own(self, *after):
        self.arrive()
        value = low(self.total(self.chosen, after))
        return value.reshape(self.tail)


def sum_y(own, *after):
    other = exchange(own, "head", 2)
    return low(wide(later(own, *after)) + wide(other))


def join(own, bit, axis, *after):
    own = later(own, *after)
    return join_parts(own, exchange(own, "head", bit), bit, axis)


def join_parts(own, other, bit, axis):
    first = lax.axis_index("head") & bit == 0
    return jnp.concatenate(
        (jnp.where(first, own, other), jnp.where(first, other, own)), axis=axis
    )


def local(
    tokens,
    segment_labels,
    joint_projection,
    output_projection,
    first_gain,
    first_offset,
    expand_weight,
    reduce_weight,
    second_gain,
    second_offset,
    cotangent,
):
    width = tokens.shape[2]
    length = segment_labels.shape[1]
    dp_size = lax.axis_size("dp")
    bits = dp_size.bit_length() - 1
    own_width = width // dp_size
    inner = reduce_weight.shape[0]
    me = lax.axis_index("head")
    group = jnp.reshape(me, (1,))
    up_order = list(range(bits))
    slopes = jnp.asarray(head_slopes(H), dtype=jnp.float32)
    row_count = tokens.shape[0] // lax.axis_size("head")
    flat = lambda value: value.reshape(row_count * length, width)
    rowed = lambda value: value.reshape(row_count, length, width)
    piece = (row_count,) + tokens.shape[1:]

    pieces, early = [], ()
    for row in range(row_count):
        early, exchange_tokens = quarters_to_owners(tokens, row, early)
        pieces.append(exchange_tokens())
    early, exchange_cotangent = quarters_to_owners(cotangent, after=early)
    front = ()
    for row in range(row_count):
        front = attend(
            later(group, *early),
            slopes,
            segment_labels,
            tokens,
            pieces[row],
            joint_projection,
            row,
            front,
        )
    own_tokens, queries, keys, values, probs, attended = front
    cotangent_pieces = exchange_cotangent(attended)
    normal, scale, hidden, gate_part, slope_part, active, total = ahead(
        group,
        flat(own_tokens),
        flat(attended),
        output_projection,
        first_gain,
        first_offset,
        expand_weight,
        reduce_weight,
    )
    blocks = 8
    *output, back_mixed, second_gain_back, second_offset_back, sent, kept = (
        reduce_gradient(
            group,
            total,
            second_gain,
            second_offset,
            cotangent,
            cotangent_pieces,
            active,
            dp_size=dp_size,
        )
    )
    output = DirectPieces(*output)
    by_device = lambda value: (
        value.reshape(blocks, width // 2, dp_size // blocks, inner // dp_size)
        .transpose(0, 2, 1, 3)
        .reshape(dp_size, width // 2, inner // dp_size)
    )
    reduce_sum = Sum(by_device(sent), by_device(kept))
    low_bit = near_bit(dp_size)
    others = [step for step in up_order if step not in (low_bit, low_bit + 1)]
    rest = (group, back_mixed, hidden, gate_part, slope_part, reduce_weight, expand_weight)
    slab = lambda value: value.reshape(dp_size, own_width, value.shape[1])
    sent, kept, back_hidden = expand_gradient(*rest, None, 0, dp_size, after=[kept])
    expand_first = Sum(slab(sent), slab(kept))
    moved = [reduce_sum.halve("near", back_hidden)]
    moved += output.come()
    sent, kept, back_hidden = expand_gradient(*rest, back_hidden, 1, dp_size, after=moved)
    expand_second = Sum(slab(sent), slab(kept))
    moved = [expand_first.halve("near", back_hidden)]
    moved = [reduce_sum.halve("far", *moved)]
    back_attended, branch, first_gain_back, first_offset_back = branch_back(
        group, back_hidden, normal, scale, first_gain, output_projection, after=moved
    )
    moved = [expand_second.halve("near", back_attended)]
    heads = (group, queries, keys, values, probs, attended, rowed(back_attended))
    columns = lambda value: value.reshape(3, row_count * length, value.shape[3])
    front = columns(attend_back(*heads, 0, 2, after=moved)[0])
    moved = [expand_first.halve("far", front)]
    moved = [reduce_sum.halve(others[0], *moved)]
    vectors = (first_gain_back, first_offset_back, second_gain_back, second_offset_back)
    sent, kept = joint_gradient(
        group, flat(own_tokens), flat(attended), front, branch, vectors, dp_size, after=moved
    )
    joint_first = Sum(slab(sent), slab(kept))
    moved = [expand_second.halve("far", kept)]
    moved = [expand_first.halve(others[0], *moved)]
    back = columns(attend_back(*heads, 2, 1, after=moved)[0])
    moved = [joint_first.halve("near", back)]
    reduce_own = reduce_sum.rest(others[1:], *moved)
    reduce_other = exchange(reduce_own, "head", 2)
    moved = [reduce_own]
    sent, kept = joint_gradient_end(group, flat(own_tokens), back, dp_size, after=moved)
    joint_last = Sum(slab(sent), slab(kept))
    moved = [expand_second.halve(others[0], kept)]
    first_own = expand_first.rest(others[1:], *moved)
    first_other = exchange(first_own, "head", 2)
    moved = [first_own]
    gradient = tokens_gradient_of(
        group, front, back, joint_projection, branch, piece, after=moved
    )

    moved = [joint_last.halve("near", gradient[0])]
    moved = [joint_first.halve("far", *moved)]
    second_own = expand_second.rest(others[1:], *moved)
    second_other = exchange(second_own, "head", 2)
    moved = [joint_last.halve("far", second_own)]
    moved = [joint_first.halve(others[0], *moved)]
    gradient = Pieces(*[later(part, *moved) for part in gradient])
    reduce_own = low(wide(later(reduce_own, *moved)) + wide(reduce_other))
    reduce_other = exchange(reduce_own, "head", 1)
    first_own = low(wide(later(first_own, reduce_own)) + wide(first_other))
    first_other = exchange(first_own, "head", 1)
    moved = [joint_last.halve(others[0], first_own)]
    second_own = low(wide(later(second_own, *moved)) + wide(second_other))
    second_other = exchange(second_own, "head", 1)
    reduce_grad = turn(later(group, second_own), reduce_own, reduce_other)
    output = output.finish(reduce_grad)
    joint_own = [joint_first.rest(others[1:], output)]
    joint_other = [exchange(joint_own[0], "head", 2)]
    joint_own += [joint_last.rest(others[1:], *joint_own)]
    joint_other += [exchange(joint_own[1], "head", 2)]
    moved = gradient.pass_on(*joint_own)
    second_grad = join_parts(later(second_own, *moved)[None], second_other[None], 1, 0)
    first_grad = join_parts(later(first_own, *moved)[None], first_other[None], 1, 0)
    expand_grad = jnp.concatenate(
        [
            piece
            for side in range(2)
            for piece in (first_grad[side], second_grad[side])
        ],
        axis=-1,
    )
    joint_own = [
        low(wide(later(own, *moved)) + wide(other))
        for own, other in zip(joint_own, joint_other)
    ]
    vectors = wide(joint_own[0][:, -128:-124])
    both = jnp.concatenate((joint_own[0][:, :-128], joint_own[1]), axis=1)
    gradient = gradient.finish(both)
    both = join_parts(both[None], exchange(both, "head", 1)[None], 1, 0)
    size = front.shape[2] // 2
    last = back.shape[2] // 2
    start = 3 * size + width // 2
    joint_grad = []
    for which in range(3):
        for begin, count in ((which * size, size), (start + which * last, last)):
            joint_grad += [both[side, :, begin : begin + count] for side in range(2)]
    projection_grad = [both[side, :, 3 * size : start] for side in range(2)]
    return (
        output,
        gradient,
        wide(jnp.concatenate(joint_grad, axis=-1)),
        wide(jnp.concatenate(projection_grad, axis=-1)),
        vectors[:, 0],
        vectors[:, 1],
        wide(expand_grad),
        reduce_grad,
        vectors[:, 2],
        vectors[:, 3],
    )


def solution(mesh):
    placed = (
        P("dp", "head", None),
        P("dp", None),
        P(),
        P(),
        P(),
        P(),
        P(),
        P(),
        P(),
        P(),
        P("dp", "head", None),
    )
    return jax.shard_map(
        local,
        mesh=mesh,
        in_specs=placed,
        out_specs=(
            P("dp", "head", None),
            P("dp", "head", None),
            P("dp", None),
            P("dp", None),
            P("dp"),
            P("dp"),
            P("dp", None),
            P("dp", None),
            P("dp"),
            P("dp"),
        ),
        check_vma=False,
    )
```

```python
import functools
import math

import jax
import jax.numpy as jnp
import numpy as np
from jax import lax
from jax.experimental import pallas as pl
from jax.experimental.pallas import tpu as pltpu
from jax.sharding import PartitionSpec as P

H = 12
DH = 64


EPSILON = 1e-12
NEG_FILL = -1e30
LOG2E = 1.4426950408889634
NN = (((1,), (0,)), ((), ()))
NT = (((1,), (1,)), ((), ()))
TN = (((0,), (0,)), ((), ()))
VMEM_MIB = {"attend": 56, "ahead": 56, "reduce_gradient": 56}
ANY = pl.BlockSpec(memory_space=pl.ANY)
SMEM = pl.BlockSpec(memory_space=pltpu.SMEM)


def head_slopes(heads_total):
    closest = 2 ** int(math.floor(math.log2(heads_total)))

    def power_slopes(number):
        first_slope = 2.0 ** (-8.0 / number)
        return [first_slope ** (counter + 1) for counter in range(number)]

    listed = power_slopes(closest)
    listed = listed + power_slopes(2 * closest)[0::2][: heads_total - closest]
    return np.array(listed, dtype=np.float32)


def low(value):
    return value.astype(jnp.bfloat16)


def wide(value):
    return value.astype(jnp.float32)


def dot(left, right, dims=NN):
    return lax.dot_general(left, right, dims, preferred_element_type=jnp.float32)


def shaped(shape, dtype=jnp.bfloat16):
    return jax.ShapeDtypeStruct(shape, dtype)


def whole(shape):
    return pl.BlockSpec(shape, lambda *_: (0,) * len(shape))


def later(value, *arrays):
    if not arrays:
        return value
    token = lax.optimization_barrier((lax.create_token(), *arrays))[0]
    return lax.optimization_barrier((token, value))[1]


def once(spec, operand):
    if spec.block_shape is not None and tuple(spec.block_shape) == operand.shape:
        return pl.BlockSpec(spec.block_shape, spec.index_map, pipeline_mode=pl.Buffered(1))
    return spec


def call(kernel, name, grid, in_specs, out_specs, out_shape, scratch, operands, after, into=()):
    operands = (later(operands[0], *after),) + tuple(operands[1:])
    count = len(operands) - 1
    extra = len(into)

    def run(me, *refs):
        kernel(me, *refs[:count], *refs[count + extra :])

    return pl.pallas_call(
        run,
        grid_spec=pltpu.PrefetchScalarGridSpec(
            num_scalar_prefetch=1,
            grid=grid,
            in_specs=[once(spec, operand) for spec, operand in zip(in_specs, operands[1:])]
            + [ANY] * extra,
            out_specs=list(out_specs),
            scratch_shapes=scratch,
        ),
        out_shape=list(out_shape),
        input_output_aliases={count + 1 + number: number for number in range(len(into))},
        compiler_params=pltpu.CompilerParams(
            vmem_limit_bytes=VMEM_MIB.get(name, 48) * 2**20, dimension_semantics=("arbitrary",) * len(grid)
        ),
        cost_estimate=pl.CostEstimate(flops=10**12, bytes_accessed=0, transcendentals=0),
        name=name,
    )(*operands, *into)


def near_bit(dp_size):
    return 0 if dp_size <= 8 else dp_size.bit_length() - 3


def arranged(blocks, swapped, low_bit=0):
    near, far = 1 << low_bit, 2 << low_bit
    result = []
    for number, block in enumerate(blocks):
        if bool(number & near) != bool(number & far):
            block = jnp.where(swapped, blocks[number ^ near ^ far], block)
        result.append(block)
    return result


def arranged_rows(value, swapped, dp_size):
    count = dp_size >> near_bit(dp_size)
    rows = value.shape[0] // count
    blocks = [value[number * rows : (number + 1) * rows] for number in range(count)]
    return jnp.concatenate(arranged(blocks, swapped), axis=0)


def normalize(value):
    center = value - jnp.mean(value, axis=-1, keepdims=True)
    scale = lax.rsqrt(jnp.mean(center * center, axis=-1, keepdims=True) + EPSILON)
    return center * scale, scale


def norm_back(scale, normal, back):
    return scale * (
        back
        - jnp.mean(back, axis=-1, keepdims=True)
        - normal * jnp.mean(back * normal, axis=-1, keepdims=True)
    )


def attend_kernel(
    me,
    slopes,
    labels,
    first,
    second,
    third,
    fourth,
    query_weight,
    key_weight,
    value_weight,
    tokens_out,
    queries_out,
    keys_out,
    values_out,
    probs_out,
    attended_out,
    bias,
    *,
    row,
    heads,
):
    group = pl.program_id(0)
    _, length, width = tokens_out.shape
    quarter = length // 4

    @pl.when(group == 0)
    def _():
        for step, piece in enumerate((first, second, third, fourth)):
            place = pl.multiple_of((me[0] ^ step) * quarter, quarter)
            tokens_out[0, pl.ds(place, quarter), :] = piece[0]
        label = labels[pl.ds(me[0] * 2 + row, 1), :]
        column = jnp.broadcast_to(label, (128, length)).T[:, :1]
        rows = lax.broadcasted_iota(jnp.int32, (length, length), 0)
        columns = lax.broadcasted_iota(jnp.int32, (length, length), 1)
        gap = -wide(jnp.abs(rows - columns))
        bias[...] = jnp.where(column == label, gap, NEG_FILL)

    tokens = tokens_out[0]
    queries = low(dot(tokens, query_weight[...]))
    keys = low(dot(tokens, key_weight[...]))
    values = low(dot(tokens, value_weight[...]))
    queries_out[0] = queries
    keys_out[0] = keys
    values_out[0] = values
    owner = lax.broadcasted_iota(jnp.int32, keys.shape, 1) // DH
    turned = values.T
    raw = []
    for head in range(heads):
        own_keys = jnp.where(owner == head, keys, jnp.zeros_like(keys))
        raw.append(dot(own_keys, queries, NT))
    parts = []
    for head in range(heads):
        slope = slopes[group * heads + head] * LOG2E
        scores = raw[head] * (DH**-0.5 * LOG2E) + bias[...] * slope
        exponent = jnp.exp2(scores - jnp.max(scores, axis=0, keepdims=True))
        probs = low(exponent * (1.0 / jnp.sum(exponent, axis=0, keepdims=True)))
        probs_out[0, head] = probs
        parts.append(dot(turned[head * DH : (head + 1) * DH], probs))
    attended_out[0] = low(jnp.concatenate(parts, axis=0).T)


def attend(me, slopes, labels, tokens, pieces, joint_projection, row, into=(), heads=4):
    _, quarter, width = tokens.shape
    length = labels.shape[1]
    rows = tokens.shape[0] // 4
    groups = H // heads
    group_width = heads * DH
    weight = [
        pl.BlockSpec((width, group_width), lambda g, me, which=which: (0, which * groups + g))
        for which in range(3)
    ]
    out = pl.BlockSpec((1, length, group_width), lambda g, me: (row, 0, g))
    like = shaped((rows, length, width))
    return call(
        functools.partial(attend_kernel, row=row, heads=heads),
        "attend",
        (groups,),
        [
            SMEM,
            whole(labels.shape),
            pl.BlockSpec((1, quarter, width), lambda g, me: (me[0] * rows + row, 0, 0)),
        ]
        + [whole((1, quarter, width))] * 3
        + weight,
        [pl.BlockSpec((1, length, width), lambda g, me: (row, 0, 0)), out, out, out]
        + [pl.BlockSpec((1, heads, length, length), lambda g, me: (row, g, 0, 0)), out],
        [like, like, like, like, shaped((rows, H, length, length)), like],
        [pltpu.VMEM((length, length), jnp.float32)],
        (me, slopes, labels, tokens, *pieces) + (joint_projection,) * 3,
        (),
        into,
    )


def attend_back_kernel(
    me, queries_ref, keys_ref, values_ref, probs_ref, attended, back_attended, back_joint, *, heads
):
    queries, keys, values = queries_ref[0], keys_ref[0], values_ref[0]
    back = back_attended[0]
    owner = lax.broadcasted_iota(jnp.int32, keys.shape, 1) // DH
    zero = jnp.zeros_like(keys)
    product = (wide(attended[0]) * wide(back)).T
    turned = keys.T
    probs_all, scores_all, back_all, queries_all, parts = [], [], [], [], []
    back_probs = [dot(jnp.where(owner == head, values, zero), back, NT) for head in range(heads)]
    for head in range(heads):
        mine = owner == head
        lanes = slice(head * DH, (head + 1) * DH)
        inner = jnp.sum(product[lanes], axis=0, keepdims=True)
        probs = probs_ref[0, head]
        back_scores = low(wide(probs) * (back_probs[head] - inner))
        probs_all.append(probs)
        scores_all.append(back_scores)
        back_all.append(jnp.where(mine, back, zero))
        queries_all.append(jnp.where(mine, queries, zero))
        parts.append(dot(turned[lanes], back_scores))
    scale = DH**-0.5
    back_joint[2, 0] = low(dot(jnp.concatenate(probs_all, 1), jnp.concatenate(back_all, 0)))
    back_joint[1, 0] = low(
        dot(jnp.concatenate(scores_all, 1), jnp.concatenate(queries_all, 0)) * scale
    )
    back_joint[0, 0] = low(jnp.concatenate(parts, 0).T * scale)


def attend_back(
    me, queries, keys, values, probs, attended, back_attended, base, groups, after=(), heads=4
):
    rows, length, _ = queries.shape
    group_width = heads * DH
    spec = pl.BlockSpec((1, length, group_width), lambda r, g, me: (r, 0, base + g))
    return call(
        functools.partial(attend_back_kernel, heads=heads),
        "attend_back",
        (rows, groups),
        [spec] * 3
        + [
            pl.BlockSpec((1, heads, length, length), lambda r, g, me: (r, base + g, 0, 0)),
            spec,
            spec,
        ],
        [pl.BlockSpec((3, 1, length, group_width), lambda r, g, me: (0, r, 0, g))],
        [shaped((3, rows, length, groups * group_width))],
        [],
        (me, queries, keys, values, probs, attended, back_attended),
        after,
    )


def send_piece(me, place, value, outs):
    far = (place % 4) ^ me[0]
    for number, out in enumerate(outs):

        @pl.when(far == number)
        def _():
            out[place // 4] = value


def ahead_kernel(
    me,
    tokens,
    attended,
    output_projection,
    first_gain,
    first_offset,
    gate_weight,
    up_weight,
    reduce_weight,
    normal_out,
    scale_out,
    hidden_out,
    gate_out,
    slope_out,
    active_out,
    total,
    *,
    block,
):
    step = pl.program_id(0)
    count, width = tokens.shape
    blocks = [pl.ds(start, block) for start in range(0, count, block)]

    @pl.when(step == 0)
    def _():
        for rows in blocks:
            branch = dot(attended[rows, :], output_projection[...])
            normal, scale = normalize(wide(tokens[rows, :]) + branch)
            normal_out[rows, :] = low(normal)
            scale_out[rows, :] = jnp.broadcast_to(scale, (block, scale_out.shape[1]))
            hidden = normal * first_gain[...][None] + first_offset[...][None]
            hidden_out[rows, :] = low(hidden)
            total[rows, :] = hidden

    blocks = [pl.ds(start, 2 * block) for start in range(0, count, 2 * block)]
    products = []
    for rows in blocks:
        hidden = hidden_out[rows, :]
        products.append((dot(hidden, gate_weight[...]), dot(hidden, up_weight[...])))
    for rows, (gate, up) in zip(blocks, products):
        share = 0.5 * (1.0 + lax.erf(gate * 0.5**0.5))
        density = jnp.exp(gate * gate * -0.5) * (2.0 * math.pi) ** -0.5
        unit = gate * share
        active = low(unit * up)
        gate_out[rows, :] = low(unit)
        slope_out[rows, :] = low(up * (share + gate * density))
        active_out[rows, :] = active
        total[rows, :] += dot(active, reduce_weight[...])


def ahead(
    me,
    tokens,
    attended,
    output_projection,
    first_gain,
    first_offset,
    expand_weight,
    reduce_weight,
    after=(),
    chunk=512,
    block=256,
):
    count, width = tokens.shape
    inner = reduce_weight.shape[0]
    steps = inner // chunk
    vector = whole((width,))
    rows = whole((count, width))
    column = pl.BlockSpec((count, chunk), lambda s, me: (0, s))
    return call(
        functools.partial(ahead_kernel, block=block),
        "ahead",
        (steps,),
        [
            rows,
            rows,
            whole((width, width)),
            vector,
            vector,
            pl.BlockSpec((width, chunk), lambda s, me: (0, s)),
            pl.BlockSpec((width, chunk), lambda s, me: (0, s + steps)),
            pl.BlockSpec((chunk, width), lambda s, me: (s, 0)),
        ],
        [rows, whole((count, 128)), rows, column, column, column, rows],
        [
            shaped((count, width)),
            shaped((count, 128), jnp.float32),
            shaped((count, width)),
            shaped((count, inner)),
            shaped((count, inner)),
            shaped((count, inner)),
            shaped((count, width), jnp.float32),
        ],
        [],
        (
            me,
            tokens,
            attended,
            output_projection,
            first_gain,
            first_offset,
            expand_weight,
            expand_weight,
            reduce_weight,
        ),
        after,
    )


def reduce_kernel(
    me,
    total,
    second_gain,
    second_offset,
    first,
    second,
    third,
    fourth,
    active,
    output_own,
    output_core,
    output_across,
    output_beyond,
    mixed_out,
    gain_out,
    offset_out,
    sent,
    kept,
    cotangent,
    turned,
    *,
    low_bit,
):
    half = turned.shape[0] // 2
    outputs = (output_own, output_core, output_across, output_beyond)

    @pl.when(pl.program_id(0) == 0)
    def _():
        count, width = total.shape
        quarter = first.shape[1]
        for number, piece in enumerate((first, second, third, fourth)):
            for row in range(piece.shape[0]):
                place = (row * 4 + (me[0] ^ number)) * quarter
                cotangent[pl.ds(pl.multiple_of(place, quarter), quarter), :] = piece[row]
        gain = jnp.zeros((1, width), jnp.float32)
        offset = gain
        for start in range(0, count, quarter):
            rows = pl.ds(start, quarter)
            normal, scale = normalize(total[rows, :])
            send_piece(
                me,
                start // quarter,
                low(normal * second_gain[...][None] + second_offset[...][None]),
                outputs,
            )
            back = wide(cotangent[rows, :])
            gain += jnp.sum(back * normal, axis=0, keepdims=True)
            offset += jnp.sum(back, axis=0, keepdims=True)
            two = norm_back(scale, normal, back * second_gain[...][None])
            mixed_out[rows, :] = low(two)
        gain_out[...] = gain
        offset_out[...] = offset
        turned[...] = mixed_out[...].T

    core = me[0] & 1
    for out, place in ((sent, 1 - core), (kept, core)):
        left = turned[pl.ds(pl.multiple_of(place * half, half), half), :]
        part = low(dot(left, active[...]))
        columns = out.shape[2]
        blocks = [
            part[:, number * columns : (number + 1) * columns] for number in range(out.shape[0])
        ]
        for number, block in enumerate(arranged(blocks, place == 1, low_bit)):
            out[number] = block


def reduce_gradient(
    me,
    total,
    second_gain,
    second_offset,
    cotangent,
    pieces,
    active,
    after=(),
    blocks=8,
    dp_size=8,
):
    count, width = total.shape
    columns = active.shape[1] // blocks
    together = 4 if dp_size <= blocks else blocks
    piece = pieces[0].shape
    rows = whole((count, width))
    vector = whole((1, width))
    out = pl.BlockSpec((together, width // 2, columns), lambda s, me: (s, 0, 0))
    like = shaped((blocks, width // 2, columns))
    return call(
        functools.partial(reduce_kernel, low_bit=together // 4 - 1),
        "reduce_gradient",
        (blocks // together,),
        [
            rows,
            whole((width,)),
            whole((width,)),
            pl.BlockSpec(piece, lambda s, me: (me[0], 0, 0)),
        ]
        + [whole(piece)] * 3
        + [pl.BlockSpec((count, columns * together), lambda s, me: (0, s))],
        [whole(piece)] * 4 + [rows, vector, vector, out, out],
        [shaped(piece)] * 4
        + [
            shaped((count, width)),
            shaped((1, width), jnp.float32),
            shaped((1, width), jnp.float32),
            like,
            like,
        ],
        [pltpu.VMEM((count, width), jnp.bfloat16), pltpu.VMEM((width, count), jnp.bfloat16)],
        (me, total, second_gain, second_offset, cotangent, *pieces, active),
        after,
    )


def expand_kernel(
    me,
    mixed,
    hidden,
    gate_part,
    slope_part,
    reduce_weight,
    gate_weight,
    up_weight,
    start,
    sent,
    kept,
    back,
    turned,
    *,
    dp_size,
):
    @pl.when(pl.program_id(0) == 0)
    def _():
        turned[...] = hidden[...].T
        back[...] = wide(mixed[...]) if start is None else start[...]

    weight = jnp.concatenate([gate_weight[...], up_weight[...]], 1)
    back_active = dot(mixed[...], reduce_weight[...], NT)
    both = jnp.concatenate(
        [low(back_active * wide(slope_part[...])), low(back_active * wide(gate_part[...]))], 1
    )
    back[...] += dot(both, weight, NT)
    gradient = low(dot(turned[...], both))
    chunk = gradient.shape[1] // 2
    first = me[0] & 1 == 0
    away = jnp.where(first, gradient[:, chunk:], gradient[:, :chunk])
    mine = jnp.where(first, gradient[:, :chunk], gradient[:, chunk:])
    sent[...] = arranged_rows(away, first, dp_size)
    kept[...] = arranged_rows(mine, jnp.logical_not(first), dp_size)


def without_start(kernel):
    return lambda *refs: kernel(*refs[:8], None, *refs[8:])


def expand_gradient(
    me,
    mixed,
    hidden,
    gate_part,
    slope_part,
    reduce_weight,
    expand_weight,
    start,
    part,
    dp_size,
    parts=2,
    after=(),
    chunk=768,
):
    count, width = mixed.shape
    inner = reduce_weight.shape[0]
    steps = inner // parts // chunk
    base = part * steps
    all_steps = inner // chunk
    rows = whole((count, width))
    column = pl.BlockSpec((count, chunk), lambda s, me: (0, base + s))
    out = pl.BlockSpec((width, chunk), lambda s, me: (0, s))
    like = shaped((width, steps * chunk))
    kernel = functools.partial(expand_kernel, dp_size=dp_size)
    if start is None:
        kernel = without_start(kernel)
    return call(
        kernel,
        "expand_gradient",
        (steps,),
        [
            rows,
            rows,
            column,
            column,
            pl.BlockSpec((chunk, width), lambda s, me: (base + s, 0)),
            pl.BlockSpec((width, chunk), lambda s, me: (0, base + s)),
            pl.BlockSpec((width, chunk), lambda s, me: (0, all_steps + base + s)),
        ]
        + [rows] * (start is not None),
        [out, out, rows],
        [like, like, shaped((count, width), jnp.float32)],
        [pltpu.VMEM((width, count), jnp.bfloat16)],
        (
            me,
            mixed,
            hidden,
            gate_part,
            slope_part,
            reduce_weight,
            expand_weight,
            expand_weight,
        )
        + (() if start is None else (start,)),
        after,
    )


def branch_kernel(
    me,
    back_hidden,
    normal,
    scale,
    first_gain,
    output_projection,
    back_attended,
    branch,
    gain_out,
    offset_out,
):
    back, normal = back_hidden[...], wide(normal[...])
    gain = jnp.sum(back * normal, axis=0, keepdims=True)
    offset = jnp.sum(back, axis=0, keepdims=True)
    one = norm_back(scale[:, :1], normal, back * first_gain[...][None])
    branch[...] = low(one)
    back_attended[...] = low(dot(low(one), output_projection[...], NT))

    @pl.when(pl.program_id(0) == 0)
    def _():
        gain_out[...] = gain
        offset_out[...] = offset

    @pl.when(pl.program_id(0) > 0)
    def _():
        gain_out[...] += gain
        offset_out[...] += offset


def branch_back(me, back_hidden, normal, scale, first_gain, output_projection, after=(), block=256):
    count, width = back_hidden.shape
    rows = pl.BlockSpec((block, width), lambda s, me: (s, 0))
    vector = whole((1, width))
    return call(
        branch_kernel,
        "branch_back",
        (count // block,),
        [
            rows,
            rows,
            pl.BlockSpec((block, 128), lambda s, me: (s, 0)),
            whole((width,)),
            whole((width, width)),
        ],
        [rows, rows, vector, vector],
        [
            shaped((count, width)),
            shaped((count, width)),
            shaped((1, width), jnp.float32),
            shaped((1, width), jnp.float32),
        ],
        [],
        (me, back_hidden, normal, scale, first_gain, output_projection),
        after,
    )


def halves(gradients, me, outs, dp_size):
    front, back = [], []
    for gradient in gradients:
        half = gradient.shape[1] // 2
        front.append(gradient[:, :half])
        back.append(gradient[:, half:])
    front, back = jnp.concatenate(front, axis=1), jnp.concatenate(back, axis=1)
    first = me[0] & 1 == 0
    away, mine = jnp.where(first, back, front), jnp.where(first, front, back)
    outs[0][...] = arranged_rows(away, first, dp_size)
    outs[1][...] = arranged_rows(mine, jnp.logical_not(first), dp_size)


def joint_end_kernel(me, tokens, back_joint, sent, kept, *, dp_size):
    turned = tokens[...].T
    gradients = [low(dot(turned, back_joint[which])) for which in range(3)]
    halves(gradients, me, (sent, kept), dp_size)


def joint_gradient_end(me, tokens, back_joint, dp_size, after=()):
    count, width = tokens.shape
    out = (width, 3 * back_joint.shape[2] // 2)
    return call(
        functools.partial(joint_end_kernel, dp_size=dp_size),
        "joint_gradient_end",
        (1,),
        [whole((count, width)), whole(back_joint.shape)],
        [whole(out)] * 2,
        [shaped(out)] * 2,
        [],
        (me, tokens, back_joint),
        after,
    )


def joint_kernel(
    me, tokens, attended, back_joint, branch, first, second, third, fourth, sent, kept, *, dp_size
):
    turned = tokens[...].T
    gradients = [low(dot(turned, back_joint[which])) for which in range(3)]
    gradients.append(low(dot(attended[...].T, branch[...])))
    rows = jnp.concatenate(
        [first[...], second[...], third[...], fourth[...]]
        + [jnp.zeros((124, first.shape[1]), jnp.float32)]
    )
    columns = low(rows.T)
    gradients.append(jnp.concatenate([columns, columns], axis=1))
    halves(gradients, me, (sent, kept), dp_size)


def joint_gradient(me, tokens, attended, back_joint, branch, vectors, dp_size, after=()):
    count, width = tokens.shape
    out = (width, 3 * back_joint.shape[2] // 2 + width // 2 + 128)
    rows = whole((count, width))
    return call(
        functools.partial(joint_kernel, dp_size=dp_size),
        "joint_gradient",
        (1,),
        [rows, rows, whole(back_joint.shape), rows] + [whole((1, width))] * 4,
        [whole(out)] * 2,
        [shaped(out)] * 2,
        [],
        (me, tokens, attended, back_joint, branch, *vectors),
        after,
    )


def tokens_kernel(me, front, back, weight, one, own, core, across, total):
    step = pl.program_id(0)
    part = dot(jnp.concatenate([front[0], back[0]], axis=1), weight[...], NT)

    @pl.when(step == 0)
    def _():
        total[...] = wide(one[...]) + part

    @pl.when(step == 1)
    def _():
        total[...] += part

    @pl.when(step == 2)
    def _():
        value = low(total[...] + part)
        quarter = own.shape[1]
        for place in range(value.shape[0] // quarter):
            rows = slice(place * quarter, (place + 1) * quarter)
            send_piece(me, place, value[rows], (own, core, across.at[0], across.at[1]))


def tokens_gradient_of(me, front, back, joint_projection, one, piece, after=()):
    count, width = one.shape
    rows = whole((count, width))
    return call(
        tokens_kernel,
        "tokens_gradient",
        (3,),
        [pl.BlockSpec((1, count, part.shape[2]), lambda s, me: (s, 0, 0)) for part in (front, back)]
        + [
            pl.BlockSpec((width, width), lambda s, me: (0, s)),
            rows,
        ],
        [whole(piece)] * 2 + [whole((2,) + piece)],
        [shaped(piece)] * 2 + [shaped((2,) + piece)],
        [pltpu.VMEM((count, width), jnp.float32)],
        (me, front, back, joint_projection, one),
        after,
    )


def turn_kernel(me, own, other, out):
    half = own.shape[0]
    mine, others = wide(own[...]).T, wide(other[...]).T
    first = me[0] & 1 == 0
    out[:, :half] = jnp.where(first, mine, others)
    out[:, half:] = jnp.where(first, others, mine)


def turn(me, own, other):
    half, count = own.shape
    return call(
        turn_kernel,
        "turn",
        (1,),
        [whole((half, count))] * 2,
        [whole((count, 2 * half))],
        [shaped((count, 2 * half), jnp.float32)],
        [],
        (me, own, other),
        (),
    )[0]


def exchange(value, axis, bit):
    sizes = (lax.axis_size("dp"), lax.axis_size("head"))
    pairs = []
    for dp in range(sizes[0]):
        for head in range(sizes[1]):
            if axis == "head":
                target = (dp, head ^ bit)
            else:
                target = (dp ^ bit[head & 1], head)
            pairs.append((dp * sizes[1] + head, target[0] * sizes[1] + target[1]))
    return lax.ppermute(value, ("dp", "head"), pairs)


def pick(pieces, place):
    value = pieces[0]
    for number in range(1, len(pieces)):
        value = jnp.where(place == number, pieces[number], value)
    return value


def quarters_to_owners(values, row=None, after=()):
    groups = lax.axis_size("head")
    me = lax.axis_index("head")
    own = values.shape[0] // groups
    values = later(values, *after)
    pieces = []
    for step in range(1, groups):
        start, size = (me ^ step) * own, own
        if row is not None:
            start, size = start + row, 1
        pieces.append(lax.dynamic_slice_in_dim(values, start, size, axis=0))
    return pieces, lambda *after: [
        exchange(later(pieces[step - 1], *after), "head", step) for step in range(1, groups)
    ]


class Pieces:
    def __init__(self, own, core, across):
        self.own = own
        self.core = core
        self.across = exchange(across, "head", 2)

    def pass_on(self, *after):
        across = later(self.across, *after)
        self.across = across[0]
        self.passed = exchange(across[1], "head", 1)
        self.core = exchange(later(self.core, *after), "head", 1)
        return [across]

    def finish(self, *after):
        pieces = [self.own, self.core, self.across, self.passed]
        pieces = [later(piece, *after) for piece in pieces]
        me = lax.axis_index("head")
        return jnp.concatenate([pick(pieces, me ^ place) for place in range(4)], axis=0)


class DirectPieces(Pieces):
    def __init__(self, own, core, across, beyond):
        self.own = own
        self.core = exchange(core, "head", 1)
        self.across = exchange(across, "head", 2)
        self.passed = exchange(beyond, "head", 3)

    def come(self):
        return [self.core, self.across, self.passed]


class Sum:
    def __init__(self, sent, kept):
        self.bits = lax.axis_size("dp").bit_length() - 1
        self.tail = kept.shape[-2:]
        self.chosen = {}
        self.terms = [(self.split(kept), ())]
        self.coming = self.split(exchange(sent, "head", 1))

    def split(self, value):
        return value.reshape((2,) * self.bits + self.tail)

    def total(self, wanted, after=()):
        value = None
        for term, cut in self.terms:
            term = later(term, *after)
            starts = [0] * term.ndim
            sizes = list(term.shape)
            for axis, place in wanted.items():
                if axis not in cut:
                    starts[axis], sizes[axis] = place, 1
            piece = wide(lax.dynamic_slice(term, starts, sizes))
            value = piece if value is None else value + piece
        return value

    def arrive(self):
        if self.coming is not None:
            self.terms.append((self.coming, tuple(self.chosen)))
            self.coming = None

    def halve(self, step, *after):
        self.arrive()
        low_bit = near_bit(1 << self.bits)
        steps = {"near": (low_bit, low_bit + 1), "far": (low_bit + 1, low_bit)}
        steps = steps.get(step, (step, step))
        axis = self.bits - 1 - steps[0]
        step = jnp.where(lax.axis_index("head") & 1 == 0, *steps)
        mine = (lax.axis_index("dp") >> step) & 1
        away = dict(self.chosen)
        away[axis] = 1 - mine
        sent = low(self.total(away, after))
        self.chosen[axis] = mine
        self.coming = exchange(sent, "dp", [1 << step for step in steps])
        return sent

    def rest(self, steps, *after):
        for step in steps:
            self.halve(step, *after)
        return self.own(*after)

    def own(self, *after):
        self.arrive()
        value = low(self.total(self.chosen, after))
        return value.reshape(self.tail)


def sum_y(own, *after):
    other = exchange(own, "head", 2)
    return low(wide(later(own, *after)) + wide(other))


def join(own, bit, axis, *after):
    own = later(own, *after)
    return join_parts(own, exchange(own, "head", bit), bit, axis)


def join_parts(own, other, bit, axis):
    first = lax.axis_index("head") & bit == 0
    return jnp.concatenate(
        (jnp.where(first, own, other), jnp.where(first, other, own)), axis=axis
    )


def local(
    tokens,
    segment_labels,
    joint_projection,
    output_projection,
    first_gain,
    first_offset,
    expand_weight,
    reduce_weight,
    second_gain,
    second_offset,
    cotangent,
):
    width = tokens.shape[2]
    length = segment_labels.shape[1]
    dp_size = lax.axis_size("dp")
    bits = dp_size.bit_length() - 1
    own_width = width // dp_size
    inner = reduce_weight.shape[0]
    me = lax.axis_index("head")
    group = jnp.reshape(me, (1,))
    up_order = list(range(bits))
    slopes = jnp.asarray(head_slopes(H), dtype=jnp.float32)
    row_count = tokens.shape[0] // lax.axis_size("head")
    flat = lambda value: value.reshape(row_count * length, width)
    rowed = lambda value: value.reshape(row_count, length, width)
    piece = (row_count,) + tokens.shape[1:]

    pieces, early = [], ()
    for row in range(row_count):
        early, exchange_tokens = quarters_to_owners(tokens, row, early)
        pieces.append(exchange_tokens())
    early, exchange_cotangent = quarters_to_owners(cotangent, after=early)
    front = ()
    for row in range(row_count):
        front = attend(
            later(group, *early),
            slopes,
            segment_labels,
            tokens,
            pieces[row],
            joint_projection,
            row,
            front,
        )
    own_tokens, queries, keys, values, probs, attended = front
    cotangent_pieces = exchange_cotangent(attended)
    normal, scale, hidden, gate_part, slope_part, active, total = ahead(
        group,
        flat(own_tokens),
        flat(attended),
        output_projection,
        first_gain,
        first_offset,
        expand_weight,
        reduce_weight,
    )
    blocks = 8
    *output, back_mixed, second_gain_back, second_offset_back, sent, kept = (
        reduce_gradient(
            group,
            total,
            second_gain,
            second_offset,
            cotangent,
            cotangent_pieces,
            active,
            dp_size=dp_size,
        )
    )
    output = DirectPieces(*output)
    by_device = lambda value: (
        value.reshape(blocks, width // 2, dp_size // blocks, inner // dp_size)
        .transpose(0, 2, 1, 3)
        .reshape(dp_size, width // 2, inner // dp_size)
    )
    reduce_sum = Sum(by_device(sent), by_device(kept))
    low_bit = near_bit(dp_size)
    others = [step for step in up_order if step not in (low_bit, low_bit + 1)]
    rest = (group, back_mixed, hidden, gate_part, slope_part, reduce_weight, expand_weight)
    slab = lambda value: value.reshape(dp_size, own_width, value.shape[1])
    sent, kept, back_hidden = expand_gradient(*rest, None, 0, dp_size, after=[kept])
    expand_first = Sum(slab(sent), slab(kept))
    moved = [reduce_sum.halve("near", back_hidden)]
    moved += output.come()
    sent, kept, back_hidden = expand_gradient(*rest, back_hidden, 1, dp_size, after=moved)
    expand_second = Sum(slab(sent), slab(kept))
    moved = [expand_first.halve("near", back_hidden)]
    moved = [reduce_sum.halve("far", *moved)]
    back_attended, branch, first_gain_back, first_offset_back = branch_back(
        group, back_hidden, normal, scale, first_gain, output_projection, after=moved
    )
    moved = [expand_second.halve("near", back_attended)]
    heads = (group, queries, keys, values, probs, attended, rowed(back_attended))
    columns = lambda value: value.reshape(3, row_count * length, value.shape[3])
    front = columns(attend_back(*heads, 0, 2, after=moved)[0])
    moved = [expand_first.halve("far", front)]
    moved = [reduce_sum.halve(others[0], *moved)]
    vectors = (first_gain_back, first_offset_back, second_gain_back, second_offset_back)
    sent, kept = joint_gradient(
        group, flat(own_tokens), flat(attended), front, branch, vectors, dp_size, after=moved
    )
    joint_first = Sum(slab(sent), slab(kept))
    moved = [expand_second.halve("far", kept)]
    moved = [expand_first.halve(others[0], *moved)]
    back = columns(attend_back(*heads, 2, 1, after=moved)[0])
    moved = [joint_first.halve("near", back)]
    reduce_own = reduce_sum.rest(others[1:], *moved)
    reduce_other = exchange(reduce_own, "head", 2)
    moved = [reduce_own]
    sent, kept = joint_gradient_end(group, flat(own_tokens), back, dp_size, after=moved)
    joint_last = Sum(slab(sent), slab(kept))
    moved = [expand_second.halve(others[0], kept)]
    first_own = expand_first.rest(others[1:], *moved)
    first_other = exchange(first_own, "head", 2)
    moved = [first_own]
    gradient = tokens_gradient_of(
        group, front, back, joint_projection, branch, piece, after=moved
    )

    moved = [joint_last.halve("near", gradient[0])]
    gradient = Pieces(*[later(part, *moved) for part in gradient])
    moved = [joint_first.halve("far", *moved)]
    second_own = expand_second.rest(others[1:], *moved)
    second_other = exchange(second_own, "head", 2)
    moved = [joint_last.halve("far", second_own)]
    moved = [joint_first.halve(others[0], *moved)]
    reduce_own = low(wide(later(reduce_own, *moved)) + wide(reduce_other))
    reduce_other = exchange(reduce_own, "head", 1)
    first_own = low(wide(later(first_own, reduce_own)) + wide(first_other))
    first_other = exchange(first_own, "head", 1)
    moved = [joint_last.halve(others[0], first_own)]
    reduce_grad = turn(later(group, *moved), reduce_own, reduce_other)
    output = output.finish(reduce_grad)
    second_own = low(wide(later(second_own, output)) + wide(second_other))
    second_other = exchange(second_own, "head", 1)
    moved = gradient.pass_on(second_own)
    joint_own = [joint_first.rest(others[1:], *moved)]
    joint_other = [exchange(joint_own[0], "head", 2)]
    joint_own += [joint_last.rest(others[1:], *joint_own)]
    joint_other += [exchange(joint_own[1], "head", 2)]
    second_grad = join_parts(later(second_own, *joint_own)[None], second_other[None], 1, 0)
    first_grad = join_parts(later(first_own, *joint_own)[None], first_other[None], 1, 0)
    expand_grad = jnp.concatenate(
        [
            piece
            for side in range(2)
            for piece in (first_grad[side], second_grad[side])
        ],
        axis=-1,
    )
    gradient = gradient.finish(*joint_own)
    joint_own = [
        low(wide(later(own, gradient)) + wide(other))
        for own, other in zip(joint_own, joint_other)
    ]
    vectors = wide(joint_own[0][:, -128:-124])
    both = jnp.concatenate((joint_own[0][:, :-128], joint_own[1]), axis=1)
    both = join_parts(both[None], exchange(both, "head", 1)[None], 1, 0)
    size = front.shape[2] // 2
    last = back.shape[2] // 2
    start = 3 * size + width // 2
    joint_grad = []
    for which in range(3):
        for begin, count in ((which * size, size), (start + which * last, last)):
            joint_grad += [both[side, :, begin : begin + count] for side in range(2)]
    projection_grad = [both[side, :, 3 * size : start] for side in range(2)]
    return (
        output,
        gradient,
        wide(jnp.concatenate(joint_grad, axis=-1)),
        wide(jnp.concatenate(projection_grad, axis=-1)),
        vectors[:, 0],
        vectors[:, 1],
        wide(expand_grad),
        reduce_grad,
        vectors[:, 2],
        vectors[:, 3],
    )


def solution(mesh):
    placed = (
        P("dp", "head", None),
        P("dp", None),
        P(),
        P(),
        P(),
        P(),
        P(),
        P(),
        P(),
        P(),
        P("dp", "head", None),
    )
    return jax.shard_map(
        local,
        mesh=mesh,
        in_specs=placed,
        out_specs=(
            P("dp", "head", None),
            P("dp", "head", None),
            P("dp", None),
            P("dp", None),
            P("dp"),
            P("dp"),
            P("dp", None),
            P("dp", None),
            P("dp"),
            P("dp"),
        ),
        check_vma=False,
    )
```

```python
import functools
import math

import jax
import jax.numpy as jnp
import numpy as np
from jax import lax
from jax.experimental import pallas as pl
from jax.experimental.pallas import tpu as pltpu
from jax.sharding import PartitionSpec as P

H = 12
DH = 64


EPSILON = 1e-12
NEG_FILL = -1e30
LOG2E = 1.4426950408889634
NN = (((1,), (0,)), ((), ()))
NT = (((1,), (1,)), ((), ()))
TN = (((0,), (0,)), ((), ()))
VMEM_MIB = {"attend": 56, "ahead": 56, "reduce_gradient": 56}
ANY = pl.BlockSpec(memory_space=pl.ANY)
SMEM = pl.BlockSpec(memory_space=pltpu.SMEM)


def head_slopes(heads_total):
    closest = 2 ** int(math.floor(math.log2(heads_total)))

    def power_slopes(number):
        first_slope = 2.0 ** (-8.0 / number)
        return [first_slope ** (counter + 1) for counter in range(number)]

    listed = power_slopes(closest)
    listed = listed + power_slopes(2 * closest)[0::2][: heads_total - closest]
    return np.array(listed, dtype=np.float32)


def low(value):
    return value.astype(jnp.bfloat16)


def wide(value):
    return value.astype(jnp.float32)


def dot(left, right, dims=NN):
    return lax.dot_general(left, right, dims, preferred_element_type=jnp.float32)


def shaped(shape, dtype=jnp.bfloat16):
    return jax.ShapeDtypeStruct(shape, dtype)


def whole(shape):
    return pl.BlockSpec(shape, lambda *_: (0,) * len(shape))


def later(value, *arrays):
    if not arrays:
        return value
    token = lax.optimization_barrier((lax.create_token(), *arrays))[0]
    return lax.optimization_barrier((token, value))[1]


def once(spec, operand):
    if spec.block_shape is not None and tuple(spec.block_shape) == operand.shape:
        return pl.BlockSpec(spec.block_shape, spec.index_map, pipeline_mode=pl.Buffered(1))
    return spec


def call(kernel, name, grid, in_specs, out_specs, out_shape, scratch, operands, after, into=()):
    operands = (later(operands[0], *after),) + tuple(operands[1:])
    count = len(operands) - 1
    extra = len(into)

    def run(me, *refs):
        kernel(me, *refs[:count], *refs[count + extra :])

    return pl.pallas_call(
        run,
        grid_spec=pltpu.PrefetchScalarGridSpec(
            num_scalar_prefetch=1,
            grid=grid,
            in_specs=[once(spec, operand) for spec, operand in zip(in_specs, operands[1:])]
            + [ANY] * extra,
            out_specs=list(out_specs),
            scratch_shapes=scratch,
        ),
        out_shape=list(out_shape),
        input_output_aliases={count + 1 + number: number for number in range(len(into))},
        compiler_params=pltpu.CompilerParams(
            vmem_limit_bytes=VMEM_MIB.get(name, 48) * 2**20, dimension_semantics=("arbitrary",) * len(grid)
        ),
        cost_estimate=pl.CostEstimate(flops=10**12, bytes_accessed=0, transcendentals=0),
        name=name,
    )(*operands, *into)


def near_bit(dp_size):
    return 0 if dp_size <= 8 else dp_size.bit_length() - 3


def arranged(blocks, swapped, low_bit=0):
    near, far = 1 << low_bit, 2 << low_bit
    result = []
    for number, block in enumerate(blocks):
        if bool(number & near) != bool(number & far):
            block = jnp.where(swapped, blocks[number ^ near ^ far], block)
        result.append(block)
    return result


def arranged_rows(value, swapped, dp_size):
    count = dp_size >> near_bit(dp_size)
    rows = value.shape[0] // count
    blocks = [value[number * rows : (number + 1) * rows] for number in range(count)]
    return jnp.concatenate(arranged(blocks, swapped), axis=0)


def normalize(value):
    center = value - jnp.mean(value, axis=-1, keepdims=True)
    scale = lax.rsqrt(jnp.mean(center * center, axis=-1, keepdims=True) + EPSILON)
    return center * scale, scale


def norm_back(scale, normal, back):
    return scale * (
        back
        - jnp.mean(back, axis=-1, keepdims=True)
        - normal * jnp.mean(back * normal, axis=-1, keepdims=True)
    )


def attend_kernel(
    me,
    slopes,
    labels,
    first,
    second,
    third,
    fourth,
    query_weight,
    key_weight,
    value_weight,
    tokens_out,
    queries_out,
    keys_out,
    values_out,
    probs_out,
    attended_out,
    bias,
    *,
    row,
    heads,
):
    group = pl.program_id(0)
    _, length, width = tokens_out.shape
    quarter = length // 4

    @pl.when(group == 0)
    def _():
        for step, piece in enumerate((first, second, third, fourth)):
            place = pl.multiple_of((me[0] ^ step) * quarter, quarter)
            tokens_out[0, pl.ds(place, quarter), :] = piece[0]
        label = labels[pl.ds(me[0] * 2 + row, 1), :]
        column = jnp.broadcast_to(label, (128, length)).T[:, :1]
        rows = lax.broadcasted_iota(jnp.int32, (length, length), 0)
        columns = lax.broadcasted_iota(jnp.int32, (length, length), 1)
        gap = -wide(jnp.abs(rows - columns))
        bias[...] = jnp.where(column == label, gap, NEG_FILL)

    tokens = tokens_out[0]
    queries = low(dot(tokens, query_weight[...]))
    keys = low(dot(tokens, key_weight[...]))
    values = low(dot(tokens, value_weight[...]))
    queries_out[0] = queries
    keys_out[0] = keys
    values_out[0] = values
    owner = lax.broadcasted_iota(jnp.int32, keys.shape, 1) // DH
    turned = values.T
    raw = []
    for head in range(heads):
        own_keys = jnp.where(owner == head, keys, jnp.zeros_like(keys))
        raw.append(dot(own_keys, queries, NT))
    parts = []
    for head in range(heads):
        slope = slopes[group * heads + head] * LOG2E
        scores = raw[head] * (DH**-0.5 * LOG2E) + bias[...] * slope
        exponent = jnp.exp2(scores - jnp.max(scores, axis=0, keepdims=True))
        probs = low(exponent * (1.0 / jnp.sum(exponent, axis=0, keepdims=True)))
        probs_out[0, head] = probs
        parts.append(dot(turned[head * DH : (head + 1) * DH], probs))
    attended_out[0] = low(jnp.concatenate(parts, axis=0).T)


def attend(me, slopes, labels, tokens, pieces, joint_projection, row, into=(), heads=4):
    _, quarter, width = tokens.shape
    length = labels.shape[1]
    rows = tokens.shape[0] // 4
    groups = H // heads
    group_width = heads * DH
    weight = [
        pl.BlockSpec((width, group_width), lambda g, me, which=which: (0, which * groups + g))
        for which in range(3)
    ]
    out = pl.BlockSpec((1, length, group_width), lambda g, me: (row, 0, g))
    like = shaped((rows, length, width))
    return call(
        functools.partial(attend_kernel, row=row, heads=heads),
        "attend",
        (groups,),
        [
            SMEM,
            whole(labels.shape),
            pl.BlockSpec((1, quarter, width), lambda g, me: (me[0] * rows + row, 0, 0)),
        ]
        + [whole((1, quarter, width))] * 3
        + weight,
        [pl.BlockSpec((1, length, width), lambda g, me: (row, 0, 0)), out, out, out]
        + [pl.BlockSpec((1, heads, length, length), lambda g, me: (row, g, 0, 0)), out],
        [like, like, like, like, shaped((rows, H, length, length)), like],
        [pltpu.VMEM((length, length), jnp.float32)],
        (me, slopes, labels, tokens, *pieces) + (joint_projection,) * 3,
        (),
        into,
    )


def attend_back_kernel(
    me, queries_ref, keys_ref, values_ref, probs_ref, attended, back_attended, back_joint, *, heads
):
    queries, keys, values = queries_ref[0], keys_ref[0], values_ref[0]
    back = back_attended[0]
    owner = lax.broadcasted_iota(jnp.int32, keys.shape, 1) // DH
    zero = jnp.zeros_like(keys)
    product = (wide(attended[0]) * wide(back)).T
    turned = keys.T
    probs_all, scores_all, back_all, queries_all, parts = [], [], [], [], []
    back_probs = [dot(jnp.where(owner == head, values, zero), back, NT) for head in range(heads)]
    for head in range(heads):
        mine = owner == head
        lanes = slice(head * DH, (head + 1) * DH)
        inner = jnp.sum(product[lanes], axis=0, keepdims=True)
        probs = probs_ref[0, head]
        back_scores = low(wide(probs) * (back_probs[head] - inner))
        probs_all.append(probs)
        scores_all.append(back_scores)
        back_all.append(jnp.where(mine, back, zero))
        queries_all.append(jnp.where(mine, queries, zero))
        parts.append(dot(turned[lanes], back_scores))
    scale = DH**-0.5
    back_joint[2, 0] = low(dot(jnp.concatenate(probs_all, 1), jnp.concatenate(back_all, 0)))
    back_joint[1, 0] = low(
        dot(jnp.concatenate(scores_all, 1), jnp.concatenate(queries_all, 0)) * scale
    )
    back_joint[0, 0] = low(jnp.concatenate(parts, 0).T * scale)


def attend_back(
    me, queries, keys, values, probs, attended, back_attended, base, groups, after=(), heads=4
):
    rows, length, _ = queries.shape
    group_width = heads * DH
    spec = pl.BlockSpec((1, length, group_width), lambda r, g, me: (r, 0, base + g))
    return call(
        functools.partial(attend_back_kernel, heads=heads),
        "attend_back",
        (rows, groups),
        [spec] * 3
        + [
            pl.BlockSpec((1, heads, length, length), lambda r, g, me: (r, base + g, 0, 0)),
            spec,
            spec,
        ],
        [pl.BlockSpec((3, 1, length, group_width), lambda r, g, me: (0, r, 0, g))],
        [shaped((3, rows, length, groups * group_width))],
        [],
        (me, queries, keys, values, probs, attended, back_attended),
        after,
    )


def send_piece(me, place, value, outs):
    far = (place % 4) ^ me[0]
    for number, out in enumerate(outs):

        @pl.when(far == number)
        def _():
            out[place // 4] = value


def ahead_kernel(
    me,
    tokens,
    attended,
    output_projection,
    first_gain,
    first_offset,
    gate_weight,
    up_weight,
    reduce_weight,
    normal_out,
    scale_out,
    hidden_out,
    gate_out,
    slope_out,
    active_out,
    total,
    *,
    block,
):
    step = pl.program_id(0)
    count, width = tokens.shape
    blocks = [pl.ds(start, block) for start in range(0, count, block)]

    @pl.when(step == 0)
    def _():
        for rows in blocks:
            branch = dot(attended[rows, :], output_projection[...])
            normal, scale = normalize(wide(tokens[rows, :]) + branch)
            normal_out[rows, :] = low(normal)
            scale_out[rows, :] = jnp.broadcast_to(scale, (block, scale_out.shape[1]))
            hidden = normal * first_gain[...][None] + first_offset[...][None]
            hidden_out[rows, :] = low(hidden)
            total[rows, :] = hidden

    blocks = [pl.ds(start, 2 * block) for start in range(0, count, 2 * block)]
    products = []
    for rows in blocks:
        hidden = hidden_out[rows, :]
        products.append((dot(hidden, gate_weight[...]), dot(hidden, up_weight[...])))
    for rows, (gate, up) in zip(blocks, products):
        share = 0.5 * (1.0 + lax.erf(gate * 0.5**0.5))
        density = jnp.exp(gate * gate * -0.5) * (2.0 * math.pi) ** -0.5
        unit = gate * share
        active = low(unit * up)
        gate_out[rows, :] = low(unit)
        slope_out[rows, :] = low(up * (share + gate * density))
        active_out[rows, :] = active
        total[rows, :] += dot(active, reduce_weight[...])


def ahead(
    me,
    tokens,
    attended,
    output_projection,
    first_gain,
    first_offset,
    expand_weight,
    reduce_weight,
    after=(),
    chunk=512,
    block=256,
):
    count, width = tokens.shape
    inner = reduce_weight.shape[0]
    steps = inner // chunk
    vector = whole((width,))
    rows = whole((count, width))
    column = pl.BlockSpec((count, chunk), lambda s, me: (0, s))
    return call(
        functools.partial(ahead_kernel, block=block),
        "ahead",
        (steps,),
        [
            rows,
            rows,
            whole((width, width)),
            vector,
            vector,
            pl.BlockSpec((width, chunk), lambda s, me: (0, s)),
            pl.BlockSpec((width, chunk), lambda s, me: (0, s + steps)),
            pl.BlockSpec((chunk, width), lambda s, me: (s, 0)),
        ],
        [rows, whole((count, 128)), rows, column, column, column, rows],
        [
            shaped((count, width)),
            shaped((count, 128), jnp.float32),
            shaped((count, width)),
            shaped((count, inner)),
            shaped((count, inner)),
            shaped((count, inner)),
            shaped((count, width), jnp.float32),
        ],
        [],
        (
            me,
            tokens,
            attended,
            output_projection,
            first_gain,
            first_offset,
            expand_weight,
            expand_weight,
            reduce_weight,
        ),
        after,
    )


def reduce_kernel(
    me,
    total,
    second_gain,
    second_offset,
    first,
    second,
    third,
    fourth,
    active,
    output_own,
    output_core,
    output_across,
    output_beyond,
    mixed_out,
    gain_out,
    offset_out,
    sent,
    kept,
    cotangent,
    turned,
    *,
    low_bit,
):
    half = turned.shape[0] // 2
    outputs = (output_own, output_core, output_across, output_beyond)

    @pl.when(pl.program_id(0) == 0)
    def _():
        count, width = total.shape
        quarter = first.shape[1]
        for number, piece in enumerate((first, second, third, fourth)):
            for row in range(piece.shape[0]):
                place = (row * 4 + (me[0] ^ number)) * quarter
                cotangent[pl.ds(pl.multiple_of(place, quarter), quarter), :] = piece[row]
        gain = jnp.zeros((1, width), jnp.float32)
        offset = gain
        for start in range(0, count, quarter):
            rows = pl.ds(start, quarter)
            normal, scale = normalize(total[rows, :])
            send_piece(
                me,
                start // quarter,
                low(normal * second_gain[...][None] + second_offset[...][None]),
                outputs,
            )
            back = wide(cotangent[rows, :])
            gain += jnp.sum(back * normal, axis=0, keepdims=True)
            offset += jnp.sum(back, axis=0, keepdims=True)
            two = norm_back(scale, normal, back * second_gain[...][None])
            mixed_out[rows, :] = low(two)
        gain_out[...] = gain
        offset_out[...] = offset
        turned[...] = mixed_out[...].T

    core = me[0] & 1
    for out, place in ((sent, 1 - core), (kept, core)):
        left = turned[pl.ds(pl.multiple_of(place * half, half), half), :]
        part = low(dot(left, active[...]))
        columns = out.shape[2]
        blocks = [
            part[:, number * columns : (number + 1) * columns] for number in range(out.shape[0])
        ]
        for number, block in enumerate(arranged(blocks, place == 1, low_bit)):
            out[number] = block


def reduce_gradient(
    me,
    total,
    second_gain,
    second_offset,
    cotangent,
    pieces,
    active,
    after=(),
    blocks=8,
    dp_size=8,
):
    count, width = total.shape
    columns = active.shape[1] // blocks
    together = 4 if dp_size <= blocks else blocks
    piece = pieces[0].shape
    rows = whole((count, width))
    vector = whole((1, width))
    out = pl.BlockSpec((together, width // 2, columns), lambda s, me: (s, 0, 0))
    like = shaped((blocks, width // 2, columns))
    return call(
        functools.partial(reduce_kernel, low_bit=together // 4 - 1),
        "reduce_gradient",
        (blocks // together,),
        [
            rows,
            whole((width,)),
            whole((width,)),
            pl.BlockSpec(piece, lambda s, me: (me[0], 0, 0)),
        ]
        + [whole(piece)] * 3
        + [pl.BlockSpec((count, columns * together), lambda s, me: (0, s))],
        [whole(piece)] * 4 + [rows, vector, vector, out, out],
        [shaped(piece)] * 4
        + [
            shaped((count, width)),
            shaped((1, width), jnp.float32),
            shaped((1, width), jnp.float32),
            like,
            like,
        ],
        [pltpu.VMEM((count, width), jnp.bfloat16), pltpu.VMEM((width, count), jnp.bfloat16)],
        (me, total, second_gain, second_offset, cotangent, *pieces, active),
        after,
    )


def expand_kernel(
    me,
    mixed,
    hidden,
    gate_part,
    slope_part,
    reduce_weight,
    gate_weight,
    up_weight,
    start,
    sent,
    kept,
    back,
    turned,
    *,
    dp_size,
):
    @pl.when(pl.program_id(0) == 0)
    def _():
        turned[...] = hidden[...].T
        back[...] = (mixed if start is None else start)[...].astype(back.dtype)

    weight = jnp.concatenate([gate_weight[...], up_weight[...]], 1)
    back_active = dot(mixed[...], reduce_weight[...], NT)
    both = jnp.concatenate(
        [low(back_active * wide(slope_part[...])), low(back_active * wide(gate_part[...]))], 1
    )
    back[...] = (wide(back[...]) + dot(both, weight, NT)).astype(back.dtype)
    gradient = low(dot(turned[...], both))
    chunk = gradient.shape[1] // 2
    first = me[0] & 1 == 0
    away = jnp.where(first, gradient[:, chunk:], gradient[:, :chunk])
    mine = jnp.where(first, gradient[:, :chunk], gradient[:, chunk:])
    sent[...] = arranged_rows(away, first, dp_size)
    kept[...] = arranged_rows(mine, jnp.logical_not(first), dp_size)


def without_start(kernel):
    return lambda *refs: kernel(*refs[:8], None, *refs[8:])


def expand_gradient(
    me,
    mixed,
    hidden,
    gate_part,
    slope_part,
    reduce_weight,
    expand_weight,
    start,
    part,
    dp_size,
    parts=2,
    after=(),
    chunk=768,
):
    count, width = mixed.shape
    inner = reduce_weight.shape[0]
    steps = inner // parts // chunk
    base = part * steps
    all_steps = inner // chunk
    rows = whole((count, width))
    column = pl.BlockSpec((count, chunk), lambda s, me: (0, base + s))
    out = pl.BlockSpec((width, chunk), lambda s, me: (0, s))
    like = shaped((width, steps * chunk))
    kernel = functools.partial(expand_kernel, dp_size=dp_size)
    if start is None:
        kernel = without_start(kernel)
    return call(
        kernel,
        "expand_gradient",
        (steps,),
        [
            rows,
            rows,
            column,
            column,
            pl.BlockSpec((chunk, width), lambda s, me: (base + s, 0)),
            pl.BlockSpec((width, chunk), lambda s, me: (0, base + s)),
            pl.BlockSpec((width, chunk), lambda s, me: (0, all_steps + base + s)),
        ]
        + [rows] * (start is not None),
        [out, out, rows],
        [like, like, shaped((count, width), jnp.bfloat16 if start is None else jnp.float32)],
        [pltpu.VMEM((width, count), jnp.bfloat16)],
        (
            me,
            mixed,
            hidden,
            gate_part,
            slope_part,
            reduce_weight,
            expand_weight,
            expand_weight,
        )
        + (() if start is None else (start,)),
        after,
    )


def branch_kernel(
    me,
    back_hidden,
    normal,
    scale,
    first_gain,
    output_projection,
    back_attended,
    branch,
    gain_out,
    offset_out,
):
    back, normal = back_hidden[...], wide(normal[...])
    gain = jnp.sum(back * normal, axis=0, keepdims=True)
    offset = jnp.sum(back, axis=0, keepdims=True)
    one = norm_back(scale[:, :1], normal, back * first_gain[...][None])
    branch[...] = low(one)
    back_attended[...] = low(dot(low(one), output_projection[...], NT))

    @pl.when(pl.program_id(0) == 0)
    def _():
        gain_out[...] = gain
        offset_out[...] = offset

    @pl.when(pl.program_id(0) > 0)
    def _():
        gain_out[...] += gain
        offset_out[...] += offset


def branch_back(me, back_hidden, normal, scale, first_gain, output_projection, after=(), block=256):
    count, width = back_hidden.shape
    rows = pl.BlockSpec((block, width), lambda s, me: (s, 0))
    vector = whole((1, width))
    return call(
        branch_kernel,
        "branch_back",
        (count // block,),
        [
            rows,
            rows,
            pl.BlockSpec((block, 128), lambda s, me: (s, 0)),
            whole((width,)),
            whole((width, width)),
        ],
        [rows, rows, vector, vector],
        [
            shaped((count, width)),
            shaped((count, width)),
            shaped((1, width), jnp.float32),
            shaped((1, width), jnp.float32),
        ],
        [],
        (me, back_hidden, normal, scale, first_gain, output_projection),
        after,
    )


def halves(gradients, me, outs, dp_size):
    front, back = [], []
    for gradient in gradients:
        half = gradient.shape[1] // 2
        front.append(gradient[:, :half])
        back.append(gradient[:, half:])
    front, back = jnp.concatenate(front, axis=1), jnp.concatenate(back, axis=1)
    first = me[0] & 1 == 0
    away, mine = jnp.where(first, back, front), jnp.where(first, front, back)
    outs[0][...] = arranged_rows(away, first, dp_size)
    outs[1][...] = arranged_rows(mine, jnp.logical_not(first), dp_size)


def joint_end_kernel(me, tokens, back_joint, sent, kept, *, dp_size):
    turned = tokens[...].T
    gradients = [low(dot(turned, back_joint[which])) for which in range(3)]
    halves(gradients, me, (sent, kept), dp_size)


def joint_gradient_end(me, tokens, back_joint, dp_size, after=()):
    count, width = tokens.shape
    out = (width, 3 * back_joint.shape[2] // 2)
    return call(
        functools.partial(joint_end_kernel, dp_size=dp_size),
        "joint_gradient_end",
        (1,),
        [whole((count, width)), whole(back_joint.shape)],
        [whole(out)] * 2,
        [shaped(out)] * 2,
        [],
        (me, tokens, back_joint),
        after,
    )


def joint_kernel(
    me, tokens, attended, back_joint, branch, first, second, third, fourth, sent, kept, *, dp_size
):
    turned = tokens[...].T
    gradients = [low(dot(turned, back_joint[which])) for which in range(3)]
    gradients.append(low(dot(attended[...].T, branch[...])))
    rows = jnp.concatenate(
        [first[...], second[...], third[...], fourth[...]]
        + [jnp.zeros((124, first.shape[1]), jnp.float32)]
    )
    columns = low(rows.T)
    gradients.append(jnp.concatenate([columns, columns], axis=1))
    halves(gradients, me, (sent, kept), dp_size)


def joint_gradient(me, tokens, attended, back_joint, branch, vectors, dp_size, after=()):
    count, width = tokens.shape
    out = (width, 3 * back_joint.shape[2] // 2 + width // 2 + 128)
    rows = whole((count, width))
    return call(
        functools.partial(joint_kernel, dp_size=dp_size),
        "joint_gradient",
        (1,),
        [rows, rows, whole(back_joint.shape), rows] + [whole((1, width))] * 4,
        [whole(out)] * 2,
        [shaped(out)] * 2,
        [],
        (me, tokens, attended, back_joint, branch, *vectors),
        after,
    )


def tokens_kernel(me, front, back, weight, one, own, core, across, total):
    step = pl.program_id(0)
    part = dot(jnp.concatenate([front[0], back[0]], axis=1), weight[...], NT)

    @pl.when(step == 0)
    def _():
        total[...] = wide(one[...]) + part

    @pl.when(step == 1)
    def _():
        total[...] += part

    @pl.when(step == 2)
    def _():
        value = low(total[...] + part)
        quarter = own.shape[1]
        for place in range(value.shape[0] // quarter):
            rows = slice(place * quarter, (place + 1) * quarter)
            send_piece(me, place, value[rows], (own, core, across.at[0], across.at[1]))


def tokens_gradient_of(me, front, back, joint_projection, one, piece, after=()):
    count, width = one.shape
    rows = whole((count, width))
    return call(
        tokens_kernel,
        "tokens_gradient",
        (3,),
        [pl.BlockSpec((1, count, part.shape[2]), lambda s, me: (s, 0, 0)) for part in (front, back)]
        + [
            pl.BlockSpec((width, width), lambda s, me: (0, s)),
            rows,
        ],
        [whole(piece)] * 2 + [whole((2,) + piece)],
        [shaped(piece)] * 2 + [shaped((2,) + piece)],
        [pltpu.VMEM((count, width), jnp.float32)],
        (me, front, back, joint_projection, one),
        after,
    )


def turn_kernel(me, own, other, out):
    half = own.shape[0]
    mine, others = wide(own[...]).T, wide(other[...]).T
    first = me[0] & 1 == 0
    out[:, :half] = jnp.where(first, mine, others)
    out[:, half:] = jnp.where(first, others, mine)


def turn(me, own, other):
    half, count = own.shape
    return call(
        turn_kernel,
        "turn",
        (1,),
        [whole((half, count))] * 2,
        [whole((count, 2 * half))],
        [shaped((count, 2 * half), jnp.float32)],
        [],
        (me, own, other),
        (),
    )[0]


def exchange(value, axis, bit):
    sizes = (lax.axis_size("dp"), lax.axis_size("head"))
    pairs = []
    for dp in range(sizes[0]):
        for head in range(sizes[1]):
            if axis == "head":
                target = (dp, head ^ bit)
            else:
                target = (dp ^ bit[head & 1], head)
            pairs.append((dp * sizes[1] + head, target[0] * sizes[1] + target[1]))
    return lax.ppermute(value, ("dp", "head"), pairs)


def pick(pieces, place):
    value = pieces[0]
    for number in range(1, len(pieces)):
        value = jnp.where(place == number, pieces[number], value)
    return value


def quarters_to_owners(values, row=None, after=()):
    groups = lax.axis_size("head")
    me = lax.axis_index("head")
    own = values.shape[0] // groups
    values = later(values, *after)
    pieces = []
    for step in range(1, groups):
        start, size = (me ^ step) * own, own
        if row is not None:
            start, size = start + row, 1
        pieces.append(lax.dynamic_slice_in_dim(values, start, size, axis=0))
    return pieces, lambda *after: [
        exchange(later(pieces[step - 1], *after), "head", step) for step in range(1, groups)
    ]


class Pieces:
    def __init__(self, own, core, across):
        self.own = own
        self.core = core
        self.across = exchange(across, "head", 2)

    def pass_on(self, *after):
        across = later(self.across, *after)
        self.across = across[0]
        self.passed = exchange(across[1], "head", 1)
        self.core = exchange(later(self.core, *after), "head", 1)
        return [across]

    def finish(self, *after):
        pieces = [self.own, self.core, self.across, self.passed]
        pieces = [later(piece, *after) for piece in pieces]
        me = lax.axis_index("head")
        return jnp.concatenate([pick(pieces, me ^ place) for place in range(4)], axis=0)


class DirectPieces(Pieces):
    def __init__(self, own, core, across, beyond):
        self.own = own
        self.core = exchange(core, "head", 1)
        self.across = exchange(across, "head", 2)
        self.passed = exchange(beyond, "head", 3)

    def come(self):
        return [self.core, self.across, self.passed]


class Sum:
    def __init__(self, sent, kept):
        self.bits = lax.axis_size("dp").bit_length() - 1
        self.tail = kept.shape[-2:]
        self.chosen = {}
        self.terms = [(self.split(kept), ())]
        self.coming = self.split(exchange(sent, "head", 1))

    def split(self, value):
        return value.reshape((2,) * self.bits + self.tail)

    def total(self, wanted, after=()):
        value = None
        for term, cut in self.terms:
            term = later(term, *after)
            starts = [0] * term.ndim
            sizes = list(term.shape)
            for axis, place in wanted.items():
                if axis not in cut:
                    starts[axis], sizes[axis] = place, 1
            piece = wide(lax.dynamic_slice(term, starts, sizes))
            value = piece if value is None else value + piece
        return value

    def arrive(self):
        if self.coming is not None:
            self.terms.append((self.coming, tuple(self.chosen)))
            self.coming = None

    def halve(self, step, *after):
        self.arrive()
        low_bit = near_bit(1 << self.bits)
        steps = {"near": (low_bit, low_bit + 1), "far": (low_bit + 1, low_bit)}
        steps = steps.get(step, (step, step))
        axis = self.bits - 1 - steps[0]
        step = jnp.where(lax.axis_index("head") & 1 == 0, *steps)
        mine = (lax.axis_index("dp") >> step) & 1
        away = dict(self.chosen)
        away[axis] = 1 - mine
        sent = low(self.total(away, after))
        self.chosen[axis] = mine
        self.coming = exchange(sent, "dp", [1 << step for step in steps])
        return sent

    def rest(self, steps, *after):
        for step in steps:
            self.halve(step, *after)
        return self.own(*after)

    def own(self, *after):
        self.arrive()
        value = low(self.total(self.chosen, after))
        return value.reshape(self.tail)


def sum_y(own, *after):
    other = exchange(own, "head", 2)
    return low(wide(later(own, *after)) + wide(other))


def join(own, bit, axis, *after):
    own = later(own, *after)
    return join_parts(own, exchange(own, "head", bit), bit, axis)


def join_parts(own, other, bit, axis):
    first = lax.axis_index("head") & bit == 0
    return jnp.concatenate(
        (jnp.where(first, own, other), jnp.where(first, other, own)), axis=axis
    )


def local(
    tokens,
    segment_labels,
    joint_projection,
    output_projection,
    first_gain,
    first_offset,
    expand_weight,
    reduce_weight,
    second_gain,
    second_offset,
    cotangent,
):
    width = tokens.shape[2]
    length = segment_labels.shape[1]
    dp_size = lax.axis_size("dp")
    bits = dp_size.bit_length() - 1
    own_width = width // dp_size
    inner = reduce_weight.shape[0]
    me = lax.axis_index("head")
    group = jnp.reshape(me, (1,))
    up_order = list(range(bits))
    slopes = jnp.asarray(head_slopes(H), dtype=jnp.float32)
    row_count = tokens.shape[0] // lax.axis_size("head")
    flat = lambda value: value.reshape(row_count * length, width)
    rowed = lambda value: value.reshape(row_count, length, width)
    piece = (row_count,) + tokens.shape[1:]

    pieces, early = [], ()
    for row in range(row_count):
        early, exchange_tokens = quarters_to_owners(tokens, row, early)
        pieces.append(exchange_tokens())
    early, exchange_cotangent = quarters_to_owners(cotangent, after=early)
    front = ()
    for row in range(row_count):
        front = attend(
            later(group, *early),
            slopes,
            segment_labels,
            tokens,
            pieces[row],
            joint_projection,
            row,
            front,
        )
    own_tokens, queries, keys, values, probs, attended = front
    cotangent_pieces = exchange_cotangent(attended)
    normal, scale, hidden, gate_part, slope_part, active, total = ahead(
        group,
        flat(own_tokens),
        flat(attended),
        output_projection,
        first_gain,
        first_offset,
        expand_weight,
        reduce_weight,
    )
    blocks = 8
    *output, back_mixed, second_gain_back, second_offset_back, sent, kept = (
        reduce_gradient(
            group,
            total,
            second_gain,
            second_offset,
            cotangent,
            cotangent_pieces,
            active,
            dp_size=dp_size,
        )
    )
    output = DirectPieces(*output)
    by_device = lambda value: (
        value.reshape(blocks, width // 2, dp_size // blocks, inner // dp_size)
        .transpose(0, 2, 1, 3)
        .reshape(dp_size, width // 2, inner // dp_size)
    )
    reduce_sum = Sum(by_device(sent), by_device(kept))
    low_bit = near_bit(dp_size)
    others = [step for step in up_order if step not in (low_bit, low_bit + 1)]
    rest = (group, back_mixed, hidden, gate_part, slope_part, reduce_weight, expand_weight)
    slab = lambda value: value.reshape(dp_size, own_width, value.shape[1])
    sent, kept, back_hidden = expand_gradient(*rest, None, 0, dp_size, after=[kept])
    expand_first = Sum(slab(sent), slab(kept))
    moved = [reduce_sum.halve("near", back_hidden)]
    moved += output.come()
    sent, kept, back_hidden = expand_gradient(*rest, back_hidden, 1, dp_size, after=moved)
    expand_second = Sum(slab(sent), slab(kept))
    moved = [expand_first.halve("near", back_hidden)]
    moved = [reduce_sum.halve("far", *moved)]
    back_attended, branch, first_gain_back, first_offset_back = branch_back(
        group, back_hidden, normal, scale, first_gain, output_projection, after=moved
    )
    moved = [expand_second.halve("near", back_attended)]
    heads = (group, queries, keys, values, probs, attended, rowed(back_attended))
    columns = lambda value: value.reshape(3, row_count * length, value.shape[3])
    front = columns(attend_back(*heads, 0, 2, after=moved)[0])
    moved = [expand_first.halve("far", front)]
    moved = [reduce_sum.halve(others[0], *moved)]
    vectors = (first_gain_back, first_offset_back, second_gain_back, second_offset_back)
    sent, kept = joint_gradient(
        group, flat(own_tokens), flat(attended), front, branch, vectors, dp_size, after=moved
    )
    joint_first = Sum(slab(sent), slab(kept))
    moved = [expand_second.halve("far", kept)]
    moved = [expand_first.halve(others[0], *moved)]
    back = columns(attend_back(*heads, 2, 1, after=moved)[0])
    moved = [joint_first.halve("near", back)]
    reduce_own = reduce_sum.rest(others[1:], *moved)
    reduce_other = exchange(reduce_own, "head", 2)
    moved = [reduce_own]
    sent, kept = joint_gradient_end(group, flat(own_tokens), back, dp_size, after=moved)
    joint_last = Sum(slab(sent), slab(kept))
    moved = [expand_second.halve(others[0], kept)]
    first_own = expand_first.rest(others[1:], *moved)
    first_other = exchange(first_own, "head", 2)
    moved = [first_own]
    gradient = tokens_gradient_of(
        group, front, back, joint_projection, branch, piece, after=moved
    )

    moved = [joint_last.halve("near", gradient[0])]
    gradient = Pieces(*[later(part, *moved) for part in gradient])
    moved = [joint_first.halve("far", *moved)]
    second_own = expand_second.rest(others[1:], *moved)
    second_other = exchange(second_own, "head", 2)
    moved = [joint_last.halve("far", second_own)]
    moved = [joint_first.halve(others[0], *moved)]
    reduce_own = low(wide(later(reduce_own, *moved)) + wide(reduce_other))
    reduce_other = exchange(reduce_own, "head", 1)
    first_own = low(wide(later(first_own, reduce_own)) + wide(first_other))
    first_other = exchange(first_own, "head", 1)
    moved = [joint_last.halve(others[0], first_own)]
    reduce_grad = turn(later(group, *moved), reduce_own, reduce_other)
    output = output.finish(reduce_grad)
    second_own = low(wide(later(second_own, output)) + wide(second_other))
    second_other = exchange(second_own, "head", 1)
    moved = gradient.pass_on(second_own)
    joint_own = [joint_first.rest(others[1:], *moved)]
    joint_other = [exchange(joint_own[0], "head", 2)]
    joint_own += [joint_last.rest(others[1:], *joint_own)]
    joint_other += [exchange(joint_own[1], "head", 2)]
    second_grad = join_parts(later(second_own, *joint_own)[None], second_other[None], 1, 0)
    first_grad = join_parts(later(first_own, *joint_own)[None], first_other[None], 1, 0)
    expand_grad = jnp.concatenate(
        [
            piece
            for side in range(2)
            for piece in (first_grad[side], second_grad[side])
        ],
        axis=-1,
    )
    gradient = gradient.finish(*joint_own)
    joint_own = [
        low(wide(later(own, gradient)) + wide(other))
        for own, other in zip(joint_own, joint_other)
    ]
    vectors = wide(joint_own[0][:, -128:-124])
    both = jnp.concatenate((joint_own[0][:, :-128], joint_own[1]), axis=1)
    both = join_parts(both[None], exchange(both, "head", 1)[None], 1, 0)
    size = front.shape[2] // 2
    last = back.shape[2] // 2
    start = 3 * size + width // 2
    joint_grad = []
    for which in range(3):
        for begin, count in ((which * size, size), (start + which * last, last)):
            joint_grad += [both[side, :, begin : begin + count] for side in range(2)]
    projection_grad = [both[side, :, 3 * size : start] for side in range(2)]
    return (
        output,
        gradient,
        wide(jnp.concatenate(joint_grad, axis=-1)),
        wide(jnp.concatenate(projection_grad, axis=-1)),
        vectors[:, 0],
        vectors[:, 1],
        wide(expand_grad),
        reduce_grad,
        vectors[:, 2],
        vectors[:, 3],
    )


def solution(mesh):
    placed = (
        P("dp", "head", None),
        P("dp", None),
        P(),
        P(),
        P(),
        P(),
        P(),
        P(),
        P(),
        P(),
        P("dp", "head", None),
    )
    return jax.shard_map(
        local,
        mesh=mesh,
        in_specs=placed,
        out_specs=(
            P("dp", "head", None),
            P("dp", "head", None),
            P("dp", None),
            P("dp", None),
            P("dp"),
            P("dp"),
            P("dp", None),
            P("dp", None),
            P("dp"),
            P("dp"),
        ),
        check_vma=False,
    )
```
